32 devices in a mesh: img: 8 (over y, x, core), strip: 4 (over z).
Axes of the slice: x: 2, y: 2, z: 4, core: 2. Of those that a mesh axis runs over, the one named last changes fastest.
Arguments:
- patches: bfloat16 [64, 576, 300], P('img', 'strip'), may hold values from -6 to 6
- pinv: float32 [100, 1024], replicated, may hold values from -0.1875 to 0.1875
- base_embed: float32 [3, 1024, 384], replicated, may hold values from -0.375 to 0.375
- bias_embed: float32 [384], replicated, may hold values from -2 to 2
- pos_grid: float32 [7, 7, 384], replicated, may hold values from -6 to 6
- pos_index: int32 [2, 2, 24], replicated, may hold values from 0 to 6
- pos_frac: float32 [2, 24], replicated, may hold values from 0 to 1
- norm_gain: float32 [2, 384], replicated, may hold values from 0.5 to 1.5
- norm_shift: float32 [2, 384], replicated, may hold values from -2 to 2
- w_qkv: bfloat16 [384, 1152], replicated, may hold values from -0.3125 to 0.3125
- bias_attn: float32 [3, 384], replicated, may hold values from -2 to 2
- w_out: bfloat16 [384, 384], replicated, may hold values from -4 to 4
- w_up: bfloat16 [384, 1536], replicated, may hold values from -0.3125 to 0.3125
- bias_up: float32 [1536], replicated, may hold values from -2 to 2
- w_down: bfloat16 [1536, 384], replicated, may hold values from -0.15625 to 0.15625
- bias_down: float32 [384], replicated, may hold values from -2 to 2
- cotangent: bfloat16 [64, 576, 384], P('img', 'strip'), may hold values from -6 to 6
Outputs:
- output: bfloat16 [64, 576, 384], P('img', 'strip')
- g_patches: bfloat16 [64, 576, 300], P('img', 'strip')
- g_base_embed: float32 [3, 1024, 384], replicated
- g_bias_embed: float32 [384], replicated
- g_pos_grid: float32 [7, 7, 384], replicated
- g_norm_gain: float32 [2, 384], replicated
- g_norm_shift: float32 [2, 384], replicated
- g_w_qkv: float32 [384, 1152], replicated
- g_bias_attn: float32 [3, 384], replicated
- g_w_out: float32 [384, 384], replicated
- g_w_up: float32 [384, 1536], replicated
- g_bias_up: float32 [1536], replicated
- g_w_down: float32 [1536, 384], replicated
- g_bias_down: float32 [384], replicated
The draws below stay inside these ranges and needn't reach their ends.
Inputs may be any that keep to these rules, and one draw needn't show every extreme that they name: `pos_index`: each entry names a row or column of the base positional grid.
All inputs are finite; a program needn't handle non-finite values.
Results may differ from the reference program's by a relative error of at most 0.015.
Values may be sent and summed in bfloat16 or wider, within the bound.
A program may use at most 192 MiB of HBM per device.

```python
import math
import jax
import jax.numpy as jnp
from jax import lax

D = 384
HEADS = 6
HD = 64
FF = 1536
BASE_GRID = 7
GRID = 24
SEQ = 576
IMAGES = 64
P2 = 100
BP2 = 1024
PIX = 300


def touch_ends(drawn, rng, low, high):
    spot = [jax.random.randint(jax.random.fold_in(rng, axis), (), 0, length) for axis, length in enumerate(drawn.shape)]
    longest = drawn.shape.index(max(drawn.shape))
    beside = spot[:longest] + [(spot[longest] + 1) % drawn.shape[longest]] + spot[longest + 1:]
    return drawn.at[tuple(spot)].set(low).at[tuple(beside)].set(high)


def level_of(own_key, shape, cuts, least, largest):
    gain = 1.0
    for dim, blocks in cuts:
        heights = jax.random.uniform(jax.random.fold_in(jax.random.fold_in(own_key, 6), dim), (blocks,), jnp.float32, least / len(cuts), largest / len(cuts))
        gain = gain * jnp.repeat(jnp.exp(heights), shape[dim] // blocks).reshape((-1,) + (1,) * (len(shape) - 1 - dim))
    return gain


def centred(rng, dims, deviation, bound, cuts=(), held_as=jnp.bfloat16):
    drawn = jax.random.normal(rng, dims, jnp.float32) * deviation
    if len(cuts) > 0:
        drawn = level_of(rng, dims, cuts, -0.22, 0.18) * drawn
    return jnp.clip(drawn, min=-bound, max=bound).astype(held_as)


def setup_inputs(seed: int = 0) -> dict:
    key_of = jax.random.split(jax.random.key(seed), 18)
    patches = centred(key_of[0], (IMAGES, SEQ, PIX), 1.0, 6.0, ((0, 8), (1, 4)))
    pinv = centred(key_of[1], (P2, BP2), BP2 ** -0.5, 0.1875, (), jnp.float32)
    base_embed = centred(key_of[2], (3, BP2, D), PIX ** -0.5, 0.375, (), jnp.float32)
    bias_embed = centred(key_of[3], (D,), 0.3, 2.0, (), jnp.float32)
    pos_grid = centred(key_of[4], (BASE_GRID, BASE_GRID, D), 1.0, 6.0, (), jnp.float32)
    pos_index = touch_ends(jax.random.randint(key_of[5], (2, 2, GRID), 0, BASE_GRID), jax.random.fold_in(key_of[5], 1), 0, BASE_GRID - 1).astype(jnp.int32)
    pos_frac = jnp.clip(jax.random.uniform(key_of[6], (2, GRID), jnp.float32, 0.0, 1.0), 0.0, 1.0)
    norm_gain = jnp.clip(1.0 + 0.1 * jax.random.normal(key_of[7], (2, D), jnp.float32), 0.5, 1.5)
    norm_shift = centred(key_of[8], (2, D), 0.3, 2.0, (), jnp.float32)
    w_qkv = centred(key_of[9], (D, 3 * D), D ** -0.5, 0.3125)
    bias_attn = centred(key_of[10], (3, D), 0.3, 2.0, (), jnp.float32)
    w_out = centred(key_of[11], (D, D), (max(D * 4 // SEQ, 1)) ** -0.5, 4.0)
    w_up = centred(key_of[12], (D, FF), D ** -0.5, 0.3125)
    bias_up = centred(key_of[13], (FF,), 0.3, 2.0, (), jnp.float32)
    w_down = centred(key_of[14], (FF, D), FF ** -0.5, 0.15625)
    bias_down = centred(key_of[15], (D,), 0.3, 2.0, (), jnp.float32)
    cotangent = centred(key_of[16], (IMAGES, SEQ, D), 1.0, 6.0, ((0, 8), (1, 4)))
    return dict(patches=patches, pinv=pinv, base_embed=base_embed, bias_embed=bias_embed, pos_grid=pos_grid, pos_index=pos_index, pos_frac=pos_frac, norm_gain=norm_gain, norm_shift=norm_shift, w_qkv=w_qkv, bias_attn=bias_attn, w_out=w_out, w_up=w_up, bias_up=bias_up, w_down=w_down, bias_down=bias_down, cotangent=cotangent)


@jax.custom_vjp
def low(v):
    return lax.optimization_barrier(v.astype(jnp.bfloat16)).astype(jnp.float32)

@jax.custom_vjp
def low_back(v):
    return v

def low_keep(v):
    return (low(v), None)

def low_pass(kept, grad):
    return (grad,)

def back_keep(v):
    return (v, None)

def back_low(kept, grad):
    return (low(grad),)
low.defvjp(low_keep, low_pass)
low_back.defvjp(back_keep, back_low)
HIGHEST = lax.Precision.HIGHEST
EPSILON = 1e-06

def resize_table(corner_index, fraction):
    base_cells = jnp.arange(BASE_GRID, dtype=jnp.int32)
    lower_hit = (corner_index[0].astype(jnp.int32)[:, None] == base_cells[None, :]).astype(jnp.float32)
    upper_hit = (corner_index[1].astype(jnp.int32)[:, None] == base_cells[None, :]).astype(jnp.float32)
    return (1.0 - fraction)[:, None] * lower_hit + fraction[:, None] * upper_hit

def layer_norm(values_in, gain_row, shift_row):
    center = values_in - lax.optimization_barrier(jnp.mean(values_in, axis=-1, keepdims=True))
    spread = lax.optimization_barrier(jnp.mean(center * center, axis=-1, keepdims=True))
    return center * lax.rsqrt(spread + EPSILON) * gain_row + shift_row

def attend_image(triple):
    queries, keys_in, values_in = triple
    scores = jnp.einsum('qhe,khe->hqk', queries, keys_in, precision=HIGHEST) * (1.0 / math.sqrt(HD))
    scores = low_back(scores)
    attn_probs = low(jax.nn.softmax(scores, axis=-1))
    return jnp.einsum('hqk,khe->qhe', attn_probs, values_in, precision=HIGHEST)

def reference(patches, pinv, base_embed, bias_embed, pos_grid, pos_index, pos_frac, norm_gain, norm_shift, w_qkv, bias_attn, w_out, w_up, bias_up, w_down, bias_down, cotangent):
    row_table = resize_table(pos_index[0], pos_frac[0].astype(jnp.float32))
    col_table = resize_table(pos_index[1], pos_frac[1].astype(jnp.float32))

    def forward_pass(patch_vals, pinv_vals, base_vals, embed_bias, grid_vals, gains, shifts, qkv_weight, attn_bias, out_weight, up_weight, up_bias, down_weight, down_bias):
        kernel = low(jnp.einsum('qk,ckd->cqd', pinv_vals, base_vals, precision=HIGHEST).reshape(PIX, D))
        position = jnp.einsum('rb,cg,bgd->rcd', row_table, col_table, grid_vals, precision=HIGHEST).reshape(SEQ, D)
        embedded = jnp.einsum('isp,pd->isd', patch_vals, kernel, precision=HIGHEST) + embed_bias + position
        embedded = low_back(embedded)
        normed = low(layer_norm(embedded, gains[0], shifts[0]))
        projected = jnp.einsum('isd,de->ise', normed, qkv_weight, precision=HIGHEST)
        queries = low(low_back(projected[:, :, :D] + attn_bias[0]))
        keys_in = low(low_back(projected[:, :, D:2 * D]))
        values_in = low(low_back(projected[:, :, 2 * D:] + attn_bias[1]))
        split_shape = (IMAGES, SEQ, HEADS, HD)
        attended = lax.map(jax.checkpoint(attend_image), (queries.reshape(split_shape), keys_in.reshape(split_shape), values_in.reshape(split_shape)))
        attended = low(low_back(attended.reshape(IMAGES, SEQ, D)))
        branch = low_back(jnp.einsum('isd,de->ise', attended, out_weight, precision=HIGHEST) + attn_bias[2])
        middle = embedded + branch
        normed_mlp = low(layer_norm(middle, gains[1], shifts[1]))
        up_proj = low_back(jnp.einsum('isd,df->isf', normed_mlp, up_weight, precision=HIGHEST) + up_bias)
        activated = low(jax.nn.gelu(up_proj, approximate=True))
        return middle + jnp.einsum('isf,fd->isd', activated, down_weight, precision=HIGHEST) + down_bias
    inputs = (patches, pinv, base_embed, bias_embed, pos_grid, norm_gain, norm_shift, w_qkv, bias_attn, w_out, w_up, bias_up, w_down, bias_down)
    inputs = tuple((item.astype(jnp.float32) for item in inputs))
    result, pullback = jax.vjp(forward_pass, *inputs)
    grads = pullback(cotangent.astype(jnp.float32))
    return (result.astype(jnp.bfloat16), grads[0].astype(jnp.bfloat16), grads[2], grads[3], grads[4], grads[5], grads[6], grads[7], grads[8], grads[9], grads[10], grads[11], grads[12], grads[13])
```

```python
import functools
import math
from types import SimpleNamespace

import jax
import jax.numpy as jnp
from jax import lax
from jax.experimental import pallas as pl
from jax.experimental.pallas import tpu as pltpu
from jax.sharding import PartitionSpec as P

HD = 64
EPSILON = 1e-06
MESH = pl.DeviceIdType.MESH
HIGHEST = lax.Precision.HIGHEST
BF = jnp.bfloat16
F32 = jnp.float32
COMM = True
MAIN, TAIL, COT = 0, 1, 2
IMG, STRIP = "img", "strip"
REP = {}


def begin(copy):
    copy.start()


def landed(copy):
    copy.wait_recv()


def sent(copy):
    copy.wait_send()


def nn(a, b, precision=None):
    return lax.dot_general(
        a, b, (((1,), (0,)), ((), ())), precision=precision, preferred_element_type=F32
    )


def nt(a, b):
    return lax.dot_general(a, b, (((1,), (1,)), ((), ())), preferred_element_type=F32)


def tn(a, b, precision=None):
    return lax.dot_general(
        a, b, (((0,), (0,)), ((), ())), precision=precision, preferred_element_type=F32
    )


def fold8(x):
    return jnp.sum(x.reshape(x.shape[0] // 8, 8, x.shape[1]), axis=0)


def rows_of(start, size):
    return pl.ds(pl.multiple_of(start, 16), size)


def chunk_of(rows):
    best = 16
    for size in range(16, 257, 16):
        if rows % size == 0:
            best = size
    return best


class Reduce:
    def __init__(self, rows, stages, extra, grad, out, recv, extra_recv, sems):
        self.rows, self.stages, self.extra, self.done = rows, stages, extra, 0
        self.grad, self.out, self.recv, self.extra_recv = grad, out, recv, extra_recv
        self.rs_s, self.rs_r, self.ag_s, self.ag_r, self.ex_s, self.ex_r, self.loc = sems
        sizes, offsets = [rows], [0]
        for axis, unit, size in stages:
            mine = self.index(axis, unit, size)
            sizes.append(sizes[-1] // size)
            offsets.append(offsets[-1] + mine * sizes[-1])
        self.sizes, self.offsets = sizes, offsets

    @staticmethod
    def index(axis, unit, size):
        return (lax.axis_index(axis) // unit) % size

    def peer(self, stage, d):
        axis, unit, size = stage
        mine = self.index(axis, unit, size)
        there = (mine + d) % size
        return {axis: lax.axis_index(axis) + unit * (there - mine)}, there

    def rs_copies(self, k):
        size, sub = self.stages[k][2], self.sizes[k + 1]
        copies = []
        for d in range(1, size):
            device, there = self.peer(self.stages[k], d)
            copies.append(
                pltpu.make_async_remote_copy(
                    src_ref=self.grad.at[rows_of(self.offsets[k] + there * sub, sub), :],
                    dst_ref=self.recv[k].at[d - 1],
                    send_sem=self.rs_s.at[k, d - 1],
                    recv_sem=self.rs_r.at[k, d - 1],
                    device_id=device,
                    device_id_type=MESH,
                )
            )
        return copies

    def rs_start(self, k):
        for copy in self.rs_copies(k):
            copy.start()

    def rs_finish(self, k):
        copies = self.rs_copies(k)
        for copy in copies:
            copy.wait_recv()
        size, sub, first = self.stages[k][2], self.sizes[k + 1], self.offsets[k + 1]
        step = chunk_of(sub)

        def body(b, carry):
            rows = rows_of(first + b * step, step)
            total = self.grad[rows, :].astype(F32)
            for d in range(size - 1):
                total = total + self.recv[k][d, rows_of(b * step, step), :].astype(F32)
            self.grad[rows, :] = total.astype(BF)
            return carry

        lax.fori_loop(0, sub // step, body, 0)
        for copy in copies:
            copy.wait_send()

    def piece(self):
        return self.grad.at[rows_of(self.offsets[-1], self.sizes[-1]), :]

    def extra_copies(self):
        copies = []
        for d in range(1, self.extra[2]):
            device, _ = self.peer(self.extra, d)
            copies.append(
                pltpu.make_async_remote_copy(
                    src_ref=self.piece(),
                    dst_ref=self.extra_recv.at[d - 1],
                    send_sem=self.ex_s.at[d - 1],
                    recv_sem=self.ex_r.at[d - 1],
                    device_id=device,
                    device_id_type=MESH,
                )
            )
        return copies

    def extra_all(self):
        if self.extra is None:
            return
        copies = self.extra_copies()
        for copy in copies:
            copy.start()
        for copy in copies:
            copy.wait()
        rows = rows_of(self.offsets[-1], self.sizes[-1])
        total = self.grad[rows, :].astype(F32)
        for d in range(self.extra[2] - 1):
            total = total + self.extra_recv[d].astype(F32)
        self.grad[rows, :] = total.astype(BF)

    def ag_copies(self, k):
        size, sub = self.stages[k][2], self.sizes[k + 1]
        region = self.out.at[rows_of(self.offsets[k + 1], sub), :]
        source = self.piece() if k == len(self.stages) - 1 else region
        copies = []
        for d in range(1, size):
            device, _ = self.peer(self.stages[k], d)
            copies.append(
                pltpu.make_async_remote_copy(
                    src_ref=source,
                    dst_ref=region,
                    send_sem=self.ag_s.at[k, d - 1],
                    recv_sem=self.ag_r.at[k, d - 1],
                    device_id=device,
                    device_id_type=MESH,
                )
            )
        return copies

    def local_copy(self):
        region = self.out.at[rows_of(self.offsets[-1], self.sizes[-1]), :]
        return pltpu.make_async_copy(self.piece(), region, self.loc.at[0])

    def left(self):
        return self.done < 2 * len(self.stages) + 1

    def step(self):
        last = len(self.stages) - 1
        n = self.done
        self.done += 1
        if n == 0:
            self.rs_start(0)
        elif n <= last:
            self.rs_finish(n - 1)
            self.rs_start(n)
        elif n == last + 1:
            self.rs_finish(last)
            self.extra_all()
            self.ag_start(last)
        else:
            k = 2 * last + 2 - n
            self.ag_finish(k)
            if k > 0:
                self.ag_start(k - 1)

    def ag_start(self, k):
        if k == len(self.stages) - 1:
            self.local_copy().start()
        for copy in self.ag_copies(k):
            copy.start()

    def ag_finish(self, k):
        if k == len(self.stages) - 1:
            self.local_copy().wait()
        for copy in self.ag_copies(k):
            copy.wait()


def layer_kernel(cfg, *refs):
    r = SimpleNamespace(**dict(zip(cfg.names, refs)))
    n_strip, strip_rows, slots = cfg.n_strip, cfg.strip_rows, cfg.slots
    seq, width, ff, pixels, area = cfg.seq, cfg.width, cfg.ff, cfg.pixels, cfg.area
    main_w = cfg.main_w
    tail = pixels - main_w
    grid_side, base_count = cfg.grid_side, cfg.base_count
    pairs = width // 128
    depth = r.base_embed.shape[1]
    ff_chunks = ff // width
    me = lax.axis_index(STRIP)
    group = 2 if n_strip % 2 == 0 else 1
    block = group * strip_rows
    blocks = n_strip // group

    def repeat(fn, *args):
        count = REP.get(fn.__name__, 1)
        if count == 1:
            fn(*args)
        else:
            lax.fori_loop(0, count, lambda t, c: (fn(*args), c)[1], 0)

    stages, extra = cfg.stages, cfg.extra
    groups, at = [], len(refs) - sum(len(g.stages) + 8 for g in cfg.groups)
    for g, grad, out in zip(cfg.groups, (r.gd, r.gu, r.gq, r.gk), (r.gd_out, r.gu_out, r.gq_out, r.gk_out)):
        n = len(g.stages)
        groups.append(Reduce(g.rows, g.stages, extra, grad, out, refs[at:at + n], refs[at + n],
                             refs[at + n + 1:at + n + 8]))
        at += n + 8
    sum_d, sum_u, sum_q, sum_k = groups
    if COMM:
        barrier = pltpu.get_barrier_semaphore()
        greeted = 0
        for stage in stages + ([extra] if extra else []):
            for d in range(1, stage[2]):
                device, _ = sum_k.peer(stage, d)
                pl.semaphore_signal(barrier, inc=1, device_id=device, device_id_type=MESH)
                greeted += 1

    loads = [
        pltpu.make_async_copy(r.w_qkv, r.wqkv, r.load_sem.at[0]),
        pltpu.make_async_copy(r.w_out, r.wout, r.load_sem.at[1]),
        pltpu.make_async_copy(r.w_up, r.wup, r.load_sem.at[2]),
        pltpu.make_async_copy(r.w_down, r.wdown, r.load_sem.at[3]),
    ]
    base_loads = [
        pltpu.make_async_copy(r.base_embed.at[c], r.wide.at[rows_of(c * depth, depth), :], r.load_sem.at[4 + c])
        for c in range(3)
    ]
    tails_load = pltpu.make_async_copy(
        r.patches.at[:, :, main_w:pixels], r.ptails, r.load_sem.at[7]
    )
    own_loads = []
    for slot in range(slots):
        rows = rows_of(me * strip_rows, strip_rows)
        own_loads.append(pltpu.make_async_copy(
            r.patches.at[me * slots + slot, :, 0:main_w], r.pmain.at[slot, rows, :],
            r.load_sem.at[8 + slot]))
        own_loads.append(pltpu.make_async_copy(
            r.cotangent.at[me * slots + slot], r.cot.at[slot, rows, :],
            r.load_sem.at[8 + slots + slot]))
    tails_load.start()
    for copy in base_loads:
        copy.start()
    for copy in own_loads:
        copy.start()
    for copy in loads:
        copy.start()

    def z_in(kind, slot, d):
        home = (me + d) % n_strip
        rows = rows_of(me * strip_rows, strip_rows)
        image = home * slots + slot
        if kind == MAIN:
            src, dst, k = r.patches.at[image, :, 0:main_w], r.pmain.at[slot, rows, :], slot
        elif kind == TAIL:
            src, dst, k = r.packed.at[home], r.ptail.at[rows, :], slots
        else:
            src, dst, k = r.cotangent.at[image], r.cot.at[slot, rows, :], slots + 1 + slot
        return pltpu.make_async_remote_copy(
            src_ref=src, dst_ref=dst, send_sem=r.zin_s.at[k, d - 1],
            recv_sem=r.zin_r.at[k, d - 1], device_id={STRIP: home}, device_id_type=MESH)

    def z_all(kind, slot, act):
        if not COMM:
            return
        for d in range(1, n_strip):
            act(z_in(kind, slot, d))

    if COMM:
        pl.semaphore_wait(barrier, greeted)
    z_all(MAIN, 0, begin)

    tails_load.wait()
    zero_tail = jnp.zeros((strip_rows, 128 // slots - tail), F32)
    for home in range(n_strip):
        parts = []
        for slot in range(slots):
            parts.append(r.ptails[home * slots + slot].astype(F32))
            parts.append(zero_tail)
        r.packed[home] = jnp.concatenate(parts, axis=1).astype(BF)
    z_all(TAIL, 0, begin)
    for slot in range(1, slots):
        z_all(MAIN, slot, begin)
    r.ptail[rows_of(me * strip_rows, strip_rows), :] = r.packed[me]

    def make_kernel():
        pinv = r.pinv[...].astype(BF)
        r.kf[...] = jnp.zeros_like(r.kf)
        for c in range(3):
            if not REP:
                base_loads[c].wait()
            r.kf[c * area:(c + 1) * area, :] = nn(pinv, r.wide[c * depth:(c + 1) * depth, :].astype(BF))
        kernel = r.kf[...].astype(BF)
        r.kmain[...] = kernel[0:main_w]
        for slot in range(slots):
            r.stage[...] = jnp.zeros_like(r.stage)
            at = slot * (128 // slots)
            r.stage[at:at + tail, :] = r.kf[main_w:pixels, :]
            r.ktail[slot] = r.stage[...].astype(BF)

    if REP:
        for copy in base_loads:
            copy.wait()
    repeat(make_kernel)

    def make_position():
        cells = r.table.shape[0]
        cell = lax.broadcasted_iota(jnp.int32, (cells, grid_side), 0).astype(F32)
        grid_row = jnp.floor((cell + 0.5) / base_count)
        corner = (grid_row, cell - grid_row * base_count)
        place = lax.broadcasted_iota(jnp.int32, (grid_side, seq), 1).astype(F32)
        which = lax.broadcasted_iota(jnp.int32, (grid_side, seq), 0).astype(F32)
        patch_row = jnp.floor((place + 0.5) / grid_side)
        patch = (patch_row, place - patch_row * grid_side)
        product = None
        for t in range(2):
            low = r.pos_index[t, 0:1, :].astype(F32)
            high = r.pos_index[t, 1:2, :].astype(F32)
            frac = r.pos_frac[t:t + 1, :]
            entry = (1.0 - frac) * (corner[t] == low).astype(F32) + frac * (corner[t] == high).astype(F32)
            spread = nn(entry, (patch[t] == which).astype(F32), HIGHEST)
            product = spread if product is None else product * spread
        valid = lax.broadcasted_iota(jnp.int32, (cells, seq), 0) < base_count * base_count
        r.table[...] = jnp.where(valid, product, 0.0)
        r.stage[...] = jnp.zeros_like(r.stage)
        for b in range(base_count):
            r.stage[b * base_count:(b + 1) * base_count, :] = r.pos_grid[b]
        r.posb[...] = tn(r.table[...], r.stage[0:cells, :], HIGHEST) + r.bias_embed[...]

    repeat(make_position)
    z_all(COT, 0, begin)
    r.sums[...] = jnp.zeros_like(r.sums)
    r.sums_up[...] = jnp.zeros_like(r.sums_up)
    for copy in loads:
        copy.wait()
    for copy in own_loads:
        copy.wait()

    def wide_rows(k, rows):
        return rows_of(k * seq + rows.start, rows.size)

    lane = lax.broadcasted_iota(jnp.int32, (1, 128), 1)
    first_head = lane < HD

    def norm(x, gain, shift):
        center = x - jnp.mean(x, axis=-1, keepdims=True)
        inv = lax.rsqrt(jnp.mean(center * center, axis=-1, keepdims=True) + EPSILON)
        unit = center * inv
        return unit * gain + shift, unit, inv

    def norm_back(g, unit, inv, gain):
        gu = g * gain
        return inv * (
            gu - jnp.mean(gu, axis=-1, keepdims=True)
            - unit * jnp.mean(gu * unit, axis=-1, keepdims=True)
        )

    def add_sum(row, x):
        r.sums[row] += fold8(x)

    B_EMBED, GAIN, SHIFT, B_Q, B_V, B_O, B_DOWN = 0, 1, 3, 5, 6, 7, 8

    def near_first(t):
        return (t + me // group) % blocks

    def wait_rows(t, kind, slot):
        if not COMM:
            return
        for part in range(group):
            d = (me - t * group - part + n_strip) % n_strip

            @pl.when(d > 0)
            def _():
                z_in(kind, slot, d).wait_recv()

    def embed(i):
        def body(b, carry):
            b = near_first(b)
            rows = rows_of(b * block, block)
            wait_rows(b, MAIN, i)
            if i == 0:
                wait_rows(b, TAIL, 0)
            emb = (
                nn(r.pmain[i, rows, :], r.kmain[...])
                + nn(r.ptail[rows, :], r.ktail[i])
                + r.posb[rows, :]
            )
            r.wide[wide_rows(i, rows), :] = emb
            y, unit, inv = norm(emb, r.norm_gain[0:1, :], r.norm_shift[0:1, :])
            y = y.astype(BF)
            r.normed[i, rows, :] = y
            r.unit[i, rows, :] = unit.astype(BF)
            r.inv[i, rows, :] = jnp.broadcast_to(inv, (block, 128))
            q = nn(y, r.wqkv[:, 0:width]) + r.bias_attn[0:1, :]
            r.qkv[i, rows, 0:width] = (q * (1.0 / math.sqrt(HD))).astype(BF)
            r.qkv[i, rows, width:2 * width] = nn(y, r.wqkv[:, width:2 * width]).astype(BF)
            v = nn(y, r.wqkv[:, 2 * width:3 * width]) + r.bias_attn[1:2, :]
            r.qkv[i, rows, 2 * width:3 * width] = v.astype(BF)
            return carry

        lax.fori_loop(0, blocks, body, 0)

    def lanes(p, part=0):
        return slice(part * width + p * 128, part * width + (p + 1) * 128)

    def ahead(tasks, front, rest, depth):
        ready = [front(*task) for task in tasks[:depth]]
        for n, task in enumerate(tasks):
            if n + depth < len(tasks):
                ready.append(front(*tasks[n + depth]))
            rest(*task, ready[n])
            ready[n] = None

    heads = [(p, h) for p in range(pairs) for h in range(2)]

    def pick(x, h):
        return jnp.where(first_head == (h == 0), x, jnp.zeros_like(x))

    def attend(i):
        outs, recips = {}, {}

        def front(p, h):
            return nt(pick(r.qkv[i, :, lanes(p)], h), r.qkv[i, :, lanes(p, 1)])

        def rest(p, h, s):
            e = jnp.exp(s - jnp.max(s, axis=-1, keepdims=True))
            recip = 1.0 / jnp.sum(e, axis=-1, keepdims=True)
            e = e.astype(BF)
            r.expo[i, 2 * p + h] = e
            outs[h] = nn(e, r.qkv[i, :, lanes(p, 2)]) * recip
            recips[h] = jnp.broadcast_to(recip, (seq, 128))
            if h == 1:
                r.att[i, :, lanes(p)] = jnp.where(first_head, outs[0], outs[1]).astype(BF)
                r.wide[(2 * slots + i) * seq:(2 * slots + i + 1) * seq, lanes(p)] = jnp.where(first_head, recips[0], recips[1])

        ahead(heads, front, rest, 2)

    c0 = math.sqrt(2.0 / math.pi)
    c1 = 0.044715

    def send_rows(t, i, remote, own):
        if not COMM:
            return
        for part in range(group):
            strip = t * group + part
            d = (strip - me + n_strip) % n_strip

            @pl.when(d > 0)
            def _():
                remote(i, d).start()

            @pl.when(d == 0)
            def _():
                own(i).start()

    def out_copy(i, d):
        strip = (me + d) % n_strip
        return pltpu.make_async_remote_copy(
            src_ref=r.outb.at[i, rows_of(strip * strip_rows, strip_rows), :],
            dst_ref=r.output.at[me * slots + i],
            send_sem=r.zout_s.at[i, d - 1], recv_sem=r.zout_r.at[i, d - 1],
            device_id={STRIP: strip}, device_id_type=MESH)

    def own_out(i):
        return pltpu.make_async_copy(
            r.outb.at[i, rows_of(me * strip_rows, strip_rows), :],
            r.output.at[me * slots + i], r.own_sem.at[i])

    def mlp(i):
        def body(t, carry):
            t = near_first(t)
            rows = rows_of(t * block, block)
            wait_rows(t, COT, i)
            mid = r.wide[wide_rows(i, rows), :] + nn(r.att[i, rows, :], r.wout[...]) + r.bias_attn[2:3, :]
            gain = r.norm_gain[1:2, :]
            y, unit, inv = norm(mid, gain, r.norm_shift[1:2, :])
            y = y.astype(BF)
            r.nm[i, rows, :] = y
            cot = r.cot[i, rows, :]

            def front(cols):
                return nn(y, r.wup[:, cols]), nt(cot, r.wdown[cols, :])

            def rest(cols, ready):
                u = ready[0] + r.bias_up[cols]
                square = u * u
                half = 0.5 + 0.5 * jnp.tanh(u * (c0 + (c0 * c1) * square))
                act = u * half
                r.act[i, rows, cols] = act.astype(BF)
                slope = half + (act - act * half) * (2.0 * c0 + (6.0 * c0 * c1) * square)
                gu = ready[1] * slope
                r.gup[i, rows, cols] = gu.astype(BF)
                r.sums_up[:, cols] += fold8(gu)

            ahead([(slice(c, c + 256),) for c in range(0, ff, 256)], front, rest, 1)
            out = mid + r.bias_down[...] + nn(r.act[i, rows, :], r.wdown[...])
            g_nm = nt(r.gup[i, rows, :], r.wup[...])
            r.outb[i, rows, :] = out.astype(BF)
            send_rows(t, i, out_copy, own_out)
            add_sum(GAIN + 1, g_nm * unit)
            add_sum(SHIFT + 1, g_nm)
            cotf = cot.astype(F32)
            add_sum(B_DOWN, cotf)
            g_mid = cotf + norm_back(g_nm, unit, inv, gain)
            r.wide[wide_rows(slots + i, rows), :] = g_mid
            add_sum(B_O, g_mid)
            gb = g_mid.astype(BF)
            r.gb[i, rows, :] = gb
            r.datt[i, rows, :] = (nt(gb, r.wout[...]) * r.wide[wide_rows(2 * slots + i, rows), :]).astype(BF)
            return carry

        lax.fori_loop(0, blocks, body, 0)

    def ds_slot(p, h):
        wide = -(-seq // 128) * 128
        return (r.act, r.gup)[p % 2].at[slots - 1, :, h * wide:h * wide + seq]

    def attend_back(i):
        gq = {}

        def front(p, h):
            return nt(pick(r.datt[i, :, lanes(p)], h), r.qkv[i, :, lanes(p, 2)])

        def rest(p, h, dp):
            prod = r.datt[i, :, lanes(p)].astype(F32) * r.att[i, :, lanes(p)].astype(F32)
            delta = jnp.sum(pick(prod, h), axis=-1, keepdims=True)
            expo = r.expo[i, 2 * p + h]
            ds = (expo.astype(F32) * (dp - delta)).astype(BF)
            ds_slot(p, h)[...] = ds
            gq[h] = nn(ds, r.qkv[i, :, lanes(p, 1)])
            if h == 0:
                return
            g_q = jnp.where(first_head, gq[0], gq[1]) * (1.0 / math.sqrt(HD))
            r.gproj[i, :, lanes(p)] = g_q.astype(BF)
            q_t, d_t = r.qkv[i, :, lanes(p)].T, r.datt[i, :, lanes(p)].T
            for part in range(2):
                half = slice(part * HD, (part + 1) * HD)
                r.tk[p, half, :] = nn(q_t[half, :], ds_slot(p, part)[...]).astype(BF)
                r.tv[p, half, :] = nn(d_t[half, :], r.expo[i, 2 * p + part]).astype(BF)
            r.gproj[i, :, lanes(p, 1)] = r.tk[p].T
            r.gproj[i, :, lanes(p, 2)] = r.tv[p].T

        ahead(heads, front, rest, 1)

    def gp_copy(i, d):
        strip = (me + d) % n_strip
        return pltpu.make_async_remote_copy(
            src_ref=r.gup.at[i, rows_of(strip * strip_rows, strip_rows), ff - main_w:ff],
            dst_ref=r.gp_main.at[me * slots + i],
            send_sem=r.zout_s.at[slots + i, d - 1], recv_sem=r.zout_r.at[slots + i, d - 1],
            device_id={STRIP: strip}, device_id_type=MESH)

    def own_gp(i):
        return pltpu.make_async_copy(
            r.gup.at[i, rows_of(me * strip_rows, strip_rows), ff - main_w:ff],
            r.gp_main.at[me * slots + i], r.own_sem.at[slots + i])

    def gpt_copy(i, d):
        strip = (me + d) % n_strip
        return pltpu.make_async_remote_copy(
            src_ref=r.gpt.at[rows_of(strip * strip_rows, strip_rows), :],
            dst_ref=r.gp_tail.at[me],
            send_sem=r.zout_s.at[2 * slots, d - 1], recv_sem=r.zout_r.at[2 * slots, d - 1],
            device_id={STRIP: strip}, device_id_type=MESH)

    def own_gpt(i):
        return pltpu.make_async_copy(
            r.gpt.at[rows_of(me * strip_rows, strip_rows), :],
            r.gp_tail.at[me], r.own_sem.at[2 * slots])

    def embed_back(i):
        def body(t, carry):
            rows = rows_of(t * block, block)
            gain = r.norm_gain[0:1, :]
            unit = r.unit[i, rows, :].astype(F32)
            gproj = r.gproj[i, rows, :]
            add_sum(B_Q, gproj[:, 0:width].astype(F32))
            add_sum(B_V, gproj[:, 2 * width:3 * width].astype(F32))
            g_n = nt(gproj, r.wqkv[...])
            add_sum(GAIN, g_n * unit)
            add_sum(SHIFT, g_n)
            inv = r.inv[i, rows, :][:, 0:1]
            g_emb = r.wide[wide_rows(slots + i, rows), :] + norm_back(g_n, unit, inv, gain)
            add_sum(B_EMBED, g_emb)
            ge = g_emb.astype(BF)
            r.act[i, rows, ff - width:ff] = ge
            r.gup[i, rows, ff - main_w:ff] = nt(ge, r.kmain[...]).astype(BF)
            part = nt(ge, r.ktail[i])
            if i > 0:
                part = part + r.gpt[rows, :].astype(F32)
            r.gpt[rows, :] = part.astype(BF)
            send_rows(t, i, gp_copy, own_gp)
            if i == slots - 1:
                send_rows(t, i, gpt_copy, own_gpt)
            return carry

        lax.fori_loop(0, blocks, body, 0)

    def both(ref, cols=slice(None)):
        return ref[:, :, cols].reshape(slots * seq, -1)

    def grads_d():
        lhs = both(r.cot).T
        for c in range(0, ff, 512):
            r.gd[c:c + 512, :] = nn(lhs, both(r.act, slice(c, c + 512))).T.astype(BF)

    def grads_u():
        lhs = both(r.nm).T
        for c in range(0, ff, 512):
            part = nn(lhs, both(r.gup, slice(c, c + 512))).astype(BF)
            for n in range(4):
                r.gu[(c // 128 + n) * width:(c // 128 + n + 1) * width, :] = part[:, n * 128:(n + 1) * 128]

    def grads_q():
        part = tn(both(r.att), both(r.gb)).astype(BF)
        for n in range(pairs):
            r.gq[(3 * pairs + n) * width:(3 * pairs + n + 1) * width, :] = part[:, n * 128:(n + 1) * 128]
        lhs = both(r.normed).T
        for c in range(3):
            part = nn(lhs, both(r.gproj, slice(c * width, (c + 1) * width))).astype(BF)
            for n in range(pairs):
                at = (c * pairs + n) * width
                r.gq[at:at + width, :] = part[:, n * 128:(n + 1) * 128]

    def grads_k():
        r.kf[0:main_w, :] = tn(both(r.pmain), both(r.act, slice(ff - width, ff)))
        at = main_w
        total = None
        for slot in range(slots):
            part = tn(r.ptail[...], r.act[slot, :, ff - width:ff])
            start = slot * (128 // slots)
            part = part[start:start + tail, :]
            total = part if total is None else total + part
        r.kf[main_w:pixels, :] = total
        summed = sum(r.act[slot, :, ff - width:ff].astype(F32) for slot in range(slots))
        g_grid = nn(r.table[...], summed, HIGHEST)
        cells = base_count * base_count
        r.kf[pixels:pixels + cells, :] = g_grid[0:cells, :]
        small = jnp.sum(r.sums[...], axis=1)
        at = cfg.small_at + small.shape[0]
        r.kf[cfg.small_at:at, :] = small
        small_up = jnp.sum(r.sums_up[...], axis=0, keepdims=True)
        for c in range(ff_chunks):
            r.kf[at + c:at + c + 1, :] = small_up[:, c * width:(c + 1) * width]
        r.gk[0:r.kf.shape[0], :] = r.kf[...].astype(BF)
        if cfg.groups[3].rows > r.kf.shape[0]:
            more = cfg.groups[3].rows - r.kf.shape[0]
            r.gk[r.kf.shape[0]:, :] = jnp.zeros((more, width), BF)

    def step(*sums):
        if COMM:
            for one in sums:
                if one.left():
                    one.step()

    for i in range(slots):
        repeat(embed, i)
        if i + 1 < slots:
            z_all(COT, i + 1, begin)
        repeat(attend, i)
    for i in range(slots):
        repeat(mlp, i)
        if i < slots - 1:
            repeat(attend_back, i)
    repeat(grads_d)
    step(sum_d)
    repeat(grads_u)
    step(sum_u, sum_d)
    for i in range(slots - 1):
        repeat(embed_back, i)
    step(sum_u)
    repeat(attend_back, slots - 1)
    repeat(grads_q)
    step(sum_q, sum_d)
    repeat(embed_back, slots - 1)
    step(sum_q, sum_u)
    repeat(grads_k)
    step(sum_k, sum_d, sum_k, sum_u, sum_d, sum_q, sum_k, sum_u, sum_q, sum_k, sum_d, sum_q, sum_k, sum_u)
    while COMM and any(one.left() for one in groups):
        step(sum_d, sum_q, sum_k, sum_u)
    if COMM:
        for slot in range(slots):
            z_all(MAIN, slot, sent)
            z_all(COT, slot, sent)
            for d in range(1, n_strip):
                out_copy(slot, d).wait()
                gp_copy(slot, d).wait()
            own_out(slot).wait()
            own_gp(slot).wait()
        z_all(TAIL, 0, sent)
        for d in range(1, n_strip):
            gpt_copy(0, d).wait()
        own_gpt(0).wait()


def finish_kernel(cfg, *refs):
    r = SimpleNamespace(**dict(zip(cfg.names, refs)))
    width, ff, slots = cfg.width, cfg.ff, cfg.slots
    pixels, area, main_w = cfg.pixels, cfg.area, cfg.main_w
    tail = pixels - main_w
    ff_chunks = ff // width
    copies = []

    def load(k, src, dst):
        copy = pltpu.make_async_copy(src, dst, r.sem.at[k])
        copy.start()
        return copy

    def send(src, dst, k):
        copy = pltpu.make_async_copy(src, dst, r.sem.at[k])
        copy.start()
        copies.append(copy)

    loads = [
        load(9, r.gk.at[0:r.kf.shape[0], :], r.tail_in),
        load(10, r.gd, r.gd_in),
        load(11, r.gu, r.gu_in),
        load(12, r.gp_main, r.main_in),
        load(13, r.gp_tail, r.last_in),
        load(14, r.out_in, r.out_buf),
        load(15, r.gq, r.gq_in),
    ]
    loads[0].wait()
    r.kf[...] = r.tail_in[...].astype(F32)
    pinv = r.pinv[...].astype(BF)
    for c in range(3):
        part = r.kf[c * area:(c + 1) * area, :].astype(BF)
        r.base[c] = tn(pinv, part)
        send(r.base.at[c], r.g_base.at[c], 1 + c)
    loads[1].wait()
    r.down[...] = r.gd_in[...].astype(F32)
    send(r.down, r.g_down, 4)
    loads[2].wait()
    for n in range(ff // 128):
        r.up[:, n * 128:(n + 1) * 128] = r.gu_in[n * width:(n + 1) * width, :].astype(F32)
    send(r.up, r.g_up, 5)
    loads[6].wait()
    pairs = width // 128
    for n in range(3 * pairs):
        r.qkv[:, n * 128:(n + 1) * 128] = r.gq_in[n * width:(n + 1) * width, :].astype(F32)
    send(r.qkv, r.g_qkv, 6)
    for n in range(pairs):
        at = (3 * pairs + n) * width
        r.wo[:, n * 128:(n + 1) * 128] = r.gq_in[at:at + width, :].astype(F32)
    send(r.wo, r.g_out, 7)
    loads[5].wait()
    send(r.out_buf, r.output, 0)
    loads[3].wait()
    loads[4].wait()
    for image in range(r.gp.shape[0]):
        r.gp[image, :, 0:main_w] = r.main_in[image]
        start = (image % slots) * (128 // slots)
        last = r.last_in[image // slots].astype(F32)[:, start:start + tail]
        r.gp[image, :, main_w:pixels] = last.astype(BF)
    send(r.gp, r.g_patches, 8)
    small = r.kf[cfg.small_at:cfg.small_at + 16, :]
    for b in range(cfg.base_count):
        at = pixels + b * cfg.base_count
        r.g_grid[b] = r.kf[at:at + cfg.base_count, :]
    r.g_bias_embed[...] = small[0]
    r.g_gain[...] = small[1:3]
    r.g_shift[...] = small[3:5]
    r.g_attn[...] = small[5:8]
    r.g_bias_down[...] = small[8]
    for c in range(ff_chunks):
        r.g_bias_up[c * width:(c + 1) * width] = small[9 + c]
    for copy in copies:
        copy.wait()


def per_device(cfg, patches, pinv, base_embed, bias_embed, pos_grid, pos_index, pos_frac, norm_gain,
               norm_shift, w_qkv, bias_attn, w_out, w_up, bias_up, w_down, bias_down, cotangent):
    images, strip_rows, pixels = patches.shape
    width, ff = w_up.shape
    n_img, n_strip = cfg.n_img, cfg.n_strip
    slots = images // n_strip
    seq = strip_rows * n_strip
    base_count = pos_grid.shape[0]
    area = pinv.shape[0]
    main_w = pixels // 128 * 128
    core = [(IMG, 1, min(2, n_img))]
    plane = [(IMG, 2, min(4, n_img // 2))] if n_img > 2 else []
    stages = core + plane + [(STRIP, 1, n_strip)]
    left = n_img // 8
    extra = (IMG, 8, left) if left > 1 else None
    parts = math.prod(s[2] for s in stages)
    unit = 16 * parts
    cells = base_count * base_count
    small_at = -(-(pixels + cells) // 8) * 8
    k_rows = -(-(small_at + 9 + ff // width) // 128) * 128

    def sum_of(values, lanes, order):
        return SimpleNamespace(rows=-(-(values // lanes) // unit) * unit, lanes=lanes, stages=order)

    groups = [sum_of(ff * width, width, stages), sum_of(ff * width, 128, stages),
              sum_of(4 * width * width, 128, stages), sum_of(k_rows * width, width, stages)]
    conf = SimpleNamespace(n_strip=n_strip, strip_rows=strip_rows, slots=slots, seq=seq, width=width, ff=ff,
                           pixels=pixels, area=area, main_w=main_w, grid_side=pos_frac.shape[1],
                           base_count=base_count, stages=stages, extra=extra, groups=groups,
                           small_at=small_at)
    vmem = pl.BlockSpec(memory_space=pltpu.VMEM)
    hbm = pl.BlockSpec(memory_space=pl.ANY)
    ins = dict(
        patches=(patches, hbm), cotangent=(cotangent, hbm), base_embed=(base_embed, hbm),
        w_qkv=(w_qkv, hbm), w_out=(w_out, hbm), w_up=(w_up, hbm), w_down=(w_down, hbm),
        pinv=(pinv, vmem), bias_embed=(bias_embed, vmem), pos_grid=(pos_grid, vmem),
        pos_index=(pos_index, vmem), pos_frac=(pos_frac, vmem), norm_gain=(norm_gain, vmem),
        norm_shift=(norm_shift, vmem), bias_attn=(bias_attn, vmem),
        bias_up=(bias_up, vmem), bias_down=(bias_down, vmem),
    )
    outs = dict(
        output=jax.ShapeDtypeStruct((images, strip_rows, width), BF),
        gp_main=jax.ShapeDtypeStruct((images, strip_rows, main_w), BF),
        gp_tail=jax.ShapeDtypeStruct((n_strip, strip_rows, 128), BF),
        **dict(zip(("gd_out", "gu_out", "gq_out", "gk_out"),
                   (jax.ShapeDtypeStruct((g.rows, g.lanes), BF) for g in groups))),
    )
    V = pltpu.VMEM
    DMA = pltpu.SemaphoreType.DMA
    scratch = dict(
        wqkv=V(w_qkv.shape, BF), wout=V(w_out.shape, BF), wup=V(w_up.shape, BF), wdown=V(w_down.shape, BF),
        wide=V((max(3 * base_embed.shape[1], 3 * slots * seq), width), F32),
        ptails=V((images, strip_rows, pixels - main_w), BF), packed=V((n_strip, strip_rows, 128), BF),
        pmain=V((slots, seq, main_w), BF), ptail=V((seq, 128), BF), cot=V((slots, seq, width), BF),
        kf=V((k_rows, width), F32), kmain=V((main_w, width), BF), ktail=V((slots, 128, width), BF),
        stage=V((128, width), F32), table=V((-(-cells // 8) * 8, seq), F32), posb=V((seq, width), F32),
        normed=V((slots, seq, width), BF), unit=V((slots, seq, width), BF),
        inv=V((slots, seq, 128), F32), qkv=V((slots, seq, 3 * width), BF),
        expo=V((slots, width // HD, seq, seq), BF),
        att=V((slots, seq, width), BF), nm=V((slots, seq, width), BF),
        act=V((slots, seq, ff), BF), gup=V((slots, seq, ff), BF), outb=V((slots, seq, width), BF),
        gb=V((slots, seq, width), BF), datt=V((slots, seq, width), BF),
        tk=V((width // 128, 128, seq), BF), tv=V((width // 128, 128, seq), BF),
        gproj=V((slots, seq, 3 * width), BF), gpt=V((seq, 128), BF),
        sums=V((9, 8, width), F32), sums_up=V((8, ff), F32),
        gd=V((groups[0].rows, groups[0].lanes), BF), gu=V((groups[1].rows, groups[1].lanes), BF),
        gq=V((groups[2].rows, groups[2].lanes), BF), gk=V((groups[3].rows, groups[3].lanes), BF),
    )
    reduce_scratch = []
    more = max(left - 1, 1)
    for g in groups:
        size = g.rows
        for stage in g.stages:
            size //= stage[2]
            reduce_scratch.append(V((stage[2] - 1, size, g.lanes), BF))
        reduce_scratch.append(V((more, size, g.lanes), BF))
        reduce_scratch += [DMA((len(g.stages), 3))] * 4 + [DMA((more,))] * 2 + [DMA((1,))]
    scratch.update(
        load_sem=DMA((8 + 2 * slots,)), zin_s=DMA((2 * slots + 1, n_strip - 1)),
        zin_r=DMA((2 * slots + 1, n_strip - 1)), zout_s=DMA((2 * slots + 1, n_strip - 1)),
        zout_r=DMA((2 * slots + 1, n_strip - 1)), own_sem=DMA((2 * slots + 1,)),
    )
    conf.names = list(ins) + list(outs) + list(scratch)
    results = pl.pallas_call(
        functools.partial(layer_kernel, conf),
        out_shape=list(outs.values()),
        in_specs=[spec for _, spec in ins.values()],
        out_specs=[hbm] * len(outs),
        scratch_shapes=list(scratch.values()) + reduce_scratch,
        compiler_params=pltpu.CompilerParams(
            collective_id=0 if COMM else None, has_side_effects=True, vmem_limit_bytes=60 << 20),
        name="layer",
    )(*[value for value, _ in ins.values()])
    output, gp_main, gp_tail, gd, gu, gq, gk = results

    f_ins = dict(out_in=(output, hbm), gp_main=(gp_main, hbm), gp_tail=(gp_tail, hbm),
                 gd=(gd, hbm), gu=(gu, hbm), gq=(gq, hbm), gk=(gk, hbm), pinv=(pinv, vmem))
    shape = jax.ShapeDtypeStruct
    f_outs = dict(
        output=(shape(output.shape, BF), hbm), g_patches=(shape(patches.shape, BF), hbm),
        g_base=(shape(base_embed.shape, F32), hbm), g_bias_embed=(shape((width,), F32), vmem),
        g_grid=(shape(pos_grid.shape, F32), vmem), g_gain=(shape(norm_gain.shape, F32), vmem),
        g_shift=(shape(norm_shift.shape, F32), vmem), g_qkv=(shape(w_qkv.shape, F32), hbm),
        g_attn=(shape(bias_attn.shape, F32), vmem), g_out=(shape(w_out.shape, F32), hbm),
        g_up=(shape(w_up.shape, F32), hbm), g_bias_up=(shape((ff,), F32), vmem),
        g_down=(shape(w_down.shape, F32), hbm), g_bias_down=(shape((width,), F32), vmem),
    )
    f_scratch = dict(
        kf=V((k_rows, width), F32), base=V(base_embed.shape, F32), down=V(w_down.shape, F32),
        up=V(w_up.shape, F32), qkv=V(w_qkv.shape, F32), wo=V(w_out.shape, F32), gp=V(patches.shape, BF),
        tail_in=V((k_rows, width), BF), gd_in=V(gd.shape, BF), gu_in=V(gu.shape, BF), gq_in=V(gq.shape, BF),
        main_in=V(gp_main.shape, BF), last_in=V(gp_tail.shape, BF), out_buf=V(output.shape, BF), sem=DMA((16,)),
    )
    f_conf = SimpleNamespace(**dict(vars(conf), names=list(f_ins) + list(f_outs) + list(f_scratch)))
    final = pl.pallas_call(
        functools.partial(finish_kernel, f_conf),
        out_shape=[s for s, _ in f_outs.values()],
        in_specs=[spec for _, spec in f_ins.values()],
        out_specs=[spec for _, spec in f_outs.values()],
        scratch_shapes=list(f_scratch.values()),
        compiler_params=pltpu.CompilerParams(vmem_limit_bytes=56 << 20),
        name="finish",
    )(*[value for value, _ in f_ins.values()])
    (output, g_patches, g_base, g_bias_embed, g_grid, g_gain, g_shift, g_qkv, g_attn, g_out, g_up,
     g_bias_up, g_down, g_bias_down) = final
    return (output, g_patches, g_base, g_bias_embed, g_grid, g_gain, g_shift, g_qkv, g_attn, g_out, g_up,
            g_bias_up, g_down, g_bias_down)


def solution(mesh):
    cfg = SimpleNamespace(n_img=mesh.shape[IMG], n_strip=mesh.shape[STRIP])
    split = P(IMG, STRIP, None)
    return jax.shard_map(
        functools.partial(per_device, cfg), mesh=mesh,
        in_specs=(split,) + (P(),) * 15 + (split,),
        out_specs=(split, split) + (P(),) * 12, check_vma=False,
    )
```

```python
import functools
import math
from types import SimpleNamespace

import jax
import jax.numpy as jnp
from jax import lax
from jax.experimental import pallas as pl
from jax.experimental.pallas import tpu as pltpu
from jax.sharding import PartitionSpec as P

HD = 64
EPSILON = 1e-06
MESH = pl.DeviceIdType.MESH
HIGHEST = lax.Precision.HIGHEST
BF = jnp.bfloat16
F32 = jnp.float32
COMM = True
MAIN, TAIL, COT = 0, 1, 2
IMG, STRIP = "img", "strip"
REP = {}


def begin(copy):
    copy.start()


def landed(copy):
    copy.wait_recv()


def sent(copy):
    copy.wait_send()


def nn(a, b, precision=None):
    return lax.dot_general(
        a, b, (((1,), (0,)), ((), ())), precision=precision, preferred_element_type=F32
    )


def nt(a, b):
    return lax.dot_general(a, b, (((1,), (1,)), ((), ())), preferred_element_type=F32)


def tn(a, b, precision=None):
    return lax.dot_general(
        a, b, (((0,), (0,)), ((), ())), precision=precision, preferred_element_type=F32
    )


def fold8(x):
    return jnp.sum(x.reshape(x.shape[0] // 8, 8, x.shape[1]), axis=0)


def rows_of(start, size):
    return pl.ds(pl.multiple_of(start, 16), size)


def chunk_of(rows):
    best = 16
    for size in range(16, 257, 16):
        if rows % size == 0:
            best = size
    return best


class Reduce:
    def __init__(self, group, grad, out, recv, extra_recv, sems):
        rows, stages = group.rows, group.stages
        self.stages, self.extras, self.done, self.rows = stages, group.extras, 0, rows
        self.grad, self.out, self.recv, self.extra_recv = grad, out, recv, extra_recv
        self.rs_s, self.rs_r, self.ag_s, self.ag_r, self.ex_s, self.ex_r, self.loc = sems
        count = len(stages)
        self.phases = [(self.rs_start, self.rs_finish, k) for k in range(count)]
        self.phases += [(self.ex_start, self.ex_finish, k) for k in range(len(self.extras))]
        self.phases += [(self.ag_start, self.ag_finish, k) for k in range(count - 1, -1, -1)]
        sizes, offsets = [rows], [0]
        for axis, unit, size in stages:
            mine = self.index(axis, unit, size)
            sizes.append(sizes[-1] // size)
            offsets.append(offsets[-1] + mine * sizes[-1])
        self.sizes, self.offsets = sizes, offsets

    @staticmethod
    def index(axis, unit, size):
        return (lax.axis_index(axis) // unit) % size

    def peer(self, stage, d):
        axis, unit, size = stage
        mine = self.index(axis, unit, size)
        there = (mine + d) % size
        return {axis: lax.axis_index(axis) + unit * (there - mine)}, there

    def rs_copies(self, k):
        size, sub = self.stages[k][2], self.sizes[k + 1]
        copies = []
        for d in range(1, size):
            device, there = self.peer(self.stages[k], d)
            copies.append(
                pltpu.make_async_remote_copy(
                    src_ref=self.grad.at[rows_of(self.offsets[k] + there * sub, sub), :],
                    dst_ref=self.recv[k].at[d - 1],
                    send_sem=self.rs_s.at[k, d - 1],
                    recv_sem=self.rs_r.at[k, d - 1],
                    device_id=device,
                    device_id_type=MESH,
                )
            )
        return copies

    def rs_start(self, k):
        for copy in self.rs_copies(k):
            copy.start()

    def rs_finish(self, k):
        copies = self.rs_copies(k)
        for copy in copies:
            copy.wait_recv()
        size, sub, first = self.stages[k][2], self.sizes[k + 1], self.offsets[k + 1]
        step = chunk_of(sub)

        def body(b, carry):
            rows = rows_of(first + b * step, step)
            total = self.grad[rows, :].astype(F32)
            for d in range(size - 1):
                total = total + self.recv[k][d, rows_of(b * step, step), :].astype(F32)
            self.grad[rows, :] = total.astype(BF)
            return carry

        lax.fori_loop(0, sub // step, body, 0)
        for copy in copies:
            copy.wait_send()

    def piece(self):
        return self.grad.at[rows_of(self.offsets[-1], self.sizes[-1]), :]

    def ex_copies(self, k):
        copies = []
        for d in range(1, self.extras[k][2]):
            device, _ = self.peer(self.extras[k], d)
            copies.append(
                pltpu.make_async_remote_copy(
                    src_ref=self.piece(),
                    dst_ref=self.extra_recv[k].at[d - 1],
                    send_sem=self.ex_s.at[k, d - 1],
                    recv_sem=self.ex_r.at[k, d - 1],
                    device_id=device,
                    device_id_type=MESH,
                )
            )
        return copies

    def ex_start(self, k):
        for copy in self.ex_copies(k):
            copy.start()

    def ex_finish(self, k):
        for copy in self.ex_copies(k):
            copy.wait()
        rows = rows_of(self.offsets[-1], self.sizes[-1])
        total = self.grad[rows, :].astype(F32)
        for d in range(self.extras[k][2] - 1):
            total = total + self.extra_recv[k][d].astype(F32)
        self.grad[rows, :] = total.astype(BF)

    def ag_copies(self, k):
        size, sub = self.stages[k][2], self.sizes[k + 1]
        region = self.out.at[rows_of(self.offsets[k + 1], sub), :]
        source = self.piece() if k == len(self.stages) - 1 else region
        copies = []
        for d in range(1, size):
            device, _ = self.peer(self.stages[k], d)
            copies.append(
                pltpu.make_async_remote_copy(
                    src_ref=source,
                    dst_ref=region,
                    send_sem=self.ag_s.at[k, d - 1],
                    recv_sem=self.ag_r.at[k, d - 1],
                    device_id=device,
                    device_id_type=MESH,
                )
            )
        return copies

    def local_copy(self):
        region = self.out.at[rows_of(self.offsets[-1], self.sizes[-1]), :]
        return pltpu.make_async_copy(self.piece(), region, self.loc.at[0])

    def left(self):
        return self.done <= len(self.phases)

    def step(self):
        n = self.done
        self.done += 1
        if n > 0:
            self.phases[n - 1][1](self.phases[n - 1][2])
        if n < len(self.phases):
            self.phases[n][0](self.phases[n][2])

    def ag_start(self, k):
        if k == len(self.stages) - 1:
            self.local_copy().start()
        for copy in self.ag_copies(k):
            copy.start()

    def ag_finish(self, k):
        if k == len(self.stages) - 1:
            self.local_copy().wait()
        for copy in self.ag_copies(k):
            copy.wait()


def layer_kernel(cfg, *refs):
    r = SimpleNamespace(**dict(zip(cfg.names, refs)))
    n_strip, strip_rows, slots = cfg.n_strip, cfg.strip_rows, cfg.slots
    seq, width, ff, pixels, area = cfg.seq, cfg.width, cfg.ff, cfg.pixels, cfg.area
    main_w = cfg.main_w
    tail = pixels - main_w
    grid_side, base_count = cfg.grid_side, cfg.base_count
    pairs = width // 128
    depth = r.base_embed.shape[1]
    ff_chunks = ff // width
    me = lax.axis_index(STRIP)
    group = 2 if n_strip % 2 == 0 else 1
    block = group * strip_rows
    blocks = n_strip // group

    def repeat(fn, *args):
        count = REP.get(fn.__name__, 1)
        if count == 1:
            fn(*args)
        else:
            lax.fori_loop(0, count, lambda t, c: (fn(*args), c)[1], 0)

    groups = []
    at = len(refs) - sum(len(g.stages) + len(g.extras) + 7 for g in cfg.groups)
    for g, grad, out in zip(cfg.groups, (r.gd, r.gu, r.gq, r.gk), (r.gd_out, r.gu_out, r.gq_out, r.gk_out)):
        n, e = len(g.stages), len(g.extras)
        groups.append(Reduce(g, grad, out, refs[at:at + n], refs[at + n:at + n + e],
                             refs[at + n + e:at + n + e + 7]))
        at += n + e + 7
    sum_d, sum_u, sum_q, sum_k = groups
    if COMM:
        barrier = pltpu.get_barrier_semaphore()
        greeted = 0
        for stage in cfg.stages + cfg.left:
            for d in range(1, stage[2]):
                device, _ = sum_k.peer(stage, d)
                pl.semaphore_signal(barrier, inc=1, device_id=device, device_id_type=MESH)
                greeted += 1

    loads = [
        pltpu.make_async_copy(r.w_qkv, r.wqkv, r.load_sem.at[0]),
        pltpu.make_async_copy(r.w_out, r.wout, r.load_sem.at[1]),
        pltpu.make_async_copy(r.w_up, r.wup, r.load_sem.at[2]),
        pltpu.make_async_copy(r.w_down, r.wdown, r.load_sem.at[3]),
    ]
    base_loads = [
        pltpu.make_async_copy(r.base_embed.at[c], r.wide.at[rows_of(c * depth, depth), :], r.load_sem.at[4 + c])
        for c in range(3)
    ]
    tails_load = pltpu.make_async_copy(
        r.patches.at[:, :, main_w:pixels], r.ptails, r.load_sem.at[7]
    )
    own_loads = []
    for slot in range(slots):
        rows = rows_of(me * strip_rows, strip_rows)
        own_loads.append(pltpu.make_async_copy(
            r.patches.at[me * slots + slot, :, 0:main_w], r.pmain.at[slot, rows, :],
            r.load_sem.at[8 + slot]))
        own_loads.append(pltpu.make_async_copy(
            r.cotangent.at[me * slots + slot], r.cot.at[slot, rows, :],
            r.load_sem.at[8 + slots + slot]))
    tails_load.start()
    for copy in base_loads:
        copy.start()
    for copy in own_loads:
        copy.start()
    for copy in loads:
        copy.start()

    def z_in(kind, slot, d):
        home = (me + d) % n_strip
        rows = rows_of(me * strip_rows, strip_rows)
        image = home * slots + slot
        if kind == MAIN:
            src, dst, k = r.patches.at[image, :, 0:main_w], r.pmain.at[slot, rows, :], slot
        elif kind == TAIL:
            src, dst, k = r.packed.at[home], r.ptail.at[rows, :], slots
        else:
            src, dst, k = r.cotangent.at[image], r.cot.at[slot, rows, :], slots + 1 + slot
        return pltpu.make_async_remote_copy(
            src_ref=src, dst_ref=dst, send_sem=r.zin_s.at[k, d - 1],
            recv_sem=r.zin_r.at[k, d - 1], device_id={STRIP: home}, device_id_type=MESH)

    def z_all(kind, slot, act):
        if not COMM:
            return
        for d in range(1, n_strip):
            act(z_in(kind, slot, d))

    if COMM:
        pl.semaphore_wait(barrier, greeted)
    z_all(MAIN, 0, begin)

    tails_load.wait()
    zero_tail = jnp.zeros((strip_rows, 128 // slots - tail), F32)
    for home in range(n_strip):
        parts = []
        for slot in range(slots):
            parts.append(r.ptails[home * slots + slot].astype(F32))
            parts.append(zero_tail)
        r.packed[home] = jnp.concatenate(parts, axis=1).astype(BF)
    z_all(TAIL, 0, begin)
    r.ptail[rows_of(me * strip_rows, strip_rows), :] = r.packed[me]

    def make_kernel():
        pinv = r.pinv[...].astype(BF)
        r.kf[...] = jnp.zeros_like(r.kf)
        for c in range(3):
            if not REP:
                base_loads[c].wait()
            r.kf[c * area:(c + 1) * area, :] = nn(pinv, r.wide[c * depth:(c + 1) * depth, :].astype(BF))
        kernel = r.kf[...].astype(BF)
        r.kmain[...] = kernel[0:main_w]
        for slot in range(slots):
            r.stage[...] = jnp.zeros_like(r.stage)
            at = slot * (128 // slots)
            r.stage[at:at + tail, :] = r.kf[main_w:pixels, :]
            r.ktail[slot] = r.stage[...].astype(BF)

    if REP:
        for copy in base_loads:
            copy.wait()
    repeat(make_kernel)

    def make_position():
        cells = r.table.shape[0]
        cell = lax.broadcasted_iota(jnp.int32, (cells, grid_side), 0).astype(F32)
        grid_row = jnp.floor((cell + 0.5) / base_count)
        corner = (grid_row, cell - grid_row * base_count)
        place = lax.broadcasted_iota(jnp.int32, (grid_side, seq), 1).astype(F32)
        which = lax.broadcasted_iota(jnp.int32, (grid_side, seq), 0).astype(F32)
        patch_row = jnp.floor((place + 0.5) / grid_side)
        patch = (patch_row, place - patch_row * grid_side)
        product = None
        for t in range(2):
            low = r.pos_index[t, 0:1, :].astype(F32)
            high = r.pos_index[t, 1:2, :].astype(F32)
            frac = r.pos_frac[t:t + 1, :]
            entry = (1.0 - frac) * (corner[t] == low).astype(F32) + frac * (corner[t] == high).astype(F32)
            spread = nn(entry, (patch[t] == which).astype(F32), HIGHEST)
            product = spread if product is None else product * spread
        valid = lax.broadcasted_iota(jnp.int32, (cells, seq), 0) < base_count * base_count
        r.table[...] = jnp.where(valid, product, 0.0)
        r.stage[...] = jnp.zeros_like(r.stage)
        for b in range(base_count):
            r.stage[b * base_count:(b + 1) * base_count, :] = r.pos_grid[b]
        r.posb[...] = tn(r.table[...], r.stage[0:cells, :], HIGHEST) + r.bias_embed[...]

    repeat(make_position)
    r.sums[...] = jnp.zeros_like(r.sums)
    r.sums_up[...] = jnp.zeros_like(r.sums_up)
    for one, used in zip(groups, ((ff + width), ff * pairs, 3 * width * pairs)):
        if one.rows > used:
            r_pad = one.grad.shape
            one.grad[used:, :] = jnp.zeros((r_pad[0] - used, r_pad[1]), BF)
    for copy in loads:
        copy.wait()
    for copy in own_loads:
        copy.wait()

    def wide_rows(k, rows):
        return rows_of(k * seq + rows.start, rows.size)

    lane = lax.broadcasted_iota(jnp.int32, (1, 128), 1)
    first_head = lane < HD

    def norm(x, gain, shift):
        center = x - jnp.mean(x, axis=-1, keepdims=True)
        inv = lax.rsqrt(jnp.mean(center * center, axis=-1, keepdims=True) + EPSILON)
        unit = center * inv
        return unit * gain + shift, unit, inv

    def norm_back(g, unit, inv, gain):
        gu = g * gain
        return inv * (
            gu - jnp.mean(gu, axis=-1, keepdims=True)
            - unit * jnp.mean(gu * unit, axis=-1, keepdims=True)
        )

    def add_sum(row, x):
        r.sums[row] += fold8(x)

    B_EMBED, GAIN, SHIFT, B_Q, B_V, B_O, B_DOWN = 0, 1, 3, 5, 6, 7, 8

    def near_first(t):
        return (t + me // group) % blocks

    def wait_rows(t, kind, slot):
        if not COMM:
            return
        for part in range(group):
            d = (me - t * group - part + n_strip) % n_strip

            @pl.when(d > 0)
            def _():
                z_in(kind, slot, d).wait_recv()

    def embed(i):
        def body(t, carry):
            b = near_first(t)
            rows = rows_of(b * block, block)
            wait_rows(b, MAIN, i)
            if i == 0:
                wait_rows(b, TAIL, 0)

            @pl.when(t == 0)
            def _():
                if i + 1 < slots:
                    z_all(MAIN, i + 1, begin)
                else:
                    z_all(COT, i, begin)

            emb = (
                nn(r.pmain[i, rows, :], r.kmain[...])
                + nn(r.ptail[rows, :], r.ktail[i])
                + r.posb[rows, :]
            )
            r.wide[wide_rows(i, rows), :] = emb
            y, unit, inv = norm(emb, r.norm_gain[0:1, :], r.norm_shift[0:1, :])
            y = y.astype(BF)
            r.normed[i, rows, :] = y
            r.unit[i, rows, :] = unit.astype(BF)
            r.inv[i, rows, :] = jnp.broadcast_to(inv, (block, 128))
            q = nn(y, r.wqkv[:, 0:width]) + r.bias_attn[0:1, :]
            r.qkv[i, rows, 0:width] = (q * (1.0 / math.sqrt(HD))).astype(BF)
            r.qkv[i, rows, width:2 * width] = nn(y, r.wqkv[:, width:2 * width]).astype(BF)
            v = nn(y, r.wqkv[:, 2 * width:3 * width]) + r.bias_attn[1:2, :]
            r.qkv[i, rows, 2 * width:3 * width] = v.astype(BF)
            return carry

        lax.fori_loop(0, blocks, body, 0)

    def lanes(p, part=0):
        return slice(part * width + p * 128, part * width + (p + 1) * 128)

    def ahead(tasks, front, rest, depth):
        ready = [front(*task) for task in tasks[:depth]]
        for n, task in enumerate(tasks):
            if n + depth < len(tasks):
                ready.append(front(*tasks[n + depth]))
            rest(*task, ready[n])
            ready[n] = None

    heads = [(p, h) for p in range(pairs) for h in range(2)]

    def pick(x, h):
        return jnp.where(first_head == (h == 0), x, jnp.zeros_like(x))

    def attend(i):
        outs, recips = {}, {}

        def front(p, h):
            return nt(pick(r.qkv[i, :, lanes(p)], h), r.qkv[i, :, lanes(p, 1)])

        def rest(p, h, s):
            e = jnp.exp(s - jnp.max(s, axis=-1, keepdims=True))
            recip = 1.0 / jnp.sum(e, axis=-1, keepdims=True)
            e = e.astype(BF)
            r.expo[i, 2 * p + h] = e
            outs[h] = nn(e, r.qkv[i, :, lanes(p, 2)]) * recip
            recips[h] = jnp.broadcast_to(recip, (seq, 128))
            if h == 1:
                r.att[i, :, lanes(p)] = jnp.where(first_head, outs[0], outs[1]).astype(BF)
                r.wide[(2 * slots + i) * seq:(2 * slots + i + 1) * seq, lanes(p)] = jnp.where(first_head, recips[0], recips[1])

        ahead(heads, front, rest, 2)

    c0 = math.sqrt(2.0 / math.pi)
    c1 = 0.044715

    def out_copy(i, d):
        strip = (me + d) % n_strip
        return pltpu.make_async_remote_copy(
            src_ref=r.outb.at[i, rows_of(strip * strip_rows, strip_rows), :],
            dst_ref=r.output.at[me * slots + i],
            send_sem=r.zout_s.at[i, d - 1], recv_sem=r.zout_r.at[i, d - 1],
            device_id={STRIP: strip}, device_id_type=MESH)

    def own_out(i):
        return pltpu.make_async_copy(
            r.outb.at[i, rows_of(me * strip_rows, strip_rows), :],
            r.output.at[me * slots + i], r.own_sem.at[i])

    def send_out(i):
        if not COMM:
            return
        for d in range(1, n_strip):
            out_copy(i, d).start()
        own_out(i).start()

    def mlp(i):
        def body(n, carry):
            t = near_first(n)
            rows = rows_of(t * block, block)
            wait_rows(t, COT, i)
            if i > 0:

                @pl.when(n == blocks - 1)
                def _():
                    send_out(i - 1)

            mid = r.wide[wide_rows(i, rows), :] + nn(r.att[i, rows, :], r.wout[...]) + r.bias_attn[2:3, :]
            gain = r.norm_gain[1:2, :]
            y, unit, inv = norm(mid, gain, r.norm_shift[1:2, :])
            y = y.astype(BF)
            r.nm[i, rows, :] = y
            cot = r.cot[i, rows, :]

            def front(cols):
                return nn(y, r.wup[:, cols]), nt(cot, r.wdown[cols, :])

            def rest(cols, ready):
                u = ready[0] + r.bias_up[cols]
                square = u * u
                half = 0.5 + 0.5 * jnp.tanh(u * (c0 + (c0 * c1) * square))
                act = u * half
                r.act[i, rows, cols] = act.astype(BF)
                slope = half + (act - act * half) * (2.0 * c0 + (6.0 * c0 * c1) * square)
                gu = ready[1] * slope
                r.gup[i, rows, cols] = gu.astype(BF)
                r.sums_up[:, cols] += fold8(gu)

            ahead([(slice(c, c + 256),) for c in range(0, ff, 256)], front, rest, 1)
            out = mid + r.bias_down[...] + nn(r.act[i, rows, :], r.wdown[...])
            g_nm = nt(r.gup[i, rows, :], r.wup[...])
            r.outb[i, rows, :] = out.astype(BF)
            add_sum(GAIN + 1, g_nm * unit)
            add_sum(SHIFT + 1, g_nm)
            cotf = cot.astype(F32)
            add_sum(B_DOWN, cotf)
            g_mid = cotf + norm_back(g_nm, unit, inv, gain)
            r.wide[wide_rows(slots + i, rows), :] = g_mid
            add_sum(B_O, g_mid)
            gb = g_mid.astype(BF)
            r.gb[i, rows, :] = gb
            r.datt[i, rows, :] = (nt(gb, r.wout[...]) * r.wide[wide_rows(2 * slots + i, rows), :]).astype(BF)
            return carry

        lax.fori_loop(0, blocks, body, 0)

    def ds_slot(p, h):
        wide = -(-seq // 128) * 128
        return (r.act, r.gup)[p % 2].at[slots - 1, :, h * wide:h * wide + seq]

    def attend_back(i):
        gq = {}

        def front(p, h):
            return nt(pick(r.datt[i, :, lanes(p)], h), r.qkv[i, :, lanes(p, 2)])

        def rest(p, h, dp):
            prod = r.datt[i, :, lanes(p)].astype(F32) * r.att[i, :, lanes(p)].astype(F32)
            delta = jnp.sum(pick(prod, h), axis=-1, keepdims=True)
            expo = r.expo[i, 2 * p + h]
            ds = (expo.astype(F32) * (dp - delta)).astype(BF)
            ds_slot(p, h)[...] = ds
            gq[h] = nn(ds, r.qkv[i, :, lanes(p, 1)])
            if h == 0:
                return
            g_q = jnp.where(first_head, gq[0], gq[1]) * (1.0 / math.sqrt(HD))
            r.gproj[i, :, lanes(p)] = g_q.astype(BF)
            q_t, d_t = r.qkv[i, :, lanes(p)].T, r.datt[i, :, lanes(p)].T
            for part in range(2):
                half = slice(part * HD, (part + 1) * HD)
                r.tk[p, half, :] = nn(q_t[half, :], ds_slot(p, part)[...]).astype(BF)
                r.tv[p, half, :] = nn(d_t[half, :], r.expo[i, 2 * p + part]).astype(BF)
            r.gproj[i, :, lanes(p, 1)] = r.tk[p].T
            r.gproj[i, :, lanes(p, 2)] = r.tv[p].T

        ahead(heads, front, rest, 1)

    def gp_copy(i, d):
        strip = (me + d) % n_strip
        return pltpu.make_async_remote_copy(
            src_ref=r.gup.at[i, rows_of(strip * strip_rows, strip_rows), ff - main_w:ff],
            dst_ref=r.gp_main.at[me * slots + i],
            send_sem=r.zout_s.at[slots + i, d - 1], recv_sem=r.zout_r.at[slots + i, d - 1],
            device_id={STRIP: strip}, device_id_type=MESH)

    def own_gp(i):
        return pltpu.make_async_copy(
            r.gup.at[i, rows_of(me * strip_rows, strip_rows), ff - main_w:ff],
            r.gp_main.at[me * slots + i], r.own_sem.at[slots + i])

    def gpt_copy(i, d):
        strip = (me + d) % n_strip
        return pltpu.make_async_remote_copy(
            src_ref=r.gpt.at[rows_of(strip * strip_rows, strip_rows), :],
            dst_ref=r.gp_tail.at[me],
            send_sem=r.zout_s.at[2 * slots, d - 1], recv_sem=r.zout_r.at[2 * slots, d - 1],
            device_id={STRIP: strip}, device_id_type=MESH)

    def own_gpt(i):
        return pltpu.make_async_copy(
            r.gpt.at[rows_of(me * strip_rows, strip_rows), :],
            r.gp_tail.at[me], r.own_sem.at[2 * slots])

    def embed_back(i):
        def body(t, carry):
            rows = rows_of(t * block, block)
            gain = r.norm_gain[0:1, :]
            unit = r.unit[i, rows, :].astype(F32)
            gproj = r.gproj[i, rows, :]
            add_sum(B_Q, gproj[:, 0:width].astype(F32))
            add_sum(B_V, gproj[:, 2 * width:3 * width].astype(F32))
            g_n = nt(gproj, r.wqkv[...])
            add_sum(GAIN, g_n * unit)
            add_sum(SHIFT, g_n)
            inv = r.inv[i, rows, :][:, 0:1]
            g_emb = r.wide[wide_rows(slots + i, rows), :] + norm_back(g_n, unit, inv, gain)
            add_sum(B_EMBED, g_emb)
            ge = g_emb.astype(BF)
            r.act[i, rows, ff - width:ff] = ge
            r.gup[i, rows, ff - main_w:ff] = nt(ge, r.kmain[...]).astype(BF)
            part = nt(ge, r.ktail[i])
            if i > 0:
                part = part + r.gpt[rows, :].astype(F32)
            r.gpt[rows, :] = part.astype(BF)
            return carry

        lax.fori_loop(0, blocks, body, 0)

    def send_gp(i):
        if not COMM:
            return
        for d in range(1, n_strip):
            gp_copy(i, d).start()
        own_gp(i).start()

    def send_tail():
        if not COMM:
            return
        for d in range(1, n_strip):
            gpt_copy(0, d).start()
        own_gpt(0).start()

    def both(ref, cols=slice(None)):
        return ref[:, :, cols].reshape(slots * seq, -1)

    def grads_d():
        lhs = both(r.cot).T
        for c in range(0, ff, 512):
            r.gd[c:c + 512, :] = nn(lhs, both(r.act, slice(c, c + 512))).T.astype(BF)
        r.gd[ff:ff + width, :] = tn(both(r.att), both(r.gb)).astype(BF)

    def grads_u():
        lhs = both(r.nm).T
        for c in range(0, ff, 512):
            part = nn(lhs, both(r.gup, slice(c, c + 512))).astype(BF)
            for n in range(4):
                r.gu[(c // 128 + n) * width:(c // 128 + n + 1) * width, :] = part[:, n * 128:(n + 1) * 128]

    def grads_q():
        lhs = both(r.normed).T
        for c in range(3):
            part = nn(lhs, both(r.gproj, slice(c * width, (c + 1) * width))).astype(BF)
            for n in range(pairs):
                at = (c * pairs + n) * width
                r.gq[at:at + width, :] = part[:, n * 128:(n + 1) * 128]

    def grads_k():
        r.kf[0:main_w, :] = tn(both(r.pmain), both(r.act, slice(ff - width, ff)))
        at = main_w
        total = None
        for slot in range(slots):
            part = tn(r.ptail[...], r.act[slot, :, ff - width:ff])
            start = slot * (128 // slots)
            part = part[start:start + tail, :]
            total = part if total is None else total + part
        r.kf[main_w:pixels, :] = total
        summed = sum(r.act[slot, :, ff - width:ff].astype(F32) for slot in range(slots))
        g_grid = nn(r.table[...], summed, HIGHEST)
        cells = base_count * base_count
        r.kf[pixels:pixels + cells, :] = g_grid[0:cells, :]
        small = jnp.sum(r.sums[...], axis=1)
        at = cfg.small_at + small.shape[0]
        r.kf[cfg.small_at:at, :] = small
        small_up = jnp.sum(r.sums_up[...], axis=0, keepdims=True)
        for c in range(ff_chunks):
            r.kf[at + c:at + c + 1, :] = small_up[:, c * width:(c + 1) * width]
        r.gk[0:r.kf.shape[0], :] = r.kf[...].astype(BF)
        if cfg.groups[3].rows > r.kf.shape[0]:
            more = cfg.groups[3].rows - r.kf.shape[0]
            r.gk[r.kf.shape[0]:, :] = jnp.zeros((more, width), BF)

    def step(*sums):
        if COMM:
            for one in sums:
                if one.left():
                    one.step()

    for i in range(slots):
        repeat(embed, i)
        if i + 1 < slots:
            z_all(COT, i, begin)
        repeat(attend, i)
    for i in range(slots):
        repeat(mlp, i)
    repeat(grads_d)
    step(sum_d)
    send_out(slots - 1)
    repeat(grads_u)
    step(sum_u, sum_d)
    repeat(attend_back, 0)
    step(sum_u)
    for i in range(1, slots):
        repeat(attend_back, i)
    repeat(grads_q)
    step(sum_q, sum_d)
    repeat(embed_back, 0)
    step(sum_q)
    for i in range(1, slots):
        repeat(embed_back, i)
    repeat(grads_k)
    step(sum_k, sum_u, sum_k, sum_d, sum_q, sum_k, sum_u, sum_d, sum_k, sum_q)
    for i in range(slots):
        send_gp(i)
    send_tail()
    step(sum_u, sum_k, sum_q, sum_d, sum_u, sum_k, sum_q, sum_d)
    while COMM and any(one.left() for one in groups):
        step(sum_d, sum_q, sum_k, sum_u)
    if COMM:
        for slot in range(slots):
            z_all(MAIN, slot, sent)
            z_all(COT, slot, sent)
            for d in range(1, n_strip):
                out_copy(slot, d).wait()
                gp_copy(slot, d).wait()
            own_out(slot).wait()
            own_gp(slot).wait()
        z_all(TAIL, 0, sent)
        for d in range(1, n_strip):
            gpt_copy(0, d).wait()
        own_gpt(0).wait()


def finish_kernel(cfg, *refs):
    r = SimpleNamespace(**dict(zip(cfg.names, refs)))
    width, ff, slots = cfg.width, cfg.ff, cfg.slots
    pixels, area, main_w = cfg.pixels, cfg.area, cfg.main_w
    tail = pixels - main_w
    ff_chunks = ff // width
    copies = []

    def load(k, src, dst):
        copy = pltpu.make_async_copy(src, dst, r.sem.at[k])
        copy.start()
        return copy

    def send(src, dst, k):
        copy = pltpu.make_async_copy(src, dst, r.sem.at[k])
        copy.start()
        copies.append(copy)

    loads = [
        load(9, r.gk.at[0:r.kf.shape[0], :], r.tail_in),
        load(10, r.gd, r.gd_in),
        load(11, r.gu, r.gu_in),
        load(12, r.gp_main, r.main_in),
        load(13, r.gp_tail, r.last_in),
        load(14, r.out_in, r.out_buf),
        load(15, r.gq, r.gq_in),
    ]
    loads[0].wait()
    r.kf[...] = r.tail_in[...].astype(F32)
    pinv = r.pinv[...].astype(BF)
    for c in range(3):
        part = r.kf[c * area:(c + 1) * area, :].astype(BF)
        r.base[c] = tn(pinv, part)
        send(r.base.at[c], r.g_base.at[c], 1 + c)
    loads[1].wait()
    r.down[...] = r.gd_in[0:ff, :].astype(F32)
    r.wo[...] = r.gd_in[ff:ff + width, :].astype(F32)
    send(r.wo, r.g_out, 7)
    send(r.down, r.g_down, 4)
    loads[2].wait()
    for n in range(ff // 128):
        r.up[:, n * 128:(n + 1) * 128] = r.gu_in[n * width:(n + 1) * width, :].astype(F32)
    send(r.up, r.g_up, 5)
    loads[6].wait()
    pairs = width // 128
    for n in range(3 * pairs):
        r.qkv[:, n * 128:(n + 1) * 128] = r.gq_in[n * width:(n + 1) * width, :].astype(F32)
    send(r.qkv, r.g_qkv, 6)
    loads[5].wait()
    send(r.out_buf, r.output, 0)
    loads[3].wait()
    loads[4].wait()
    for image in range(r.gp.shape[0]):
        r.gp[image, :, 0:main_w] = r.main_in[image]
        start = (image % slots) * (128 // slots)
        last = r.last_in[image // slots].astype(F32)[:, start:start + tail]
        r.gp[image, :, main_w:pixels] = last.astype(BF)
    send(r.gp, r.g_patches, 8)
    small = r.kf[cfg.small_at:cfg.small_at + 16, :]
    for b in range(cfg.base_count):
        at = pixels + b * cfg.base_count
        r.g_grid[b] = r.kf[at:at + cfg.base_count, :]
    r.g_bias_embed[...] = small[0]
    r.g_gain[...] = small[1:3]
    r.g_shift[...] = small[3:5]
    r.g_attn[...] = small[5:8]
    r.g_bias_down[...] = small[8]
    for c in range(ff_chunks):
        r.g_bias_up[c * width:(c + 1) * width] = small[9 + c]
    for copy in copies:
        copy.wait()


def per_device(cfg, patches, pinv, base_embed, bias_embed, pos_grid, pos_index, pos_frac, norm_gain,
               norm_shift, w_qkv, bias_attn, w_out, w_up, bias_up, w_down, bias_down, cotangent):
    images, strip_rows, pixels = patches.shape
    width, ff = w_up.shape
    n_img, n_strip = cfg.n_img, cfg.n_strip
    slots = images // n_strip
    seq = strip_rows * n_strip
    base_count = pos_grid.shape[0]
    area = pinv.shape[0]
    main_w = pixels // 128 * 128
    core = [(IMG, 1, min(2, n_img))]
    plane = [(IMG, 2, min(4, n_img // 2))] if n_img > 2 else []
    stages = core + plane + [(STRIP, 1, n_strip)]
    halves = [(STRIP, 1, 2), (STRIP, 2, n_strip // 2)] if n_strip % 2 == 0 else [(STRIP, 1, n_strip)]
    left = [(IMG, 8, n_img // 8)] if n_img > 8 else []
    cells = base_count * base_count
    small_at = -(-(pixels + cells) // 8) * 8
    k_rows = -(-(small_at + 9 + ff // width) // 128) * 128

    def sum_of(values, lanes, order, extras):
        unit = 16 * math.prod(s[2] for s in order)
        return SimpleNamespace(rows=-(-(values // lanes) // unit) * unit, lanes=lanes, stages=order,
                               extras=extras + left)

    groups = [sum_of((ff + width) * width, width, stages, []), sum_of(ff * width, 128, stages, []),
              sum_of(3 * width * width, 128, stages, []),
              sum_of(k_rows * width, width, core + plane, halves)]
    conf = SimpleNamespace(n_strip=n_strip, strip_rows=strip_rows, slots=slots, seq=seq, width=width, ff=ff,
                           pixels=pixels, area=area, main_w=main_w, grid_side=pos_frac.shape[1],
                           base_count=base_count, stages=stages, left=left, groups=groups,
                           small_at=small_at)
    vmem = pl.BlockSpec(memory_space=pltpu.VMEM)
    hbm = pl.BlockSpec(memory_space=pl.ANY)
    ins = dict(
        patches=(patches, hbm), cotangent=(cotangent, hbm), base_embed=(base_embed, hbm),
        w_qkv=(w_qkv, hbm), w_out=(w_out, hbm), w_up=(w_up, hbm), w_down=(w_down, hbm),
        pinv=(pinv, vmem), bias_embed=(bias_embed, vmem), pos_grid=(pos_grid, vmem),
        pos_index=(pos_index, vmem), pos_frac=(pos_frac, vmem), norm_gain=(norm_gain, vmem),
        norm_shift=(norm_shift, vmem), bias_attn=(bias_attn, vmem),
        bias_up=(bias_up, vmem), bias_down=(bias_down, vmem),
    )
    outs = dict(
        output=jax.ShapeDtypeStruct((images, strip_rows, width), BF),
        gp_main=jax.ShapeDtypeStruct((images, strip_rows, main_w), BF),
        gp_tail=jax.ShapeDtypeStruct((n_strip, strip_rows, 128), BF),
        **dict(zip(("gd_out", "gu_out", "gq_out", "gk_out"),
                   (jax.ShapeDtypeStruct((g.rows, g.lanes), BF) for g in groups))),
    )
    V = pltpu.VMEM
    DMA = pltpu.SemaphoreType.DMA
    scratch = dict(
        wqkv=V(w_qkv.shape, BF), wout=V(w_out.shape, BF), wup=V(w_up.shape, BF), wdown=V(w_down.shape, BF),
        wide=V((max(3 * base_embed.shape[1], 3 * slots * seq), width), F32),
        ptails=V((images, strip_rows, pixels - main_w), BF), packed=V((n_strip, strip_rows, 128), BF),
        pmain=V((slots, seq, main_w), BF), ptail=V((seq, 128), BF), cot=V((slots, seq, width), BF),
        kf=V((k_rows, width), F32), kmain=V((main_w, width), BF), ktail=V((slots, 128, width), BF),
        stage=V((128, width), F32), table=V((-(-cells // 8) * 8, seq), F32), posb=V((seq, width), F32),
        normed=V((slots, seq, width), BF), unit=V((slots, seq, width), BF),
        inv=V((slots, seq, 128), F32), qkv=V((slots, seq, 3 * width), BF),
        expo=V((slots, width // HD, seq, seq), BF),
        att=V((slots, seq, width), BF), nm=V((slots, seq, width), BF),
        act=V((slots, seq, ff), BF), gup=V((slots, seq, ff), BF), outb=V((slots, seq, width), BF),
        gb=V((slots, seq, width), BF), datt=V((slots, seq, width), BF),
        tk=V((width // 128, 128, seq), BF), tv=V((width // 128, 128, seq), BF),
        gproj=V((slots, seq, 3 * width), BF), gpt=V((seq, 128), BF),
        sums=V((9, 8, width), F32), sums_up=V((8, ff), F32),
        gd=V((groups[0].rows, groups[0].lanes), BF), gu=V((groups[1].rows, groups[1].lanes), BF),
        gq=V((groups[2].rows, groups[2].lanes), BF), gk=V((groups[3].rows, groups[3].lanes), BF),
    )
    reduce_scratch = []
    for g in groups:
        size = g.rows
        for stage in g.stages:
            size //= stage[2]
            reduce_scratch.append(V((stage[2] - 1, size, g.lanes), BF))
        reduce_scratch += [V((stage[2] - 1, size, g.lanes), BF) for stage in g.extras]
        many = max([s[2] - 1 for s in g.extras] + [1])
        reduce_scratch += [DMA((len(g.stages), 3))] * 4 + [DMA((max(len(g.extras), 1), many))] * 2 + [DMA((1,))]
    scratch.update(
        load_sem=DMA((8 + 2 * slots,)), zin_s=DMA((2 * slots + 1, n_strip - 1)),
        zin_r=DMA((2 * slots + 1, n_strip - 1)), zout_s=DMA((2 * slots + 1, n_strip - 1)),
        zout_r=DMA((2 * slots + 1, n_strip - 1)), own_sem=DMA((2 * slots + 1,)),
    )
    conf.names = list(ins) + list(outs) + list(scratch)
    results = pl.pallas_call(
        functools.partial(layer_kernel, conf),
        out_shape=list(outs.values()),
        in_specs=[spec for _, spec in ins.values()],
        out_specs=[hbm] * len(outs),
        scratch_shapes=list(scratch.values()) + reduce_scratch,
        compiler_params=pltpu.CompilerParams(
            collective_id=0 if COMM else None, has_side_effects=True, vmem_limit_bytes=60 << 20),
        name="layer",
    )(*[value for value, _ in ins.values()])
    output, gp_main, gp_tail, gd, gu, gq, gk = results

    f_ins = dict(out_in=(output, hbm), gp_main=(gp_main, hbm), gp_tail=(gp_tail, hbm),
                 gd=(gd, hbm), gu=(gu, hbm), gq=(gq, hbm), gk=(gk, hbm), pinv=(pinv, vmem))
    shape = jax.ShapeDtypeStruct
    f_outs = dict(
        output=(shape(output.shape, BF), hbm), g_patches=(shape(patches.shape, BF), hbm),
        g_base=(shape(base_embed.shape, F32), hbm), g_bias_embed=(shape((width,), F32), vmem),
        g_grid=(shape(pos_grid.shape, F32), vmem), g_gain=(shape(norm_gain.shape, F32), vmem),
        g_shift=(shape(norm_shift.shape, F32), vmem), g_qkv=(shape(w_qkv.shape, F32), hbm),
        g_attn=(shape(bias_attn.shape, F32), vmem), g_out=(shape(w_out.shape, F32), hbm),
        g_up=(shape(w_up.shape, F32), hbm), g_bias_up=(shape((ff,), F32), vmem),
        g_down=(shape(w_down.shape, F32), hbm), g_bias_down=(shape((width,), F32), vmem),
    )
    f_scratch = dict(
        kf=V((k_rows, width), F32), base=V(base_embed.shape, F32), down=V(w_down.shape, F32),
        up=V(w_up.shape, F32), qkv=V(w_qkv.shape, F32), wo=V(w_out.shape, F32), gp=V(patches.shape, BF),
        tail_in=V((k_rows, width), BF), gd_in=V(gd.shape, BF), gu_in=V(gu.shape, BF), gq_in=V(gq.shape, BF),
        main_in=V(gp_main.shape, BF), last_in=V(gp_tail.shape, BF), out_buf=V(output.shape, BF), sem=DMA((16,)),
    )
    f_conf = SimpleNamespace(**dict(vars(conf), names=list(f_ins) + list(f_outs) + list(f_scratch)))
    final = pl.pallas_call(
        functools.partial(finish_kernel, f_conf),
        out_shape=[s for s, _ in f_outs.values()],
        in_specs=[spec for _, spec in f_ins.values()],
        out_specs=[spec for _, spec in f_outs.values()],
        scratch_shapes=list(f_scratch.values()),
        compiler_params=pltpu.CompilerParams(vmem_limit_bytes=56 << 20),
        name="finish",
    )(*[value for value, _ in f_ins.values()])
    (output, g_patches, g_base, g_bias_embed, g_grid, g_gain, g_shift, g_qkv, g_attn, g_out, g_up,
     g_bias_up, g_down, g_bias_down) = final
    return (output, g_patches, g_base, g_bias_embed, g_grid, g_gain, g_shift, g_qkv, g_attn, g_out, g_up,
            g_bias_up, g_down, g_bias_down)


def solution(mesh):
    cfg = SimpleNamespace(n_img=mesh.shape[IMG], n_strip=mesh.shape[STRIP])
    split = P(IMG, STRIP, None)
    return jax.shard_map(
        functools.partial(per_device, cfg), mesh=mesh,
        in_specs=(split,) + (P(),) * 15 + (split,),
        out_specs=(split, split) + (P(),) * 12, check_vma=False,
    )
```

```python
import functools
import math
from types import SimpleNamespace

import jax
import jax.numpy as jnp
from jax import lax
from jax.experimental import pallas as pl
from jax.experimental.pallas import tpu as pltpu
from jax.sharding import PartitionSpec as P

HD = 64
EPSILON = 1e-06
MESH = pl.DeviceIdType.MESH
HIGHEST = lax.Precision.HIGHEST
BF = jnp.bfloat16
F32 = jnp.float32
COMM = True
MAIN, TAIL, COT = 0, 1, 2
IMG, STRIP = "img", "strip"
REP = {}


def begin(copy):
    copy.start()


def landed(copy):
    copy.wait_recv()


def sent(copy):
    copy.wait_send()


def nn(a, b, precision=None):
    return lax.dot_general(
        a, b, (((1,), (0,)), ((), ())), precision=precision, preferred_element_type=F32
    )


def nt(a, b):
    return lax.dot_general(a, b, (((1,), (1,)), ((), ())), preferred_element_type=F32)


def tn(a, b, precision=None):
    return lax.dot_general(
        a, b, (((0,), (0,)), ((), ())), precision=precision, preferred_element_type=F32
    )


def fold8(x):
    return jnp.sum(x.reshape(x.shape[0] // 8, 8, x.shape[1]), axis=0)


def rows_of(start, size):
    return pl.ds(pl.multiple_of(start, 16), size)


def chunk_of(rows):
    best = 16
    for size in range(16, 257, 16):
        if rows % size == 0:
            best = size
    return best


class Reduce:
    def __init__(self, group, grad, out, recv, extra_recv, sems):
        rows, stages = group.rows, group.stages
        self.stages, self.extras, self.done, self.rows = stages, group.extras, 0, rows
        self.grad, self.out, self.recv, self.extra_recv = grad, out, recv, extra_recv
        self.rs_s, self.rs_r, self.ag_s, self.ag_r, self.ex_s, self.ex_r, self.loc = sems
        count = len(stages)
        self.phases = [(self.rs_start, self.rs_finish, k) for k in range(count)]
        self.phases += [(self.ex_start, self.ex_finish, k) for k in range(len(self.extras))]
        for k in range(count - 1, -1, -1):
            if group.relay and stages[k] == (IMG, 2, 4):
                self.phases.append((self.near_start, self.near_finish, k))
                self.phases.append((self.far_start, self.far_finish, k))
            else:
                self.phases.append((self.ag_start, self.ag_finish, k))
        sizes, offsets = [rows], [0]
        for axis, unit, size in stages:
            mine = self.index(axis, unit, size)
            sizes.append(sizes[-1] // size)
            offsets.append(offsets[-1] + mine * sizes[-1])
        self.sizes, self.offsets = sizes, offsets

    @staticmethod
    def index(axis, unit, size):
        return (lax.axis_index(axis) // unit) % size

    def peer(self, stage, d):
        axis, unit, size = stage
        mine = self.index(axis, unit, size)
        there = (mine + d) % size
        return {axis: lax.axis_index(axis) + unit * (there - mine)}, there

    def rs_copies(self, k):
        size, sub = self.stages[k][2], self.sizes[k + 1]
        copies = []
        for d in range(1, size):
            device, there = self.peer(self.stages[k], d)
            copies.append(
                pltpu.make_async_remote_copy(
                    src_ref=self.grad.at[rows_of(self.offsets[k] + there * sub, sub), :],
                    dst_ref=self.recv[k].at[d - 1],
                    send_sem=self.rs_s.at[k, d - 1],
                    recv_sem=self.rs_r.at[k, d - 1],
                    device_id=device,
                    device_id_type=MESH,
                )
            )
        return copies

    def rs_start(self, k):
        for copy in self.rs_copies(k):
            copy.start()

    def rs_finish(self, k):
        copies = self.rs_copies(k)
        for copy in copies:
            copy.wait_recv()
        size, sub, first = self.stages[k][2], self.sizes[k + 1], self.offsets[k + 1]
        step = chunk_of(sub)

        def body(b, carry):
            rows = rows_of(first + b * step, step)
            total = self.grad[rows, :].astype(F32)
            for d in range(size - 1):
                total = total + self.recv[k][d, rows_of(b * step, step), :].astype(F32)
            self.grad[rows, :] = total.astype(BF)
            return carry

        lax.fori_loop(0, sub // step, body, 0)
        for copy in copies:
            copy.wait_send()

    def piece(self):
        return self.grad.at[rows_of(self.offsets[-1], self.sizes[-1]), :]

    def ex_copies(self, k):
        copies = []
        for d in range(1, self.extras[k][2]):
            device, _ = self.peer(self.extras[k], d)
            copies.append(
                pltpu.make_async_remote_copy(
                    src_ref=self.piece(),
                    dst_ref=self.extra_recv[k].at[d - 1],
                    send_sem=self.ex_s.at[k, d - 1],
                    recv_sem=self.ex_r.at[k, d - 1],
                    device_id=device,
                    device_id_type=MESH,
                )
            )
        return copies

    def ex_start(self, k):
        for copy in self.ex_copies(k):
            copy.start()

    def ex_finish(self, k):
        for copy in self.ex_copies(k):
            copy.wait()
        rows = rows_of(self.offsets[-1], self.sizes[-1])
        total = self.grad[rows, :].astype(F32)
        for d in range(self.extras[k][2] - 1):
            total = total + self.extra_recv[k][d].astype(F32)
        self.grad[rows, :] = total.astype(BF)

    def ag_copies(self, k):
        size, sub = self.stages[k][2], self.sizes[k + 1]
        region = self.out.at[rows_of(self.offsets[k + 1], sub), :]
        source = self.piece() if k == len(self.stages) - 1 else region
        copies = []
        for d in range(1, size):
            device, _ = self.peer(self.stages[k], d)
            copies.append(
                pltpu.make_async_remote_copy(
                    src_ref=source,
                    dst_ref=region,
                    send_sem=self.ag_s.at[k, d - 1],
                    recv_sem=self.ag_r.at[k, d - 1],
                    device_id=device,
                    device_id_type=MESH,
                )
            )
        return copies

    def plane(self, k):
        mine = self.index(*self.stages[k])
        return mine, mine + 1 - 2 * (mine % 2), mine + 2 - 4 * (mine // 2)

    def plane_copy(self, k, slot, piece, part, there):
        mine, _, _ = self.plane(k)
        rows = self.sizes[k + 1] // (1 if part is None else 2)
        start = self.offsets[k] + piece * self.sizes[k + 1] + (part or 0) * rows
        region = self.out.at[rows_of(start, rows), :]
        return pltpu.make_async_remote_copy(
            src_ref=region, dst_ref=region, send_sem=self.ag_s.at[k, slot], recv_sem=self.ag_r.at[k, slot],
            device_id={IMG: lax.axis_index(IMG) + 2 * (there - mine)}, device_id_type=MESH)

    def near_copies(self, k):
        mine, along_x, along_y = self.plane(k)
        return [self.plane_copy(k, 0, mine, None, along_x), self.plane_copy(k, 1, mine, None, along_y)]

    def far_copies(self, k):
        _, along_x, along_y = self.plane(k)
        return [self.plane_copy(k, 2, along_x, 0, along_y), self.plane_copy(k, 3, along_y, 1, along_x)]

    def near_start(self, k):
        for copy in self.near_copies(k):
            copy.start()

    def near_finish(self, k):
        for copy in self.near_copies(k):
            copy.wait()

    def far_start(self, k):
        for copy in self.far_copies(k):
            copy.start()

    def far_finish(self, k):
        for copy in self.far_copies(k):
            copy.wait()

    def local_copy(self):
        region = self.out.at[rows_of(self.offsets[-1], self.sizes[-1]), :]
        return pltpu.make_async_copy(self.piece(), region, self.loc.at[0])

    def left(self):
        return self.done <= len(self.phases)

    def step(self):
        n = self.done
        self.done += 1
        if n > 0:
            self.phases[n - 1][1](self.phases[n - 1][2])
        if n < len(self.phases):
            self.phases[n][0](self.phases[n][2])

    def ag_start(self, k):
        if k == len(self.stages) - 1:
            self.local_copy().start()
        for copy in self.ag_copies(k):
            copy.start()

    def ag_finish(self, k):
        if k == len(self.stages) - 1:
            self.local_copy().wait()
        for copy in self.ag_copies(k):
            copy.wait()


def layer_kernel(cfg, *refs):
    r = SimpleNamespace(**dict(zip(cfg.names, refs)))
    n_strip, strip_rows, slots = cfg.n_strip, cfg.strip_rows, cfg.slots
    seq, width, ff, pixels, area = cfg.seq, cfg.width, cfg.ff, cfg.pixels, cfg.area
    main_w = cfg.main_w
    tail = pixels - main_w
    grid_side, base_count = cfg.grid_side, cfg.base_count
    pairs = width // 128
    depth = r.base_embed.shape[1]
    ff_chunks = ff // width
    me = lax.axis_index(STRIP)
    group = 2 if n_strip % 2 == 0 else 1
    block = group * strip_rows
    blocks = n_strip // group

    def repeat(fn, *args):
        count = REP.get(fn.__name__, 1)
        if count == 1:
            fn(*args)
        else:
            lax.fori_loop(0, count, lambda t, c: (fn(*args), c)[1], 0)

    groups = []
    at = len(refs) - sum(len(g.stages) + len(g.extras) + 7 for g in cfg.groups)
    for g, grad, out in zip(cfg.groups, (r.gd, r.gu, r.gq, r.gk), (r.gd_out, r.gu_out, r.gq_out, r.gk_out)):
        n, e = len(g.stages), len(g.extras)
        groups.append(Reduce(g, grad, out, refs[at:at + n], refs[at + n:at + n + e],
                             refs[at + n + e:at + n + e + 7]))
        at += n + e + 7
    sum_d, sum_u, sum_q, sum_k = groups
    if COMM:
        barrier = pltpu.get_barrier_semaphore()
        greeted = 0
        for stage in cfg.stages + cfg.left:
            for d in range(1, stage[2]):
                device, _ = sum_k.peer(stage, d)
                pl.semaphore_signal(barrier, inc=1, device_id=device, device_id_type=MESH)
                greeted += 1

    loads = [
        pltpu.make_async_copy(r.w_qkv, r.wqkv, r.load_sem.at[0]),
        pltpu.make_async_copy(r.w_out, r.wout, r.load_sem.at[1]),
        pltpu.make_async_copy(r.w_up, r.wup, r.load_sem.at[2]),
        pltpu.make_async_copy(r.w_down, r.wdown, r.load_sem.at[3]),
    ]
    base_loads = [
        pltpu.make_async_copy(r.base_embed.at[c], r.wide.at[rows_of(c * depth, depth), :], r.load_sem.at[4 + c])
        for c in range(3)
    ]
    tails_load = pltpu.make_async_copy(
        r.patches.at[:, :, main_w:pixels], r.ptails, r.load_sem.at[7]
    )
    own_loads = []
    for slot in range(slots):
        rows = rows_of(me * strip_rows, strip_rows)
        own_loads.append(pltpu.make_async_copy(
            r.patches.at[me * slots + slot, :, 0:main_w], r.pmain.at[slot, rows, :],
            r.load_sem.at[8 + slot]))
        own_loads.append(pltpu.make_async_copy(
            r.cotangent.at[me * slots + slot], r.cot.at[slot, rows, :],
            r.load_sem.at[8 + slots + slot]))
    tails_load.start()
    for copy in base_loads:
        copy.start()
    for copy in own_loads:
        copy.start()
    for copy in loads:
        copy.start()

    def z_in(kind, slot, d):
        home = (me + d) % n_strip
        rows = rows_of(me * strip_rows, strip_rows)
        image = home * slots + slot
        if kind == MAIN:
            src, dst, k = r.patches.at[image, :, 0:main_w], r.pmain.at[slot, rows, :], slot
        elif kind == TAIL:
            src, dst, k = r.packed.at[home], r.ptail.at[rows, :], slots
        else:
            src, dst, k = r.cotangent.at[image], r.cot.at[slot, rows, :], slots + 1 + slot
        return pltpu.make_async_remote_copy(
            src_ref=src, dst_ref=dst, send_sem=r.zin_s.at[k, d - 1],
            recv_sem=r.zin_r.at[k, d - 1], device_id={STRIP: home}, device_id_type=MESH)

    def z_all(kind, slot, act):
        if not COMM:
            return
        for d in range(1, n_strip):
            act(z_in(kind, slot, d))

    if COMM:
        pl.semaphore_wait(barrier, greeted)
    z_all(MAIN, 0, begin)

    tails_load.wait()
    zero_tail = jnp.zeros((strip_rows, 128 // slots - tail), F32)
    for home in range(n_strip):
        parts = []
        for slot in range(slots):
            parts.append(r.ptails[home * slots + slot].astype(F32))
            parts.append(zero_tail)
        r.packed[home] = jnp.concatenate(parts, axis=1).astype(BF)
    z_all(TAIL, 0, begin)
    r.ptail[rows_of(me * strip_rows, strip_rows), :] = r.packed[me]

    def make_kernel():
        pinv = r.pinv[...].astype(BF)
        r.kf[...] = jnp.zeros_like(r.kf)
        for c in range(3):
            if not REP:
                base_loads[c].wait()
            r.kf[c * area:(c + 1) * area, :] = nn(pinv, r.wide[c * depth:(c + 1) * depth, :].astype(BF))
        kernel = r.kf[...].astype(BF)
        r.kmain[...] = kernel[0:main_w]
        for slot in range(slots):
            r.stage[...] = jnp.zeros_like(r.stage)
            at = slot * (128 // slots)
            r.stage[at:at + tail, :] = r.kf[main_w:pixels, :]
            r.ktail[slot] = r.stage[...].astype(BF)

    if REP:
        for copy in base_loads:
            copy.wait()
    repeat(make_kernel)

    def make_position():
        cells = r.table.shape[0]
        cell = lax.broadcasted_iota(jnp.int32, (cells, grid_side), 0).astype(F32)
        grid_row = jnp.floor((cell + 0.5) / base_count)
        corner = (grid_row, cell - grid_row * base_count)
        place = lax.broadcasted_iota(jnp.int32, (grid_side, seq), 1).astype(F32)
        which = lax.broadcasted_iota(jnp.int32, (grid_side, seq), 0).astype(F32)
        patch_row = jnp.floor((place + 0.5) / grid_side)
        patch = (patch_row, place - patch_row * grid_side)
        product = None
        for t in range(2):
            low = r.pos_index[t, 0:1, :].astype(F32)
            high = r.pos_index[t, 1:2, :].astype(F32)
            frac = r.pos_frac[t:t + 1, :]
            entry = (1.0 - frac) * (corner[t] == low).astype(F32) + frac * (corner[t] == high).astype(F32)
            spread = nn(entry, (patch[t] == which).astype(F32), HIGHEST)
            product = spread if product is None else product * spread
        valid = lax.broadcasted_iota(jnp.int32, (cells, seq), 0) < base_count * base_count
        r.table[...] = jnp.where(valid, product, 0.0)
        r.stage[...] = jnp.zeros_like(r.stage)
        for b in range(base_count):
            r.stage[b * base_count:(b + 1) * base_count, :] = r.pos_grid[b]
        r.posb[...] = tn(r.table[...], r.stage[0:cells, :], HIGHEST) + r.bias_embed[...]

    repeat(make_position)
    r.sums[...] = jnp.zeros_like(r.sums)
    r.sums_up[...] = jnp.zeros_like(r.sums_up)
    for one, used in zip(groups, ((ff + width), ff * pairs, 3 * width * pairs)):
        if one.rows > used:
            r_pad = one.grad.shape
            one.grad[used:, :] = jnp.zeros((r_pad[0] - used, r_pad[1]), BF)
    for copy in loads:
        copy.wait()
    for copy in own_loads:
        copy.wait()

    def wide_rows(k, rows):
        return rows_of(k * seq + rows.start, rows.size)

    lane = lax.broadcasted_iota(jnp.int32, (1, 128), 1)
    first_head = lane < HD

    def norm(x, gain, shift):
        center = x - jnp.mean(x, axis=-1, keepdims=True)
        inv = lax.rsqrt(jnp.mean(center * center, axis=-1, keepdims=True) + EPSILON)
        unit = center * inv
        return unit * gain + shift, unit, inv

    def norm_back(g, unit, inv, gain):
        gu = g * gain
        return inv * (
            gu - jnp.mean(gu, axis=-1, keepdims=True)
            - unit * jnp.mean(gu * unit, axis=-1, keepdims=True)
        )

    def add_sum(row, x):
        r.sums[row] += fold8(x)

    B_EMBED, GAIN, SHIFT, B_Q, B_V, B_O, B_DOWN = 0, 1, 3, 5, 6, 7, 8

    def near_first(t):
        return (t + me // group) % blocks

    def wait_rows(t, kind, slot):
        if not COMM:
            return
        for part in range(group):
            d = (me - t * group - part + n_strip) % n_strip

            @pl.when(d > 0)
            def _():
                z_in(kind, slot, d).wait_recv()

    def embed(i):
        def body(t, carry):
            b = near_first(t)
            rows = rows_of(b * block, block)
            wait_rows(b, MAIN, i)
            if i == 0:
                wait_rows(b, TAIL, 0)

            @pl.when(t == 0)
            def _():
                if i + 1 < slots:
                    z_all(MAIN, i + 1, begin)
                else:
                    z_all(COT, i, begin)

            emb = (
                nn(r.pmain[i, rows, :], r.kmain[...])
                + nn(r.ptail[rows, :], r.ktail[i])
                + r.posb[rows, :]
            )
            r.wide[wide_rows(i, rows), :] = emb
            y, unit, inv = norm(emb, r.norm_gain[0:1, :], r.norm_shift[0:1, :])
            y = y.astype(BF)
            r.normed[i, rows, :] = y
            r.unit[i, rows, :] = unit.astype(BF)
            r.inv[i, rows, :] = jnp.broadcast_to(inv, (block, 128))
            q = nn(y, r.wqkv[:, 0:width]) + r.bias_attn[0:1, :]
            r.qkv[i, rows, 0:width] = (q * (1.0 / math.sqrt(HD))).astype(BF)
            r.qkv[i, rows, width:2 * width] = nn(y, r.wqkv[:, width:2 * width]).astype(BF)
            v = nn(y, r.wqkv[:, 2 * width:3 * width]) + r.bias_attn[1:2, :]
            r.qkv[i, rows, 2 * width:3 * width] = v.astype(BF)
            return carry

        lax.fori_loop(0, blocks, body, 0)

    def lanes(p, part=0):
        return slice(part * width + p * 128, part * width + (p + 1) * 128)

    def ahead(tasks, front, rest, depth):
        ready = [front(*task) for task in tasks[:depth]]
        for n, task in enumerate(tasks):
            if n + depth < len(tasks):
                ready.append(front(*tasks[n + depth]))
            rest(*task, ready[n])
            ready[n] = None

    heads = [(p, h) for p in range(pairs) for h in range(2)]

    def pick(x, h):
        return jnp.where(first_head == (h == 0), x, jnp.zeros_like(x))

    def attend(i):
        outs, recips = {}, {}

        def front(p, h):
            return nt(pick(r.qkv[i, :, lanes(p)], h), r.qkv[i, :, lanes(p, 1)])

        def rest(p, h, s):
            e = jnp.exp(s - jnp.max(s, axis=-1, keepdims=True))
            recip = 1.0 / jnp.sum(e, axis=-1, keepdims=True)
            e = e.astype(BF)
            r.expo[i, 2 * p + h] = e
            outs[h] = nn(e, r.qkv[i, :, lanes(p, 2)]) * recip
            recips[h] = jnp.broadcast_to(recip, (seq, 128))
            if h == 1:
                r.att[i, :, lanes(p)] = jnp.where(first_head, outs[0], outs[1]).astype(BF)
                r.wide[(2 * slots + i) * seq:(2 * slots + i + 1) * seq, lanes(p)] = jnp.where(first_head, recips[0], recips[1])

        ahead(heads, front, rest, 2)

    c0 = math.sqrt(2.0 / math.pi)
    c1 = 0.044715

    def out_copy(i, d):
        strip = (me + d) % n_strip
        return pltpu.make_async_remote_copy(
            src_ref=r.outb.at[i, rows_of(strip * strip_rows, strip_rows), :],
            dst_ref=r.output.at[me * slots + i],
            send_sem=r.zout_s.at[i, d - 1], recv_sem=r.zout_r.at[i, d - 1],
            device_id={STRIP: strip}, device_id_type=MESH)

    def own_out(i):
        return pltpu.make_async_copy(
            r.outb.at[i, rows_of(me * strip_rows, strip_rows), :],
            r.output.at[me * slots + i], r.own_sem.at[i])

    def send_out(i):
        if not COMM:
            return
        for d in range(1, n_strip):
            out_copy(i, d).start()
        own_out(i).start()

    def mlp(i):
        def body(n, carry):
            t = near_first(n)
            rows = rows_of(t * block, block)
            wait_rows(t, COT, i)
            if i > 0:

                @pl.when(n == blocks - 1)
                def _():
                    send_out(i - 1)

            mid = r.wide[wide_rows(i, rows), :] + nn(r.att[i, rows, :], r.wout[...]) + r.bias_attn[2:3, :]
            gain = r.norm_gain[1:2, :]
            y, unit, inv = norm(mid, gain, r.norm_shift[1:2, :])
            y = y.astype(BF)
            r.nm[i, rows, :] = y
            cot = r.cot[i, rows, :]

            def front(cols):
                return nn(y, r.wup[:, cols]), nt(cot, r.wdown[cols, :])

            def rest(cols, ready):
                u = ready[0] + r.bias_up[cols]
                square = u * u
                half = 0.5 + 0.5 * jnp.tanh(u * (c0 + (c0 * c1) * square))
                act = u * half
                r.act[i, rows, cols] = act.astype(BF)
                slope = half + (act - act * half) * (2.0 * c0 + (6.0 * c0 * c1) * square)
                gu = ready[1] * slope
                r.gup[i, rows, cols] = gu.astype(BF)
                r.sums_up[:, cols] += fold8(gu)

            ahead([(slice(c, c + 256),) for c in range(0, ff, 256)], front, rest, 1)
            out = mid + r.bias_down[...] + nn(r.act[i, rows, :], r.wdown[...])
            g_nm = nt(r.gup[i, rows, :], r.wup[...])
            r.outb[i, rows, :] = out.astype(BF)
            add_sum(GAIN + 1, g_nm * unit)
            add_sum(SHIFT + 1, g_nm)
            cotf = cot.astype(F32)
            add_sum(B_DOWN, cotf)
            g_mid = cotf + norm_back(g_nm, unit, inv, gain)
            r.wide[wide_rows(slots + i, rows), :] = g_mid
            add_sum(B_O, g_mid)
            gb = g_mid.astype(BF)
            r.gb[i, rows, :] = gb
            r.datt[i, rows, :] = (nt(gb, r.wout[...]) * r.wide[wide_rows(2 * slots + i, rows), :]).astype(BF)
            return carry

        lax.fori_loop(0, blocks, body, 0)

    def ds_slot(p, h):
        wide = -(-seq // 128) * 128
        return (r.act, r.gup)[p % 2].at[slots - 1, :, h * wide:h * wide + seq]

    def attend_back(i):
        gq = {}

        def front(p, h):
            return nt(pick(r.datt[i, :, lanes(p)], h), r.qkv[i, :, lanes(p, 2)])

        def rest(p, h, dp):
            prod = r.datt[i, :, lanes(p)].astype(F32) * r.att[i, :, lanes(p)].astype(F32)
            delta = jnp.sum(pick(prod, h), axis=-1, keepdims=True)
            expo = r.expo[i, 2 * p + h]
            ds = (expo.astype(F32) * (dp - delta)).astype(BF)
            ds_slot(p, h)[...] = ds
            gq[h] = nn(ds, r.qkv[i, :, lanes(p, 1)])
            if h == 0:
                return
            g_q = jnp.where(first_head, gq[0], gq[1]) * (1.0 / math.sqrt(HD))
            r.gproj[i, :, lanes(p)] = g_q.astype(BF)
            q_t, d_t = r.qkv[i, :, lanes(p)].T, r.datt[i, :, lanes(p)].T
            for part in range(2):
                half = slice(part * HD, (part + 1) * HD)
                r.tk[p, half, :] = nn(q_t[half, :], ds_slot(p, part)[...]).astype(BF)
                r.tv[p, half, :] = nn(d_t[half, :], r.expo[i, 2 * p + part]).astype(BF)
            r.gproj[i, :, lanes(p, 1)] = r.tk[p].T
            r.gproj[i, :, lanes(p, 2)] = r.tv[p].T

        ahead(heads, front, rest, 1)

    def gp_copy(i, d):
        strip = (me + d) % n_strip
        return pltpu.make_async_remote_copy(
            src_ref=r.gup.at[i, rows_of(strip * strip_rows, strip_rows), ff - main_w:ff],
            dst_ref=r.gp_main.at[me * slots + i],
            send_sem=r.zout_s.at[slots + i, d - 1], recv_sem=r.zout_r.at[slots + i, d - 1],
            device_id={STRIP: strip}, device_id_type=MESH)

    def own_gp(i):
        return pltpu.make_async_copy(
            r.gup.at[i, rows_of(me * strip_rows, strip_rows), ff - main_w:ff],
            r.gp_main.at[me * slots + i], r.own_sem.at[slots + i])

    def gpt_copy(i, d):
        strip = (me + d) % n_strip
        return pltpu.make_async_remote_copy(
            src_ref=r.gpt.at[rows_of(strip * strip_rows, strip_rows), :],
            dst_ref=r.gp_tail.at[me],
            send_sem=r.zout_s.at[2 * slots, d - 1], recv_sem=r.zout_r.at[2 * slots, d - 1],
            device_id={STRIP: strip}, device_id_type=MESH)

    def own_gpt(i):
        return pltpu.make_async_copy(
            r.gpt.at[rows_of(me * strip_rows, strip_rows), :],
            r.gp_tail.at[me], r.own_sem.at[2 * slots])

    def embed_back(i):
        def body(t, carry):
            rows = rows_of(t * block, block)
            gain = r.norm_gain[0:1, :]
            unit = r.unit[i, rows, :].astype(F32)
            gproj = r.gproj[i, rows, :]
            add_sum(B_Q, gproj[:, 0:width].astype(F32))
            add_sum(B_V, gproj[:, 2 * width:3 * width].astype(F32))
            g_n = nt(gproj, r.wqkv[...])
            add_sum(GAIN, g_n * unit)
            add_sum(SHIFT, g_n)
            inv = r.inv[i, rows, :][:, 0:1]
            g_emb = r.wide[wide_rows(slots + i, rows), :] + norm_back(g_n, unit, inv, gain)
            add_sum(B_EMBED, g_emb)
            ge = g_emb.astype(BF)
            r.act[i, rows, ff - width:ff] = ge
            r.gup[i, rows, ff - main_w:ff] = nt(ge, r.kmain[...]).astype(BF)
            part = nt(ge, r.ktail[i])
            if i > 0:
                part = part + r.gpt[rows, :].astype(F32)
            r.gpt[rows, :] = part.astype(BF)
            return carry

        lax.fori_loop(0, blocks, body, 0)

    def send_gp(i):
        if not COMM:
            return
        for d in range(1, n_strip):
            gp_copy(i, d).start()
        own_gp(i).start()

    def send_tail():
        if not COMM:
            return
        for d in range(1, n_strip):
            gpt_copy(0, d).start()
        own_gpt(0).start()

    def both(ref, cols=slice(None)):
        return ref[:, :, cols].reshape(slots * seq, -1)

    def grads_d():
        lhs = both(r.cot).T
        for c in range(0, ff, 512):
            r.gd[c:c + 512, :] = nn(lhs, both(r.act, slice(c, c + 512))).T.astype(BF)
        r.gd[ff:ff + width, :] = tn(both(r.att), both(r.gb)).astype(BF)

    def grads_u():
        lhs = both(r.nm).T
        for c in range(0, ff, 512):
            part = nn(lhs, both(r.gup, slice(c, c + 512))).astype(BF)
            for n in range(4):
                r.gu[(c // 128 + n) * width:(c // 128 + n + 1) * width, :] = part[:, n * 128:(n + 1) * 128]

    def grads_q():
        lhs = both(r.normed).T
        for c in range(3):
            part = nn(lhs, both(r.gproj, slice(c * width, (c + 1) * width))).astype(BF)
            for n in range(pairs):
                at = (c * pairs + n) * width
                r.gq[at:at + width, :] = part[:, n * 128:(n + 1) * 128]

    def grads_k():
        r.kf[0:main_w, :] = tn(both(r.pmain), both(r.act, slice(ff - width, ff)))
        at = main_w
        total = None
        for slot in range(slots):
            part = tn(r.ptail[...], r.act[slot, :, ff - width:ff])
            start = slot * (128 // slots)
            part = part[start:start + tail, :]
            total = part if total is None else total + part
        r.kf[main_w:pixels, :] = total
        summed = sum(r.act[slot, :, ff - width:ff].astype(F32) for slot in range(slots))
        g_grid = nn(r.table[...], summed, HIGHEST)
        cells = base_count * base_count
        r.kf[pixels:pixels + cells, :] = g_grid[0:cells, :]
        small = jnp.sum(r.sums[...], axis=1)
        at = cfg.small_at + small.shape[0]
        r.kf[cfg.small_at:at, :] = small
        small_up = jnp.sum(r.sums_up[...], axis=0, keepdims=True)
        for c in range(ff_chunks):
            r.kf[at + c:at + c + 1, :] = small_up[:, c * width:(c + 1) * width]
        r.gk[0:r.kf.shape[0], :] = r.kf[...].astype(BF)
        if cfg.groups[3].rows > r.kf.shape[0]:
            more = cfg.groups[3].rows - r.kf.shape[0]
            r.gk[r.kf.shape[0]:, :] = jnp.zeros((more, width), BF)

    def step(*sums):
        if COMM:
            for one in sums:
                if one.left():
                    one.step()

    for i in range(slots):
        repeat(embed, i)
        if i + 1 < slots:
            z_all(COT, i, begin)
        repeat(attend, i)
    for i in range(slots):
        repeat(mlp, i)
    repeat(grads_d)
    step(sum_d)
    send_out(slots - 1)
    repeat(grads_u)
    step(sum_u, sum_d)
    repeat(attend_back, 0)
    step(sum_u)
    for i in range(1, slots):
        repeat(attend_back, i)
    repeat(grads_q)
    step(sum_q, sum_d)
    repeat(embed_back, 0)
    step(sum_q)
    for i in range(1, slots):
        repeat(embed_back, i)
    repeat(grads_k)
    step(sum_k, sum_u, sum_k, sum_d, sum_q, sum_k, sum_u, sum_d, sum_k, sum_q)
    for i in range(slots):
        send_gp(i)
    send_tail()
    if COMM:
        for slot in range(slots):
            z_all(MAIN, slot, sent)
            z_all(COT, slot, sent)
            for d in range(1, n_strip):
                out_copy(slot, d).wait()
            own_out(slot).wait()
        z_all(TAIL, 0, sent)
    step(sum_u, sum_d, sum_k, sum_q, sum_u, sum_d, sum_k, sum_q, sum_u, sum_d)
    while COMM and any(one.left() for one in groups):
        step(sum_d, sum_q, sum_k, sum_u)
    if COMM:
        for slot in range(slots):
            for d in range(1, n_strip):
                gp_copy(slot, d).wait()
            own_gp(slot).wait()
        for d in range(1, n_strip):
            gpt_copy(0, d).wait()
        own_gpt(0).wait()


def finish_kernel(cfg, *refs):
    r = SimpleNamespace(**dict(zip(cfg.names, refs)))
    width, ff, slots = cfg.width, cfg.ff, cfg.slots
    pixels, area, main_w = cfg.pixels, cfg.area, cfg.main_w
    tail = pixels - main_w
    ff_chunks = ff // width
    copies = []

    def load(k, src, dst):
        copy = pltpu.make_async_copy(src, dst, r.sem.at[k])
        copy.start()
        return copy

    def send(src, dst, k):
        copy = pltpu.make_async_copy(src, dst, r.sem.at[k])
        copy.start()
        copies.append(copy)

    loads = [
        load(9, r.gk.at[0:r.kf.shape[0], :], r.tail_in),
        load(10, r.gd, r.gd_in),
        load(11, r.gu, r.gu_in),
        load(12, r.gp_main, r.main_in),
        load(13, r.gp_tail, r.last_in),
        load(14, r.out_in, r.out_buf),
        load(15, r.gq, r.gq_in),
        load(16, r.pinv, r.pinv_in),
    ]
    loads[0].wait()
    r.kf[...] = r.tail_in[...].astype(F32)
    small = r.kf[cfg.small_at:cfg.small_at + 16, :]
    for b in range(cfg.base_count):
        at = pixels + b * cfg.base_count
        r.s_grid[b] = r.kf[at:at + cfg.base_count, :]
    r.s_bias_embed[...] = small[0]
    r.s_gain[...] = small[1:3]
    r.s_shift[...] = small[3:5]
    r.s_attn[...] = small[5:8]
    r.s_bias_down[...] = small[8]
    for c in range(ff_chunks):
        r.s_bias_up[c * width:(c + 1) * width] = small[9 + c]
    few = ((r.s_grid, r.g_grid), (r.s_bias_embed, r.g_bias_embed), (r.s_gain, r.g_gain), (r.s_shift, r.g_shift),
           (r.s_attn, r.g_attn), (r.s_bias_down, r.g_bias_down), (r.s_bias_up, r.g_bias_up))
    for n, (held, place) in enumerate(few):
        send(held, place, 17 + n)
    loads[7].wait()
    pinv = r.pinv_in[...].astype(BF)
    for c in range(3):
        part = r.kf[c * area:(c + 1) * area, :].astype(BF)
        r.base[c] = tn(pinv, part)
        send(r.base.at[c], r.g_base.at[c], 1 + c)
    loads[1].wait()
    r.down[...] = r.gd_in[0:ff, :].astype(F32)
    r.wo[...] = r.gd_in[ff:ff + width, :].astype(F32)
    send(r.wo, r.g_out, 7)
    send(r.down, r.g_down, 4)
    loads[2].wait()
    for n in range(ff // 128):
        r.up[:, n * 128:(n + 1) * 128] = r.gu_in[n * width:(n + 1) * width, :].astype(F32)
    send(r.up, r.g_up, 5)
    loads[6].wait()
    pairs = width // 128
    for n in range(3 * pairs):
        r.qkv[:, n * 128:(n + 1) * 128] = r.gq_in[n * width:(n + 1) * width, :].astype(F32)
    send(r.qkv, r.g_qkv, 6)
    loads[5].wait()
    send(r.out_buf, r.output, 0)
    loads[3].wait()
    loads[4].wait()
    for image in range(r.gp.shape[0]):
        r.gp[image, :, 0:main_w] = r.main_in[image]
        start = (image % slots) * (128 // slots)
        last = r.last_in[image // slots].astype(F32)[:, start:start + tail]
        r.gp[image, :, main_w:pixels] = last.astype(BF)
    send(r.gp, r.g_patches, 8)
    for copy in copies:
        copy.wait()


def per_device(cfg, patches, pinv, base_embed, bias_embed, pos_grid, pos_index, pos_frac, norm_gain,
               norm_shift, w_qkv, bias_attn, w_out, w_up, bias_up, w_down, bias_down, cotangent):
    images, strip_rows, pixels = patches.shape
    width, ff = w_up.shape
    n_img, n_strip = cfg.n_img, cfg.n_strip
    slots = images // n_strip
    seq = strip_rows * n_strip
    base_count = pos_grid.shape[0]
    area = pinv.shape[0]
    main_w = pixels // 128 * 128
    core = [(IMG, 1, min(2, n_img))]
    plane = [(IMG, 2, min(4, n_img // 2))] if n_img > 2 else []
    stages = core + plane + [(STRIP, 1, n_strip)]
    halves = [(STRIP, 1, 2), (STRIP, 2, n_strip // 2)] if n_strip % 2 == 0 else [(STRIP, 1, n_strip)]
    left = [(IMG, 8, n_img // 8)] if n_img > 8 else []
    cells = base_count * base_count
    small_at = -(-(pixels + cells) // 8) * 8
    k_rows = -(-(small_at + 9 + ff // width) // 128) * 128

    def sum_of(values, lanes, order, extras, relay=False):
        unit = 16 * math.prod(s[2] for s in order)
        return SimpleNamespace(rows=-(-(values // lanes) // unit) * unit, lanes=lanes, stages=order,
                               extras=extras + left, relay=relay)

    groups = [sum_of((ff + width) * width, width, stages, [], True), sum_of(ff * width, 128, stages, [], True),
              sum_of(3 * width * width, 128, stages, []),
              sum_of(k_rows * width, width, core + plane, halves)]
    conf = SimpleNamespace(n_strip=n_strip, strip_rows=strip_rows, slots=slots, seq=seq, width=width, ff=ff,
                           pixels=pixels, area=area, main_w=main_w, grid_side=pos_frac.shape[1],
                           base_count=base_count, stages=stages, left=left, groups=groups,
                           small_at=small_at)
    vmem = pl.BlockSpec(memory_space=pltpu.VMEM)
    hbm = pl.BlockSpec(memory_space=pl.ANY)
    ins = dict(
        patches=(patches, hbm), cotangent=(cotangent, hbm), base_embed=(base_embed, hbm),
        w_qkv=(w_qkv, hbm), w_out=(w_out, hbm), w_up=(w_up, hbm), w_down=(w_down, hbm),
        pinv=(pinv, vmem), bias_embed=(bias_embed, vmem), pos_grid=(pos_grid, vmem),
        pos_index=(pos_index, vmem), pos_frac=(pos_frac, vmem), norm_gain=(norm_gain, vmem),
        norm_shift=(norm_shift, vmem), bias_attn=(bias_attn, vmem),
        bias_up=(bias_up, vmem), bias_down=(bias_down, vmem),
    )
    outs = dict(
        output=jax.ShapeDtypeStruct((images, strip_rows, width), BF),
        gp_main=jax.ShapeDtypeStruct((images, strip_rows, main_w), BF),
        gp_tail=jax.ShapeDtypeStruct((n_strip, strip_rows, 128), BF),
        **dict(zip(("gd_out", "gu_out", "gq_out", "gk_out"),
                   (jax.ShapeDtypeStruct((g.rows, g.lanes), BF) for g in groups))),
    )
    V = pltpu.VMEM
    DMA = pltpu.SemaphoreType.DMA
    scratch = dict(
        wqkv=V(w_qkv.shape, BF), wout=V(w_out.shape, BF), wup=V(w_up.shape, BF), wdown=V(w_down.shape, BF),
        wide=V((max(3 * base_embed.shape[1], 3 * slots * seq), width), F32),
        ptails=V((images, strip_rows, pixels - main_w), BF), packed=V((n_strip, strip_rows, 128), BF),
        pmain=V((slots, seq, main_w), BF), ptail=V((seq, 128), BF), cot=V((slots, seq, width), BF),
        kf=V((k_rows, width), F32), kmain=V((main_w, width), BF), ktail=V((slots, 128, width), BF),
        stage=V((128, width), F32), table=V((-(-cells // 8) * 8, seq), F32), posb=V((seq, width), F32),
        normed=V((slots, seq, width), BF), unit=V((slots, seq, width), BF),
        inv=V((slots, seq, 128), F32), qkv=V((slots, seq, 3 * width), BF),
        expo=V((slots, width // HD, seq, seq), BF),
        att=V((slots, seq, width), BF), nm=V((slots, seq, width), BF),
        act=V((slots, seq, ff), BF), gup=V((slots, seq, ff), BF), outb=V((slots, seq, width), BF),
        gb=V((slots, seq, width), BF), datt=V((slots, seq, width), BF),
        tk=V((width // 128, 128, seq), BF), tv=V((width // 128, 128, seq), BF),
        gproj=V((slots, seq, 3 * width), BF), gpt=V((seq, 128), BF),
        sums=V((9, 8, width), F32), sums_up=V((8, ff), F32),
        gd=V((groups[0].rows, groups[0].lanes), BF), gu=V((groups[1].rows, groups[1].lanes), BF),
        gq=V((groups[2].rows, groups[2].lanes), BF), gk=V((groups[3].rows, groups[3].lanes), BF),
    )
    reduce_scratch = []
    for g in groups:
        size = g.rows
        for stage in g.stages:
            size //= stage[2]
            reduce_scratch.append(V((stage[2] - 1, size, g.lanes), BF))
        reduce_scratch += [V((stage[2] - 1, size, g.lanes), BF) for stage in g.extras]
        many = max([s[2] - 1 for s in g.extras] + [1])
        reduce_scratch += [DMA((len(g.stages), 4))] * 4 + [DMA((max(len(g.extras), 1), many))] * 2 + [DMA((1,))]
    scratch.update(
        load_sem=DMA((8 + 2 * slots,)), zin_s=DMA((2 * slots + 1, n_strip - 1)),
        zin_r=DMA((2 * slots + 1, n_strip - 1)), zout_s=DMA((2 * slots + 1, n_strip - 1)),
        zout_r=DMA((2 * slots + 1, n_strip - 1)), own_sem=DMA((2 * slots + 1,)),
    )
    conf.names = list(ins) + list(outs) + list(scratch)
    results = pl.pallas_call(
        functools.partial(layer_kernel, conf),
        out_shape=list(outs.values()),
        in_specs=[spec for _, spec in ins.values()],
        out_specs=[hbm] * len(outs),
        scratch_shapes=list(scratch.values()) + reduce_scratch,
        compiler_params=pltpu.CompilerParams(
            collective_id=0 if COMM else None, has_side_effects=True, vmem_limit_bytes=60 << 20),
        name="layer",
    )(*[value for value, _ in ins.values()])
    output, gp_main, gp_tail, gd, gu, gq, gk = results

    f_ins = dict(out_in=(output, hbm), gp_main=(gp_main, hbm), gp_tail=(gp_tail, hbm),
                 gd=(gd, hbm), gu=(gu, hbm), gq=(gq, hbm), gk=(gk, hbm), pinv=(pinv, hbm))
    shape = jax.ShapeDtypeStruct
    f_outs = dict(
        output=(shape(output.shape, BF), hbm), g_patches=(shape(patches.shape, BF), hbm),
        g_base=(shape(base_embed.shape, F32), hbm), g_bias_embed=(shape((width,), F32), hbm),
        g_grid=(shape(pos_grid.shape, F32), hbm), g_gain=(shape(norm_gain.shape, F32), hbm),
        g_shift=(shape(norm_shift.shape, F32), hbm), g_qkv=(shape(w_qkv.shape, F32), hbm),
        g_attn=(shape(bias_attn.shape, F32), hbm), g_out=(shape(w_out.shape, F32), hbm),
        g_up=(shape(w_up.shape, F32), hbm), g_bias_up=(shape((ff,), F32), hbm),
        g_down=(shape(w_down.shape, F32), hbm), g_bias_down=(shape((width,), F32), hbm),
    )
    f_scratch = dict(
        kf=V((k_rows, width), F32), base=V(base_embed.shape, F32), down=V(w_down.shape, F32),
        up=V(w_up.shape, F32), qkv=V(w_qkv.shape, F32), wo=V(w_out.shape, F32), gp=V(patches.shape, BF),
        tail_in=V((k_rows, width), BF), gd_in=V(gd.shape, BF), gu_in=V(gu.shape, BF), gq_in=V(gq.shape, BF),
        main_in=V(gp_main.shape, BF), last_in=V(gp_tail.shape, BF), out_buf=V(output.shape, BF), pinv_in=V(pinv.shape, F32), s_grid=V(pos_grid.shape, F32), s_bias_embed=V((width,), F32),
        s_gain=V(norm_gain.shape, F32), s_shift=V(norm_shift.shape, F32), s_attn=V(bias_attn.shape, F32),
        s_bias_down=V((width,), F32), s_bias_up=V((ff,), F32), sem=DMA((24,)),
    )
    f_conf = SimpleNamespace(**dict(vars(conf), names=list(f_ins) + list(f_outs) + list(f_scratch)))
    final = pl.pallas_call(
        functools.partial(finish_kernel, f_conf),
        out_shape=[s for s, _ in f_outs.values()],
        in_specs=[spec for _, spec in f_ins.values()],
        out_specs=[spec for _, spec in f_outs.values()],
        scratch_shapes=list(f_scratch.values()),
        compiler_params=pltpu.CompilerParams(vmem_limit_bytes=56 << 20),
        name="finish",
    )(*[value for value, _ in f_ins.values()])
    (output, g_patches, g_base, g_bias_embed, g_grid, g_gain, g_shift, g_qkv, g_attn, g_out, g_up,
     g_bias_up, g_down, g_bias_down) = final
    return (output, g_patches, g_base, g_bias_embed, g_grid, g_gain, g_shift, g_qkv, g_attn, g_out, g_up,
            g_bias_up, g_down, g_bias_down)


def solution(mesh):
    cfg = SimpleNamespace(n_img=mesh.shape[IMG], n_strip=mesh.shape[STRIP])
    split = P(IMG, STRIP, None)
    return jax.shard_map(
        functools.partial(per_device, cfg), mesh=mesh,
        in_specs=(split,) + (P(),) * 15 + (split,),
        out_specs=(split, split) + (P(),) * 12, check_vma=False,
    )
```

```python
import functools
import math
from types import SimpleNamespace

import jax
import jax.numpy as jnp
from jax import lax
from jax.experimental import pallas as pl
from jax.experimental.pallas import tpu as pltpu
from jax.sharding import PartitionSpec as P

HD = 64
EPSILON = 1e-06
MESH = pl.DeviceIdType.MESH
HIGHEST = lax.Precision.HIGHEST
BF = jnp.bfloat16
F32 = jnp.float32
COMM = True
MAIN, TAIL, COT = 0, 1, 2
IMG, STRIP = "img", "strip"
REP = {}


def begin(copy):
    copy.start()


def landed(copy):
    copy.wait_recv()


def sent(copy):
    copy.wait_send()


def nn(a, b, precision=None):
    return lax.dot_general(
        a, b, (((1,), (0,)), ((), ())), precision=precision, preferred_element_type=F32
    )


def nt(a, b):
    return lax.dot_general(a, b, (((1,), (1,)), ((), ())), preferred_element_type=F32)


def tn(a, b, precision=None):
    return lax.dot_general(
        a, b, (((0,), (0,)), ((), ())), precision=precision, preferred_element_type=F32
    )


def fold8(x):
    return jnp.sum(x.reshape(x.shape[0] // 8, 8, x.shape[1]), axis=0)


def rows_of(start, size):
    return pl.ds(pl.multiple_of(start, 16), size)


def chunk_of(rows):
    best = 16
    for size in range(16, 257, 16):
        if rows % size == 0:
            best = size
    return best


class Reduce:
    def __init__(self, group, grad, out, recv, extra_recv, sems):
        rows, stages = group.rows, group.stages
        self.stages, self.extras, self.done, self.rows = stages, group.extras, 0, rows
        self.grad, self.out, self.recv, self.extra_recv = grad, out, recv, extra_recv
        self.rs_s, self.rs_r, self.ag_s, self.ag_r, self.ex_s, self.ex_r, self.loc = sems
        count = len(stages)
        self.phases = [(self.rs_start, self.rs_finish, k) for k in range(count)]
        self.phases += [(self.ex_start, self.ex_finish, k) for k in range(len(self.extras))]
        for k in range(count - 1, -1, -1):
            if group.relay and stages[k] == (IMG, 2, 4):
                self.phases.append((self.near_start, self.near_finish, k))
                self.phases.append((self.far_start, self.far_finish, k))
            else:
                self.phases.append((self.ag_start, self.ag_finish, k))
        sizes, offsets = [rows], [0]
        for axis, unit, size in stages:
            mine = self.index(axis, unit, size)
            sizes.append(sizes[-1] // size)
            offsets.append(offsets[-1] + mine * sizes[-1])
        self.sizes, self.offsets = sizes, offsets

    @staticmethod
    def index(axis, unit, size):
        return (lax.axis_index(axis) // unit) % size

    def peer(self, stage, d):
        axis, unit, size = stage
        mine = self.index(axis, unit, size)
        there = (mine + d) % size
        return {axis: lax.axis_index(axis) + unit * (there - mine)}, there

    def rs_copies(self, k):
        size, sub = self.stages[k][2], self.sizes[k + 1]
        copies = []
        for d in range(1, size):
            device, there = self.peer(self.stages[k], d)
            copies.append(
                pltpu.make_async_remote_copy(
                    src_ref=self.grad.at[rows_of(self.offsets[k] + there * sub, sub), :],
                    dst_ref=self.recv[k].at[d - 1],
                    send_sem=self.rs_s.at[k, d - 1],
                    recv_sem=self.rs_r.at[k, d - 1],
                    device_id=device,
                    device_id_type=MESH,
                )
            )
        return copies

    def rs_start(self, k):
        for copy in self.rs_copies(k):
            copy.start()

    def rs_finish(self, k):
        copies = self.rs_copies(k)
        for copy in copies:
            copy.wait_recv()
        size, sub, first = self.stages[k][2], self.sizes[k + 1], self.offsets[k + 1]
        step = chunk_of(sub)

        def body(b, carry):
            rows = rows_of(first + b * step, step)
            total = self.grad[rows, :].astype(F32)
            for d in range(size - 1):
                total = total + self.recv[k][d, rows_of(b * step, step), :].astype(F32)
            self.grad[rows, :] = total.astype(BF)
            return carry

        lax.fori_loop(0, sub // step, body, 0)
        for copy in copies:
            copy.wait_send()

    def piece(self):
        return self.grad.at[rows_of(self.offsets[-1], self.sizes[-1]), :]

    def ex_copies(self, k):
        copies = []
        for d in range(1, self.extras[k][2]):
            device, _ = self.peer(self.extras[k], d)
            copies.append(
                pltpu.make_async_remote_copy(
                    src_ref=self.piece(),
                    dst_ref=self.extra_recv[k].at[d - 1],
                    send_sem=self.ex_s.at[k, d - 1],
                    recv_sem=self.ex_r.at[k, d - 1],
                    device_id=device,
                    device_id_type=MESH,
                )
            )
        return copies

    def ex_start(self, k):
        for copy in self.ex_copies(k):
            copy.start()

    def ex_finish(self, k):
        for copy in self.ex_copies(k):
            copy.wait()
        rows = rows_of(self.offsets[-1], self.sizes[-1])
        total = self.grad[rows, :].astype(F32)
        for d in range(self.extras[k][2] - 1):
            total = total + self.extra_recv[k][d].astype(F32)
        self.grad[rows, :] = total.astype(BF)

    def ag_copies(self, k):
        size, sub = self.stages[k][2], self.sizes[k + 1]
        region = self.out.at[rows_of(self.offsets[k + 1], sub), :]
        source = self.piece() if k == len(self.stages) - 1 else region
        copies = []
        for d in range(1, size):
            device, _ = self.peer(self.stages[k], d)
            copies.append(
                pltpu.make_async_remote_copy(
                    src_ref=source,
                    dst_ref=region,
                    send_sem=self.ag_s.at[k, d - 1],
                    recv_sem=self.ag_r.at[k, d - 1],
                    device_id=device,
                    device_id_type=MESH,
                )
            )
        return copies

    def plane(self, k):
        mine = self.index(*self.stages[k])
        return mine, mine + 1 - 2 * (mine % 2), mine + 2 - 4 * (mine // 2)

    def plane_copy(self, k, slot, piece, part, there):
        mine, _, _ = self.plane(k)
        rows = self.sizes[k + 1] // (1 if part is None else 2)
        start = self.offsets[k] + piece * self.sizes[k + 1] + (part or 0) * rows
        region = self.out.at[rows_of(start, rows), :]
        return pltpu.make_async_remote_copy(
            src_ref=region, dst_ref=region, send_sem=self.ag_s.at[k, slot], recv_sem=self.ag_r.at[k, slot],
            device_id={IMG: lax.axis_index(IMG) + 2 * (there - mine)}, device_id_type=MESH)

    def near_copies(self, k):
        mine, along_x, along_y = self.plane(k)
        return [self.plane_copy(k, 0, mine, None, along_x), self.plane_copy(k, 1, mine, None, along_y)]

    def far_copies(self, k):
        _, along_x, along_y = self.plane(k)
        return [self.plane_copy(k, 2, along_x, 0, along_y), self.plane_copy(k, 3, along_y, 1, along_x)]

    def near_start(self, k):
        for copy in self.near_copies(k):
            copy.start()

    def near_finish(self, k):
        for copy in self.near_copies(k):
            copy.wait()

    def far_start(self, k):
        for copy in self.far_copies(k):
            copy.start()

    def far_finish(self, k):
        for copy in self.far_copies(k):
            copy.wait()

    def local_copy(self):
        region = self.out.at[rows_of(self.offsets[-1], self.sizes[-1]), :]
        return pltpu.make_async_copy(self.piece(), region, self.loc.at[0])

    def left(self):
        return self.done <= len(self.phases)

    def step(self):
        n = self.done
        self.done += 1
        if n > 0:
            self.phases[n - 1][1](self.phases[n - 1][2])
        if n < len(self.phases):
            self.phases[n][0](self.phases[n][2])

    def ag_start(self, k):
        if k == len(self.stages) - 1:
            self.local_copy().start()
        for copy in self.ag_copies(k):
            copy.start()

    def ag_finish(self, k):
        if k == len(self.stages) - 1:
            self.local_copy().wait()
        for copy in self.ag_copies(k):
            copy.wait()


def layer_kernel(cfg, *refs):
    r = SimpleNamespace(**dict(zip(cfg.names, refs)))
    n_strip, strip_rows, slots = cfg.n_strip, cfg.strip_rows, cfg.slots
    seq, width, ff, pixels, area = cfg.seq, cfg.width, cfg.ff, cfg.pixels, cfg.area
    main_w = cfg.main_w
    tail = pixels - main_w
    grid_side, base_count = cfg.grid_side, cfg.base_count
    pairs = width // 128
    depth = r.base_embed.shape[1]
    ff_chunks = ff // width
    me = lax.axis_index(STRIP)
    group = 2 if n_strip % 2 == 0 else 1
    block = group * strip_rows
    blocks = n_strip // group

    def repeat(fn, *args):
        count = REP.get(fn.__name__, 1)
        if count == 1:
            fn(*args)
        else:
            lax.fori_loop(0, count, lambda t, c: (fn(*args), c)[1], 0)

    groups = []
    at = len(refs) - sum(len(g.stages) + len(g.extras) + 7 for g in cfg.groups)
    for g, grad, out in zip(cfg.groups, (r.gd, r.gu, r.gq, r.gk), (r.gd_out, r.gu_out, r.gq_out, r.gk_out)):
        n, e = len(g.stages), len(g.extras)
        groups.append(Reduce(g, grad, out, refs[at:at + n], refs[at + n:at + n + e],
                             refs[at + n + e:at + n + e + 7]))
        at += n + e + 7
    sum_d, sum_u, sum_q, sum_k = groups
    if COMM:
        barrier = pltpu.get_barrier_semaphore()
        greeted = 0
        for stage in cfg.stages + cfg.left:
            for d in range(1, stage[2]):
                device, _ = sum_k.peer(stage, d)
                pl.semaphore_signal(barrier, inc=1, device_id=device, device_id_type=MESH)
                greeted += 1

    loads = [
        pltpu.make_async_copy(r.w_qkv, r.wqkv, r.load_sem.at[0]),
        pltpu.make_async_copy(r.w_out, r.wout, r.load_sem.at[1]),
        pltpu.make_async_copy(r.w_up, r.wup, r.load_sem.at[2]),
        pltpu.make_async_copy(r.w_down, r.wdown, r.load_sem.at[3]),
    ]
    base_loads = [
        pltpu.make_async_copy(r.base_embed.at[c], r.wide.at[rows_of(c * depth, depth), :], r.load_sem.at[4 + c])
        for c in range(3)
    ]
    tails_load = pltpu.make_async_copy(
        r.patches.at[:, :, main_w:pixels], r.ptails, r.load_sem.at[7]
    )
    own_loads = []
    for slot in range(slots):
        rows = rows_of(me * strip_rows, strip_rows)
        own_loads.append(pltpu.make_async_copy(
            r.patches.at[me * slots + slot, :, 0:main_w], r.pmain.at[slot, rows, :],
            r.load_sem.at[8 + slot]))
        own_loads.append(pltpu.make_async_copy(
            r.cotangent.at[me * slots + slot], r.cot.at[slot, rows, :],
            r.load_sem.at[8 + slots + slot]))
    tails_load.start()
    for copy in base_loads:
        copy.start()
    for copy in own_loads:
        copy.start()
    for copy in loads:
        copy.start()

    def z_in(kind, slot, d):
        home = (me + d) % n_strip
        rows = rows_of(me * strip_rows, strip_rows)
        image = home * slots + slot
        if kind == MAIN:
            src, dst, k = r.patches.at[image, :, 0:main_w], r.pmain.at[slot, rows, :], slot
        elif kind == TAIL:
            src, dst, k = r.packed.at[home], r.ptail.at[rows, :], slots
        else:
            src, dst, k = r.cotangent.at[image], r.cot.at[slot, rows, :], slots + 1 + slot
        return pltpu.make_async_remote_copy(
            src_ref=src, dst_ref=dst, send_sem=r.zin_s.at[k, d - 1],
            recv_sem=r.zin_r.at[k, d - 1], device_id={STRIP: home}, device_id_type=MESH)

    def z_all(kind, slot, act):
        if not COMM:
            return
        for k in range(n_strip - 1):
            d = k + 1
            if act is begin and n_strip == 4:
                d = jnp.where(me == 2, (1, 3, 2)[k], d)
            act(z_in(kind, slot, d))

    if COMM:
        pl.semaphore_wait(barrier, greeted)
    z_all(MAIN, 0, begin)

    tails_load.wait()
    zero_tail = jnp.zeros((strip_rows, 128 // slots - tail), F32)
    for home in range(n_strip):
        parts = []
        for slot in range(slots):
            parts.append(r.ptails[home * slots + slot].astype(F32))
            parts.append(zero_tail)
        r.packed[home] = jnp.concatenate(parts, axis=1).astype(BF)
    z_all(TAIL, 0, begin)
    r.ptail[rows_of(me * strip_rows, strip_rows), :] = r.packed[me]

    def make_kernel():
        pinv = r.pinv[...].astype(BF)
        r.kf[...] = jnp.zeros_like(r.kf)
        for c in range(3):
            if not REP:
                base_loads[c].wait()
            r.kf[c * area:(c + 1) * area, :] = nn(pinv, r.wide[c * depth:(c + 1) * depth, :].astype(BF))
        kernel = r.kf[...].astype(BF)
        r.kmain[...] = kernel[0:main_w]
        for slot in range(slots):
            r.stage[...] = jnp.zeros_like(r.stage)
            at = slot * (128 // slots)
            r.stage[at:at + tail, :] = r.kf[main_w:pixels, :]
            r.ktail[slot] = r.stage[...].astype(BF)

    if REP:
        for copy in base_loads:
            copy.wait()
    repeat(make_kernel)

    def make_position():
        cells = r.table.shape[0]
        cell = lax.broadcasted_iota(jnp.int32, (cells, grid_side), 0).astype(F32)
        grid_row = jnp.floor((cell + 0.5) / base_count)
        corner = (grid_row, cell - grid_row * base_count)
        place = lax.broadcasted_iota(jnp.int32, (grid_side, seq), 1).astype(F32)
        which = lax.broadcasted_iota(jnp.int32, (grid_side, seq), 0).astype(F32)
        patch_row = jnp.floor((place + 0.5) / grid_side)
        patch = (patch_row, place - patch_row * grid_side)
        product = None
        for t in range(2):
            low = r.pos_index[t, 0:1, :].astype(F32)
            high = r.pos_index[t, 1:2, :].astype(F32)
            frac = r.pos_frac[t:t + 1, :]
            entry = (1.0 - frac) * (corner[t] == low).astype(F32) + frac * (corner[t] == high).astype(F32)
            spread = nn(entry, (patch[t] == which).astype(F32), HIGHEST)
            product = spread if product is None else product * spread
        valid = lax.broadcasted_iota(jnp.int32, (cells, seq), 0) < base_count * base_count
        r.table[...] = jnp.where(valid, product, 0.0)
        r.stage[...] = jnp.zeros_like(r.stage)
        for b in range(base_count):
            r.stage[b * base_count:(b + 1) * base_count, :] = r.pos_grid[b]
        r.posb[...] = tn(r.table[...], r.stage[0:cells, :], HIGHEST) + r.bias_embed[...]

    repeat(make_position)
    r.sums[...] = jnp.zeros_like(r.sums)
    r.sums_up[...] = jnp.zeros_like(r.sums_up)
    for one, used in zip(groups, ((ff + width), ff * pairs, 3 * width * pairs)):
        if one.rows > used:
            r_pad = one.grad.shape
            one.grad[used:, :] = jnp.zeros((r_pad[0] - used, r_pad[1]), BF)
    for copy in loads:
        copy.wait()
    for copy in own_loads:
        copy.wait()

    def wide_rows(k, rows):
        return rows_of(k * seq + rows.start, rows.size)

    lane = lax.broadcasted_iota(jnp.int32, (1, 128), 1)
    first_head = lane < HD

    def norm(x, gain, shift):
        center = x - jnp.mean(x, axis=-1, keepdims=True)
        inv = lax.rsqrt(jnp.mean(center * center, axis=-1, keepdims=True) + EPSILON)
        unit = center * inv
        return unit * gain + shift, unit, inv

    def norm_back(g, unit, inv, gain):
        gu = g * gain
        return inv * (
            gu - jnp.mean(gu, axis=-1, keepdims=True)
            - unit * jnp.mean(gu * unit, axis=-1, keepdims=True)
        )

    def add_sum(row, x):
        r.sums[row] += fold8(x)

    B_EMBED, GAIN, SHIFT, B_Q, B_V, B_O, B_DOWN = 0, 1, 3, 5, 6, 7, 8

    def near_first(t):
        return (t + me // group) % blocks

    def wait_rows(t, kind, slot):
        if not COMM:
            return
        for part in range(group):
            d = (me - t * group - part + n_strip) % n_strip

            @pl.when(d > 0)
            def _():
                z_in(kind, slot, d).wait_recv()

    def embed(i):
        def body(t, carry):
            b = near_first(t)
            rows = rows_of(b * block, block)
            wait_rows(b, MAIN, i)
            if i == 0:
                wait_rows(b, TAIL, 0)

            @pl.when(t == 0)
            def _():
                if i + 1 < slots:
                    z_all(MAIN, i + 1, begin)
                else:
                    z_all(COT, i, begin)

            emb = (
                nn(r.pmain[i, rows, :], r.kmain[...])
                + nn(r.ptail[rows, :], r.ktail[i])
                + r.posb[rows, :]
            )
            r.wide[wide_rows(i, rows), :] = emb
            y, unit, inv = norm(emb, r.norm_gain[0:1, :], r.norm_shift[0:1, :])
            y = y.astype(BF)
            r.normed[i, rows, :] = y
            r.unit[i, rows, :] = unit.astype(BF)
            r.inv[i, rows, :] = jnp.broadcast_to(inv, (block, 128))
            q = nn(y, r.wqkv[:, 0:width]) + r.bias_attn[0:1, :]
            r.qkv[i, rows, 0:width] = (q * (1.0 / math.sqrt(HD))).astype(BF)
            r.qkv[i, rows, width:2 * width] = nn(y, r.wqkv[:, width:2 * width]).astype(BF)
            v = nn(y, r.wqkv[:, 2 * width:3 * width]) + r.bias_attn[1:2, :]
            r.qkv[i, rows, 2 * width:3 * width] = v.astype(BF)
            return carry

        lax.fori_loop(0, blocks, body, 0)

    def lanes(p, part=0):
        return slice(part * width + p * 128, part * width + (p + 1) * 128)

    def ahead(tasks, front, rest, depth):
        ready = [front(*task) for task in tasks[:depth]]
        for n, task in enumerate(tasks):
            if n + depth < len(tasks):
                ready.append(front(*tasks[n + depth]))
            rest(*task, ready[n])
            ready[n] = None

    heads = [(p, h) for p in range(pairs) for h in range(2)]

    def pick(x, h):
        return jnp.where(first_head == (h == 0), x, jnp.zeros_like(x))

    def attend(i):
        outs, recips = {}, {}

        def front(p, h):
            return nt(pick(r.qkv[i, :, lanes(p)], h), r.qkv[i, :, lanes(p, 1)])

        def rest(p, h, s):
            e = jnp.exp(s - jnp.max(s, axis=-1, keepdims=True))
            recip = 1.0 / jnp.sum(e, axis=-1, keepdims=True)
            e = e.astype(BF)
            r.expo[i, 2 * p + h] = e
            outs[h] = nn(e, r.qkv[i, :, lanes(p, 2)]) * recip
            recips[h] = jnp.broadcast_to(recip, (seq, 128))
            if h == 1:
                r.att[i, :, lanes(p)] = jnp.where(first_head, outs[0], outs[1]).astype(BF)
                r.wide[(2 * slots + i) * seq:(2 * slots + i + 1) * seq, lanes(p)] = jnp.where(first_head, recips[0], recips[1])

        ahead(heads, front, rest, 2)

    c0 = math.sqrt(2.0 / math.pi)
    c1 = 0.044715

    def out_copy(i, d):
        strip = (me + d) % n_strip
        return pltpu.make_async_remote_copy(
            src_ref=r.outb.at[i, rows_of(strip * strip_rows, strip_rows), :],
            dst_ref=r.output.at[me * slots + i],
            send_sem=r.zout_s.at[i, d - 1], recv_sem=r.zout_r.at[i, d - 1],
            device_id={STRIP: strip}, device_id_type=MESH)

    def own_out(i):
        return pltpu.make_async_copy(
            r.outb.at[i, rows_of(me * strip_rows, strip_rows), :],
            r.output.at[me * slots + i], r.own_sem.at[i])

    def send_out(i):
        if not COMM:
            return
        for d in range(1, n_strip):
            out_copy(i, d).start()
        own_out(i).start()

    def mlp(i):
        def body(n, carry):
            t = near_first(n)
            rows = rows_of(t * block, block)
            wait_rows(t, COT, i)
            if i > 0:

                @pl.when(n == blocks - 1)
                def _():
                    send_out(i - 1)

            mid = r.wide[wide_rows(i, rows), :] + nn(r.att[i, rows, :], r.wout[...]) + r.bias_attn[2:3, :]
            gain = r.norm_gain[1:2, :]
            y, unit, inv = norm(mid, gain, r.norm_shift[1:2, :])
            y = y.astype(BF)
            r.nm[i, rows, :] = y
            cot = r.cot[i, rows, :]

            def front(cols):
                return nn(y, r.wup[:, cols]), nt(cot, r.wdown[cols, :])

            def rest(cols, ready):
                u = ready[0] + r.bias_up[cols]
                square = u * u
                half = 0.5 + 0.5 * jnp.tanh(u * (c0 + (c0 * c1) * square))
                act = u * half
                r.act[i, rows, cols] = act.astype(BF)
                slope = half + (act - act * half) * (2.0 * c0 + (6.0 * c0 * c1) * square)
                gu = ready[1] * slope
                r.gup[i, rows, cols] = gu.astype(BF)
                r.sums_up[:, cols] += fold8(gu)

            ahead([(slice(c, c + 256),) for c in range(0, ff, 256)], front, rest, 1)
            out = mid + r.bias_down[...] + nn(r.act[i, rows, :], r.wdown[...])
            g_nm = nt(r.gup[i, rows, :], r.wup[...])
            r.outb[i, rows, :] = out.astype(BF)
            add_sum(GAIN + 1, g_nm * unit)
            add_sum(SHIFT + 1, g_nm)
            cotf = cot.astype(F32)
            add_sum(B_DOWN, cotf)
            g_mid = cotf + norm_back(g_nm, unit, inv, gain)
            r.wide[wide_rows(slots + i, rows), :] = g_mid
            add_sum(B_O, g_mid)
            gb = g_mid.astype(BF)
            r.gb[i, rows, :] = gb
            r.datt[i, rows, :] = (nt(gb, r.wout[...]) * r.wide[wide_rows(2 * slots + i, rows), :]).astype(BF)
            return carry

        lax.fori_loop(0, blocks, body, 0)

    def ds_slot(p, h):
        wide = -(-seq // 128) * 128
        return (r.act, r.gup)[p % 2].at[slots - 1, :, h * wide:h * wide + seq]

    def attend_back(i):
        gq = {}

        def front(p, h):
            return nt(pick(r.datt[i, :, lanes(p)], h), r.qkv[i, :, lanes(p, 2)])

        def rest(p, h, dp):
            prod = r.datt[i, :, lanes(p)].astype(F32) * r.att[i, :, lanes(p)].astype(F32)
            delta = jnp.sum(pick(prod, h), axis=-1, keepdims=True)
            expo = r.expo[i, 2 * p + h]
            ds = (expo.astype(F32) * (dp - delta)).astype(BF)
            ds_slot(p, h)[...] = ds
            gq[h] = nn(ds, r.qkv[i, :, lanes(p, 1)])
            if h == 0:
                return
            g_q = jnp.where(first_head, gq[0], gq[1]) * (1.0 / math.sqrt(HD))
            r.gproj[i, :, lanes(p)] = g_q.astype(BF)
            q_t, d_t = r.qkv[i, :, lanes(p)].T, r.datt[i, :, lanes(p)].T
            for part in range(2):
                half = slice(part * HD, (part + 1) * HD)
                r.tk[p, half, :] = nn(q_t[half, :], ds_slot(p, part)[...]).astype(BF)
                r.tv[p, half, :] = nn(d_t[half, :], r.expo[i, 2 * p + part]).astype(BF)
            r.gproj[i, :, lanes(p, 1)] = r.tk[p].T
            r.gproj[i, :, lanes(p, 2)] = r.tv[p].T

        ahead(heads, front, rest, 1)

    def gp_copy(i, d):
        strip = (me + d) % n_strip
        return pltpu.make_async_remote_copy(
            src_ref=r.gup.at[i, rows_of(strip * strip_rows, strip_rows), ff - main_w:ff],
            dst_ref=r.gp_main.at[me * slots + i],
            send_sem=r.zout_s.at[slots + i, d - 1], recv_sem=r.zout_r.at[slots + i, d - 1],
            device_id={STRIP: strip}, device_id_type=MESH)

    def own_gp(i):
        return pltpu.make_async_copy(
            r.gup.at[i, rows_of(me * strip_rows, strip_rows), ff - main_w:ff],
            r.gp_main.at[me * slots + i], r.own_sem.at[slots + i])

    def gpt_copy(i, d):
        strip = (me + d) % n_strip
        return pltpu.make_async_remote_copy(
            src_ref=r.gpt.at[rows_of(strip * strip_rows, strip_rows), :],
            dst_ref=r.gp_tail.at[me],
            send_sem=r.zout_s.at[2 * slots, d - 1], recv_sem=r.zout_r.at[2 * slots, d - 1],
            device_id={STRIP: strip}, device_id_type=MESH)

    def own_gpt(i):
        return pltpu.make_async_copy(
            r.gpt.at[rows_of(me * strip_rows, strip_rows), :],
            r.gp_tail.at[me], r.own_sem.at[2 * slots])

    def embed_back(i):
        def body(t, carry):
            rows = rows_of(t * block, block)
            gain = r.norm_gain[0:1, :]
            unit = r.unit[i, rows, :].astype(F32)
            gproj = r.gproj[i, rows, :]
            add_sum(B_Q, gproj[:, 0:width].astype(F32))
            add_sum(B_V, gproj[:, 2 * width:3 * width].astype(F32))
            g_n = nt(gproj, r.wqkv[...])
            add_sum(GAIN, g_n * unit)
            add_sum(SHIFT, g_n)
            inv = r.inv[i, rows, :][:, 0:1]
            g_emb = r.wide[wide_rows(slots + i, rows), :] + norm_back(g_n, unit, inv, gain)
            add_sum(B_EMBED, g_emb)
            ge = g_emb.astype(BF)
            r.act[i, rows, ff - width:ff] = ge
            r.gup[i, rows, ff - main_w:ff] = nt(ge, r.kmain[...]).astype(BF)
            part = nt(ge, r.ktail[i])
            if i > 0:
                part = part + r.gpt[rows, :].astype(F32)
            r.gpt[rows, :] = part.astype(BF)
            return carry

        lax.fori_loop(0, blocks, body, 0)

    early = 2 if n_strip > 2 else 1

    def send_early():
        if COMM:
            gp_copy(0, early).start()

    def send_gp(i):
        if not COMM:
            return
        for d in range(1, n_strip):
            if i > 0 or d != early:
                gp_copy(i, d).start()
        own_gp(i).start()

    def send_tail():
        if not COMM:
            return
        for d in range(1, n_strip):
            gpt_copy(0, d).start()
        own_gpt(0).start()

    def both(ref, cols=slice(None)):
        return ref[:, :, cols].reshape(slots * seq, -1)

    def grads_d():
        lhs = both(r.cot).T
        for c in range(0, ff, 512):
            r.gd[c:c + 512, :] = nn(lhs, both(r.act, slice(c, c + 512))).T.astype(BF)
        r.gd[ff:ff + width, :] = tn(both(r.att), both(r.gb)).astype(BF)

    def grads_u():
        lhs = both(r.nm).T
        for c in range(0, ff, 512):
            part = nn(lhs, both(r.gup, slice(c, c + 512))).astype(BF)
            for n in range(4):
                r.gu[(c // 128 + n) * width:(c // 128 + n + 1) * width, :] = part[:, n * 128:(n + 1) * 128]

    def grads_q():
        lhs = both(r.normed).T
        for c in range(3):
            part = nn(lhs, both(r.gproj, slice(c * width, (c + 1) * width))).astype(BF)
            for n in range(pairs):
                at = (c * pairs + n) * width
                r.gq[at:at + width, :] = part[:, n * 128:(n + 1) * 128]

    def grads_k():
        r.kf[0:main_w, :] = tn(both(r.pmain), both(r.act, slice(ff - width, ff)))
        at = main_w
        total = None
        for slot in range(slots):
            part = tn(r.ptail[...], r.act[slot, :, ff - width:ff])
            start = slot * (128 // slots)
            part = part[start:start + tail, :]
            total = part if total is None else total + part
        r.kf[main_w:pixels, :] = total
        summed = sum(r.act[slot, :, ff - width:ff].astype(F32) for slot in range(slots))
        g_grid = nn(r.table[...], summed, HIGHEST)
        cells = base_count * base_count
        r.kf[pixels:pixels + cells, :] = g_grid[0:cells, :]
        small = jnp.sum(r.sums[...], axis=1)
        at = cfg.small_at + small.shape[0]
        r.kf[cfg.small_at:at, :] = small
        small_up = jnp.sum(r.sums_up[...], axis=0, keepdims=True)
        for c in range(ff_chunks):
            r.kf[at + c:at + c + 1, :] = small_up[:, c * width:(c + 1) * width]
        r.gk[0:r.kf.shape[0], :] = r.kf[...].astype(BF)
        if cfg.groups[3].rows > r.kf.shape[0]:
            more = cfg.groups[3].rows - r.kf.shape[0]
            r.gk[r.kf.shape[0]:, :] = jnp.zeros((more, width), BF)

    def step(*sums):
        if COMM:
            for one in sums:
                if one.left():
                    one.step()

    for i in range(slots):
        repeat(embed, i)
        if i + 1 < slots:
            z_all(COT, i, begin)
        repeat(attend, i)
    for i in range(slots):
        repeat(mlp, i)
    repeat(grads_d)
    step(sum_d)
    send_out(slots - 1)
    repeat(grads_u)
    step(sum_u, sum_d)
    repeat(attend_back, 0)
    step(sum_u)
    for i in range(1, slots):
        repeat(attend_back, i)
    repeat(grads_q)
    step(sum_q, sum_d)
    repeat(embed_back, 0)
    step(sum_q)
    send_early()
    for i in range(1, slots):
        repeat(embed_back, i)
    repeat(grads_k)
    step(sum_k, sum_u, sum_k, sum_d, sum_q, sum_k, sum_u, sum_d, sum_k, sum_q)
    for i in range(slots):
        send_gp(i)
    send_tail()
    if COMM:
        for slot in range(slots):
            z_all(MAIN, slot, sent)
            z_all(COT, slot, sent)
            for d in range(1, n_strip):
                out_copy(slot, d).wait()
            own_out(slot).wait()
        z_all(TAIL, 0, sent)
    step(sum_u, sum_d, sum_k, sum_q, sum_u, sum_d, sum_k, sum_q, sum_u, sum_d)
    while COMM and any(one.left() for one in groups):
        step(sum_d, sum_q, sum_k, sum_u)
    if COMM:
        for slot in range(slots):
            for d in range(1, n_strip):
                gp_copy(slot, d).wait()
            own_gp(slot).wait()
        for d in range(1, n_strip):
            gpt_copy(0, d).wait()
        own_gpt(0).wait()


def finish_kernel(cfg, *refs):
    r = SimpleNamespace(**dict(zip(cfg.names, refs)))
    width, ff, slots = cfg.width, cfg.ff, cfg.slots
    pixels, area, main_w = cfg.pixels, cfg.area, cfg.main_w
    tail = pixels - main_w
    ff_chunks = ff // width
    copies = []

    def load(k, src, dst):
        copy = pltpu.make_async_copy(src, dst, r.sem.at[k])
        copy.start()
        return copy

    def send(src, dst, k):
        copy = pltpu.make_async_copy(src, dst, r.sem.at[k])
        copy.start()
        copies.append(copy)

    loads = [
        load(9, r.gk.at[0:r.kf.shape[0], :], r.tail_in),
        load(10, r.gd, r.gd_in),
        load(11, r.gu, r.gu_in),
        load(12, r.gp_main, r.main_in),
        load(13, r.gp_tail, r.last_in),
        load(14, r.out_in, r.out_buf),
        load(15, r.gq, r.gq_in),
        load(16, r.pinv, r.pinv_in),
    ]
    loads[0].wait()
    r.kf[...] = r.tail_in[...].astype(F32)
    small = r.kf[cfg.small_at:cfg.small_at + 16, :]
    for b in range(cfg.base_count):
        at = pixels + b * cfg.base_count
        r.s_grid[b] = r.kf[at:at + cfg.base_count, :]
    r.s_bias_embed[...] = small[0]
    r.s_gain[...] = small[1:3]
    r.s_shift[...] = small[3:5]
    r.s_attn[...] = small[5:8]
    r.s_bias_down[...] = small[8]
    for c in range(ff_chunks):
        r.s_bias_up[c * width:(c + 1) * width] = small[9 + c]
    few = ((r.s_grid, r.g_grid), (r.s_bias_embed, r.g_bias_embed), (r.s_gain, r.g_gain), (r.s_shift, r.g_shift),
           (r.s_attn, r.g_attn), (r.s_bias_down, r.g_bias_down), (r.s_bias_up, r.g_bias_up))
    for n, (held, place) in enumerate(few):
        send(held, place, 17 + n)
    loads[7].wait()
    pinv = r.pinv_in[...].astype(BF)
    for c in range(3):
        part = r.kf[c * area:(c + 1) * area, :].astype(BF)
        r.base[c] = tn(pinv, part)
        send(r.base.at[c], r.g_base.at[c], 1 + c)
    loads[1].wait()
    r.down[...] = r.gd_in[0:ff, :].astype(F32)
    r.wo[...] = r.gd_in[ff:ff + width, :].astype(F32)
    send(r.wo, r.g_out, 7)
    send(r.down, r.g_down, 4)
    loads[2].wait()
    for n in range(ff // 128):
        r.up[:, n * 128:(n + 1) * 128] = r.gu_in[n * width:(n + 1) * width, :].astype(F32)
    send(r.up, r.g_up, 5)
    loads[6].wait()
    pairs = width // 128
    for n in range(3 * pairs):
        r.qkv[:, n * 128:(n + 1) * 128] = r.gq_in[n * width:(n + 1) * width, :].astype(F32)
    send(r.qkv, r.g_qkv, 6)
    loads[5].wait()
    send(r.out_buf, r.output, 0)
    loads[3].wait()
    loads[4].wait()
    for image in range(r.gp.shape[0]):
        r.gp[image, :, 0:main_w] = r.main_in[image]
        start = (image % slots) * (128 // slots)
        last = r.last_in[image // slots].astype(F32)[:, start:start + tail]
        r.gp[image, :, main_w:pixels] = last.astype(BF)
    send(r.gp, r.g_patches, 8)
    for copy in copies:
        copy.wait()


def per_device(cfg, patches, pinv, base_embed, bias_embed, pos_grid, pos_index, pos_frac, norm_gain,
               norm_shift, w_qkv, bias_attn, w_out, w_up, bias_up, w_down, bias_down, cotangent):
    images, strip_rows, pixels = patches.shape
    width, ff = w_up.shape
    n_img, n_strip = cfg.n_img, cfg.n_strip
    slots = images // n_strip
    seq = strip_rows * n_strip
    base_count = pos_grid.shape[0]
    area = pinv.shape[0]
    main_w = pixels // 128 * 128
    core = [(IMG, 1, min(2, n_img))]
    plane = [(IMG, 2, min(4, n_img // 2))] if n_img > 2 else []
    stages = core + plane + [(STRIP, 1, n_strip)]
    halves = [(STRIP, 1, 2), (STRIP, 2, n_strip // 2)] if n_strip % 2 == 0 else [(STRIP, 1, n_strip)]
    left = [(IMG, 8, n_img // 8)] if n_img > 8 else []
    cells = base_count * base_count
    small_at = -(-(pixels + cells) // 8) * 8
    k_rows = -(-(small_at + 9 + ff // width) // 128) * 128

    def sum_of(values, lanes, order, extras, relay=False):
        unit = 16 * math.prod(s[2] for s in order)
        return SimpleNamespace(rows=-(-(values // lanes) // unit) * unit, lanes=lanes, stages=order,
                               extras=extras + left, relay=relay)

    groups = [sum_of((ff + width) * width, width, stages, [], True), sum_of(ff * width, 128, stages, [], True),
              sum_of(3 * width * width, 128, stages, []),
              sum_of(k_rows * width, width, core + plane, halves)]
    conf = SimpleNamespace(n_strip=n_strip, strip_rows=strip_rows, slots=slots, seq=seq, width=width, ff=ff,
                           pixels=pixels, area=area, main_w=main_w, grid_side=pos_frac.shape[1],
                           base_count=base_count, stages=stages, left=left, groups=groups,
                           small_at=small_at)
    vmem = pl.BlockSpec(memory_space=pltpu.VMEM)
    hbm = pl.BlockSpec(memory_space=pl.ANY)
    ins = dict(
        patches=(patches, hbm), cotangent=(cotangent, hbm), base_embed=(base_embed, hbm),
        w_qkv=(w_qkv, hbm), w_out=(w_out, hbm), w_up=(w_up, hbm), w_down=(w_down, hbm),
        pinv=(pinv, vmem), bias_embed=(bias_embed, vmem), pos_grid=(pos_grid, vmem),
        pos_index=(pos_index, vmem), pos_frac=(pos_frac, vmem), norm_gain=(norm_gain, vmem),
        norm_shift=(norm_shift, vmem), bias_attn=(bias_attn, vmem),
        bias_up=(bias_up, vmem), bias_down=(bias_down, vmem),
    )
    outs = dict(
        output=jax.ShapeDtypeStruct((images, strip_rows, width), BF),
        gp_main=jax.ShapeDtypeStruct((images, strip_rows, main_w), BF),
        gp_tail=jax.ShapeDtypeStruct((n_strip, strip_rows, 128), BF),
        **dict(zip(("gd_out", "gu_out", "gq_out", "gk_out"),
                   (jax.ShapeDtypeStruct((g.rows, g.lanes), BF) for g in groups))),
    )
    V = pltpu.VMEM
    DMA = pltpu.SemaphoreType.DMA
    scratch = dict(
        wqkv=V(w_qkv.shape, BF), wout=V(w_out.shape, BF), wup=V(w_up.shape, BF), wdown=V(w_down.shape, BF),
        wide=V((max(3 * base_embed.shape[1], 3 * slots * seq), width), F32),
        ptails=V((images, strip_rows, pixels - main_w), BF), packed=V((n_strip, strip_rows, 128), BF),
        pmain=V((slots, seq, main_w), BF), ptail=V((seq, 128), BF), cot=V((slots, seq, width), BF),
        kf=V((k_rows, width), F32), kmain=V((main_w, width), BF), ktail=V((slots, 128, width), BF),
        stage=V((128, width), F32), table=V((-(-cells // 8) * 8, seq), F32), posb=V((seq, width), F32),
        normed=V((slots, seq, width), BF), unit=V((slots, seq, width), BF),
        inv=V((slots, seq, 128), F32), qkv=V((slots, seq, 3 * width), BF),
        expo=V((slots, width // HD, seq, seq), BF),
        att=V((slots, seq, width), BF), nm=V((slots, seq, width), BF),
        act=V((slots, seq, ff), BF), gup=V((slots, seq, ff), BF), outb=V((slots, seq, width), BF),
        gb=V((slots, seq, width), BF), datt=V((slots, seq, width), BF),
        tk=V((width // 128, 128, seq), BF), tv=V((width // 128, 128, seq), BF),
        gproj=V((slots, seq, 3 * width), BF), gpt=V((seq, 128), BF),
        sums=V((9, 8, width), F32), sums_up=V((8, ff), F32),
        gd=V((groups[0].rows, groups[0].lanes), BF), gu=V((groups[1].rows, groups[1].lanes), BF),
        gq=V((groups[2].rows, groups[2].lanes), BF), gk=V((groups[3].rows, groups[3].lanes), BF),
    )
    reduce_scratch = []
    for g in groups:
        size = g.rows
        for stage in g.stages:
            size //= stage[2]
            reduce_scratch.append(V((stage[2] - 1, size, g.lanes), BF))
        reduce_scratch += [V((stage[2] - 1, size, g.lanes), BF) for stage in g.extras]
        many = max([s[2] - 1 for s in g.extras] + [1])
        reduce_scratch += [DMA((len(g.stages), 4))] * 4 + [DMA((max(len(g.extras), 1), many))] * 2 + [DMA((1,))]
    scratch.update(
        load_sem=DMA((8 + 2 * slots,)), zin_s=DMA((2 * slots + 1, n_strip - 1)),
        zin_r=DMA((2 * slots + 1, n_strip - 1)), zout_s=DMA((2 * slots + 1, n_strip - 1)),
        zout_r=DMA((2 * slots + 1, n_strip - 1)), own_sem=DMA((2 * slots + 1,)),
    )
    conf.names = list(ins) + list(outs) + list(scratch)
    results = pl.pallas_call(
        functools.partial(layer_kernel, conf),
        out_shape=list(outs.values()),
        in_specs=[spec for _, spec in ins.values()],
        out_specs=[hbm] * len(outs),
        scratch_shapes=list(scratch.values()) + reduce_scratch,
        compiler_params=pltpu.CompilerParams(
            collective_id=0 if COMM else None, has_side_effects=True, vmem_limit_bytes=60 << 20),
        name="layer",
    )(*[value for value, _ in ins.values()])
    output, gp_main, gp_tail, gd, gu, gq, gk = results

    f_ins = dict(out_in=(output, hbm), gp_main=(gp_main, hbm), gp_tail=(gp_tail, hbm),
                 gd=(gd, hbm), gu=(gu, hbm), gq=(gq, hbm), gk=(gk, hbm), pinv=(pinv, hbm))
    shape = jax.ShapeDtypeStruct
    f_outs = dict(
        output=(shape(output.shape, BF), hbm), g_patches=(shape(patches.shape, BF), hbm),
        g_base=(shape(base_embed.shape, F32), hbm), g_bias_embed=(shape((width,), F32), hbm),
        g_grid=(shape(pos_grid.shape, F32), hbm), g_gain=(shape(norm_gain.shape, F32), hbm),
        g_shift=(shape(norm_shift.shape, F32), hbm), g_qkv=(shape(w_qkv.shape, F32), hbm),
        g_attn=(shape(bias_attn.shape, F32), hbm), g_out=(shape(w_out.shape, F32), hbm),
        g_up=(shape(w_up.shape, F32), hbm), g_bias_up=(shape((ff,), F32), hbm),
        g_down=(shape(w_down.shape, F32), hbm), g_bias_down=(shape((width,), F32), hbm),
    )
    f_scratch = dict(
        kf=V((k_rows, width), F32), base=V(base_embed.shape, F32), down=V(w_down.shape, F32),
        up=V(w_up.shape, F32), qkv=V(w_qkv.shape, F32), wo=V(w_out.shape, F32), gp=V(patches.shape, BF),
        tail_in=V((k_rows, width), BF), gd_in=V(gd.shape, BF), gu_in=V(gu.shape, BF), gq_in=V(gq.shape, BF),
        main_in=V(gp_main.shape, BF), last_in=V(gp_tail.shape, BF), out_buf=V(output.shape, BF), pinv_in=V(pinv.shape, F32), s_grid=V(pos_grid.shape, F32), s_bias_embed=V((width,), F32),
        s_gain=V(norm_gain.shape, F32), s_shift=V(norm_shift.shape, F32), s_attn=V(bias_attn.shape, F32),
        s_bias_down=V((width,), F32), s_bias_up=V((ff,), F32), sem=DMA((24,)),
    )
    f_conf = SimpleNamespace(**dict(vars(conf), names=list(f_ins) + list(f_outs) + list(f_scratch)))
    final = pl.pallas_call(
        functools.partial(finish_kernel, f_conf),
        out_shape=[s for s, _ in f_outs.values()],
        in_specs=[spec for _, spec in f_ins.values()],
        out_specs=[spec for _, spec in f_outs.values()],
        scratch_shapes=list(f_scratch.values()),
        compiler_params=pltpu.CompilerParams(vmem_limit_bytes=56 << 20),
        name="finish",
    )(*[value for value, _ in f_ins.values()])
    (output, g_patches, g_base, g_bias_embed, g_grid, g_gain, g_shift, g_qkv, g_attn, g_out, g_up,
     g_bias_up, g_down, g_bias_down) = final
    return (output, g_patches, g_base, g_bias_embed, g_grid, g_gain, g_shift, g_qkv, g_attn, g_out, g_up,
            g_bias_up, g_down, g_bias_down)


def solution(mesh):
    cfg = SimpleNamespace(n_img=mesh.shape[IMG], n_strip=mesh.shape[STRIP])
    split = P(IMG, STRIP, None)
    return jax.shard_map(
        functools.partial(per_device, cfg), mesh=mesh,
        in_specs=(split,) + (P(),) * 15 + (split,),
        out_specs=(split, split) + (P(),) * 12, check_vma=False,
    )
```

```python
import functools
import math
from types import SimpleNamespace

import jax
import jax.numpy as jnp
from jax import lax
from jax.experimental import pallas as pl
from jax.experimental.pallas import tpu as pltpu
from jax.sharding import PartitionSpec as P

HD = 64
EPSILON = 1e-06
MESH = pl.DeviceIdType.MESH
HIGHEST = lax.Precision.HIGHEST
BF = jnp.bfloat16
F32 = jnp.float32
COMM = True
MAIN, TAIL, COT = 0, 1, 2
IMG, STRIP = "img", "strip"
REP = {}


def begin(copy):
    copy.start()


def landed(copy):
    copy.wait_recv()


def sent(copy):
    copy.wait_send()


def nn(a, b, precision=None):
    return lax.dot_general(
        a, b, (((1,), (0,)), ((), ())), precision=precision, preferred_element_type=F32
    )


def nt(a, b):
    return lax.dot_general(a, b, (((1,), (1,)), ((), ())), preferred_element_type=F32)


def tn(a, b, precision=None):
    return lax.dot_general(
        a, b, (((0,), (0,)), ((), ())), precision=precision, preferred_element_type=F32
    )


def fold8(x):
    return jnp.sum(x.reshape(x.shape[0] // 8, 8, x.shape[1]), axis=0)


def rows_of(start, size):
    return pl.ds(pl.multiple_of(start, 16), size)


def chunk_of(rows):
    best = 16
    for size in range(16, 257, 16):
        if rows % size == 0:
            best = size
    return best


class Reduce:
    def __init__(self, group, grad, out, recv, extra_recv, sems):
        rows, stages = group.rows, group.stages
        self.stages, self.extras, self.done, self.rows = stages, group.extras, 0, rows
        self.grad, self.out, self.recv, self.extra_recv = grad, out, recv, extra_recv
        self.rs_s, self.rs_r, self.ag_s, self.ag_r, self.ex_s, self.ex_r, self.loc = sems
        count = len(stages)
        self.phases = [(self.rs_start, self.rs_finish, k) for k in range(count)]
        self.phases += [(self.ex_start, self.ex_finish, k) for k in range(len(self.extras))]
        for k in range(count - 1, -1, -1):
            if group.relay and stages[k] == (IMG, 2, 4):
                self.phases.append((self.near_start, self.near_finish, k))
                self.phases.append((self.far_start, self.far_finish, k))
            else:
                self.phases.append((self.ag_start, self.ag_finish, k))
        sizes, offsets = [rows], [0]
        for axis, unit, size in stages:
            mine = self.index(axis, unit, size)
            sizes.append(sizes[-1] // size)
            offsets.append(offsets[-1] + mine * sizes[-1])
        self.sizes, self.offsets = sizes, offsets

    @staticmethod
    def index(axis, unit, size):
        return (lax.axis_index(axis) // unit) % size

    def peer(self, stage, d):
        axis, unit, size = stage
        mine = self.index(axis, unit, size)
        there = (mine + d) % size
        return {axis: lax.axis_index(axis) + unit * (there - mine)}, there

    def rs_copies(self, k):
        size, sub = self.stages[k][2], self.sizes[k + 1]
        copies = []
        for d in range(1, size):
            device, there = self.peer(self.stages[k], d)
            copies.append(
                pltpu.make_async_remote_copy(
                    src_ref=self.grad.at[rows_of(self.offsets[k] + there * sub, sub), :],
                    dst_ref=self.recv[k].at[d - 1],
                    send_sem=self.rs_s.at[k, d - 1],
                    recv_sem=self.rs_r.at[k, d - 1],
                    device_id=device,
                    device_id_type=MESH,
                )
            )
        return copies

    def rs_start(self, k):
        for copy in self.rs_copies(k):
            copy.start()

    def rs_finish(self, k):
        copies = self.rs_copies(k)
        for copy in copies:
            copy.wait_recv()
        size, sub, first = self.stages[k][2], self.sizes[k + 1], self.offsets[k + 1]
        step = chunk_of(sub)

        def body(b, carry):
            rows = rows_of(first + b * step, step)
            total = self.grad[rows, :].astype(F32)
            for d in range(size - 1):
                total = total + self.recv[k][d, rows_of(b * step, step), :].astype(F32)
            self.grad[rows, :] = total.astype(BF)
            return carry

        lax.fori_loop(0, sub // step, body, 0)
        for copy in copies:
            copy.wait_send()

    def piece(self):
        return self.grad.at[rows_of(self.offsets[-1], self.sizes[-1]), :]

    def ex_copies(self, k):
        copies = []
        for d in range(1, self.extras[k][2]):
            device, _ = self.peer(self.extras[k], d)
            copies.append(
                pltpu.make_async_remote_copy(
                    src_ref=self.piece(),
                    dst_ref=self.extra_recv[k].at[d - 1],
                    send_sem=self.ex_s.at[k, d - 1],
                    recv_sem=self.ex_r.at[k, d - 1],
                    device_id=device,
                    device_id_type=MESH,
                )
            )
        return copies

    def ex_start(self, k):
        for copy in self.ex_copies(k):
            copy.start()

    def ex_finish(self, k):
        for copy in self.ex_copies(k):
            copy.wait()
        rows = rows_of(self.offsets[-1], self.sizes[-1])
        total = self.grad[rows, :].astype(F32)
        for d in range(self.extras[k][2] - 1):
            total = total + self.extra_recv[k][d].astype(F32)
        self.grad[rows, :] = total.astype(BF)

    def ag_copies(self, k):
        size, sub = self.stages[k][2], self.sizes[k + 1]
        region = self.out.at[rows_of(self.offsets[k + 1], sub), :]
        source = self.piece() if k == len(self.stages) - 1 else region
        copies = []
        for d in range(1, size):
            device, _ = self.peer(self.stages[k], d)
            copies.append(
                pltpu.make_async_remote_copy(
                    src_ref=source,
                    dst_ref=region,
                    send_sem=self.ag_s.at[k, d - 1],
                    recv_sem=self.ag_r.at[k, d - 1],
                    device_id=device,
                    device_id_type=MESH,
                )
            )
        return copies

    def plane(self, k):
        mine = self.index(*self.stages[k])
        return mine, mine + 1 - 2 * (mine % 2), mine + 2 - 4 * (mine // 2)

    def plane_copy(self, k, slot, piece, part, there):
        mine, _, _ = self.plane(k)
        rows = self.sizes[k + 1] // (1 if part is None else 2)
        start = self.offsets[k] + piece * self.sizes[k + 1] + (part or 0) * rows
        region = self.out.at[rows_of(start, rows), :]
        return pltpu.make_async_remote_copy(
            src_ref=region, dst_ref=region, send_sem=self.ag_s.at[k, slot], recv_sem=self.ag_r.at[k, slot],
            device_id={IMG: lax.axis_index(IMG) + 2 * (there - mine)}, device_id_type=MESH)

    def near_copies(self, k):
        mine, along_x, along_y = self.plane(k)
        return [self.plane_copy(k, 0, mine, None, along_x), self.plane_copy(k, 1, mine, None, along_y)]

    def far_copies(self, k):
        _, along_x, along_y = self.plane(k)
        return [self.plane_copy(k, 2, along_x, 0, along_y), self.plane_copy(k, 3, along_y, 1, along_x)]

    def near_start(self, k):
        for copy in self.near_copies(k):
            copy.start()

    def near_finish(self, k):
        for copy in self.near_copies(k):
            copy.wait()

    def far_start(self, k):
        for copy in self.far_copies(k):
            copy.start()

    def far_finish(self, k):
        for copy in self.far_copies(k):
            copy.wait()

    def local_copy(self):
        region = self.out.at[rows_of(self.offsets[-1], self.sizes[-1]), :]
        return pltpu.make_async_copy(self.piece(), region, self.loc.at[0])

    def left(self):
        return self.done <= len(self.phases)

    def step(self):
        n = self.done
        self.done += 1
        if n > 0:
            self.phases[n - 1][1](self.phases[n - 1][2])
        if n < len(self.phases):
            self.phases[n][0](self.phases[n][2])

    def ag_start(self, k):
        if k == len(self.stages) - 1:
            self.local_copy().start()
        for copy in self.ag_copies(k):
            copy.start()

    def ag_finish(self, k):
        if k == len(self.stages) - 1:
            self.local_copy().wait()
        for copy in self.ag_copies(k):
            copy.wait()


def layer_kernel(cfg, *refs):
    r = SimpleNamespace(**dict(zip(cfg.names, refs)))
    n_strip, strip_rows, slots = cfg.n_strip, cfg.strip_rows, cfg.slots
    seq, width, ff, pixels, area = cfg.seq, cfg.width, cfg.ff, cfg.pixels, cfg.area
    main_w = cfg.main_w
    tail = pixels - main_w
    grid_side, base_count = cfg.grid_side, cfg.base_count
    pairs = width // 128
    depth = r.base_embed.shape[1]
    ff_chunks = ff // width
    me = lax.axis_index(STRIP)
    group = 2 if n_strip % 2 == 0 else 1
    block = group * strip_rows
    blocks = n_strip // group

    def repeat(fn, *args):
        count = REP.get(fn.__name__, 1)
        if count == 1:
            fn(*args)
        else:
            lax.fori_loop(0, count, lambda t, c: (fn(*args), c)[1], 0)

    groups = []
    at = len(refs) - sum(len(g.stages) + len(g.extras) + 7 for g in cfg.groups)
    for g, grad, out in zip(cfg.groups, (r.gd, r.gu, r.gq, r.gk), (r.gd_out, r.gu_out, r.gq_out, r.gk_out)):
        n, e = len(g.stages), len(g.extras)
        groups.append(Reduce(g, grad, out, refs[at:at + n], refs[at + n:at + n + e],
                             refs[at + n + e:at + n + e + 7]))
        at += n + e + 7
    sum_d, sum_u, sum_q, sum_k = groups
    if COMM:
        barrier = pltpu.get_barrier_semaphore()
        greeted = 0
        for stage in cfg.stages + cfg.left:
            for d in range(1, stage[2]):
                device, _ = sum_k.peer(stage, d)
                pl.semaphore_signal(barrier, inc=1, device_id=device, device_id_type=MESH)
                greeted += 1

    loads = [
        pltpu.make_async_copy(r.w_qkv, r.wqkv, r.load_sem.at[0]),
        pltpu.make_async_copy(r.w_out, r.wout, r.load_sem.at[1]),
        pltpu.make_async_copy(r.w_up, r.wup, r.load_sem.at[2]),
        pltpu.make_async_copy(r.w_down, r.wdown, r.load_sem.at[3]),
    ]
    base_loads = [
        pltpu.make_async_copy(r.base_embed.at[c], r.wide.at[rows_of(c * depth, depth), :], r.load_sem.at[4 + c])
        for c in range(3)
    ]
    tails_load = pltpu.make_async_copy(
        r.patches.at[:, :, main_w:pixels], r.ptails, r.load_sem.at[7]
    )
    own_loads = []
    for slot in range(slots):
        rows = rows_of(me * strip_rows, strip_rows)
        own_loads.append(pltpu.make_async_copy(
            r.patches.at[me * slots + slot, :, 0:main_w], r.pmain.at[slot, rows, :],
            r.load_sem.at[8 + slot]))
        own_loads.append(pltpu.make_async_copy(
            r.cotangent.at[me * slots + slot], r.cot.at[slot, rows, :],
            r.load_sem.at[8 + slots + slot]))
    tails_load.start()
    for copy in base_loads:
        copy.start()
    for copy in own_loads:
        copy.start()
    for copy in loads:
        copy.start()

    def z_in(kind, slot, d):
        home = (me + d) % n_strip
        rows = rows_of(me * strip_rows, strip_rows)
        image = home * slots + slot
        if kind == MAIN:
            src, dst, k = r.patches.at[image, :, 0:main_w], r.pmain.at[slot, rows, :], slot
        elif kind == TAIL:
            src, dst, k = r.packed.at[home], r.ptail.at[rows, :], slots
        else:
            src, dst, k = r.cotangent.at[image], r.cot.at[slot, rows, :], slots + 1 + slot
        return pltpu.make_async_remote_copy(
            src_ref=src, dst_ref=dst, send_sem=r.zin_s.at[k, d - 1],
            recv_sem=r.zin_r.at[k, d - 1], device_id={STRIP: home}, device_id_type=MESH)

    def z_all(kind, slot, act):
        if not COMM:
            return
        for k in range(n_strip - 1):
            d = k + 1
            if act is begin and n_strip == 4:
                d = jnp.where(me == 2, (1, 3, 2)[k], d)
            act(z_in(kind, slot, d))

    if COMM:
        pl.semaphore_wait(barrier, greeted)
    z_all(MAIN, 0, begin)

    tails_load.wait()
    zero_tail = jnp.zeros((strip_rows, 128 // slots - tail), F32)
    for home in range(n_strip):
        parts = []
        for slot in range(slots):
            parts.append(r.ptails[home * slots + slot].astype(F32))
            parts.append(zero_tail)
        r.packed[home] = jnp.concatenate(parts, axis=1).astype(BF)
    z_all(TAIL, 0, begin)
    r.ptail[rows_of(me * strip_rows, strip_rows), :] = r.packed[me]

    def make_kernel():
        pinv = r.pinv[...].astype(BF)
        r.kf[...] = jnp.zeros_like(r.kf)
        for c in range(3):
            if not REP:
                base_loads[c].wait()
            r.kf[c * area:(c + 1) * area, :] = nn(pinv, r.wide[c * depth:(c + 1) * depth, :].astype(BF))
        kernel = r.kf[...].astype(BF)
        r.kmain[...] = kernel[0:main_w]
        for slot in range(slots):
            r.stage[...] = jnp.zeros_like(r.stage)
            at = slot * (128 // slots)
            r.stage[at:at + tail, :] = r.kf[main_w:pixels, :]
            r.ktail[slot] = r.stage[...].astype(BF)

    if REP:
        for copy in base_loads:
            copy.wait()
    repeat(make_kernel)

    def make_position():
        cells = r.table.shape[0]
        cell = lax.broadcasted_iota(jnp.int32, (cells, grid_side), 0).astype(F32)
        grid_row = jnp.floor((cell + 0.5) / base_count)
        corner = (grid_row, cell - grid_row * base_count)
        place = lax.broadcasted_iota(jnp.int32, (grid_side, seq), 1).astype(F32)
        which = lax.broadcasted_iota(jnp.int32, (grid_side, seq), 0).astype(F32)
        patch_row = jnp.floor((place + 0.5) / grid_side)
        patch = (patch_row, place - patch_row * grid_side)
        product = None
        for t in range(2):
            low = r.pos_index[t, 0:1, :].astype(F32)
            high = r.pos_index[t, 1:2, :].astype(F32)
            frac = r.pos_frac[t:t + 1, :]
            entry = (1.0 - frac) * (corner[t] == low).astype(F32) + frac * (corner[t] == high).astype(F32)
            spread = nn(entry, (patch[t] == which).astype(F32), HIGHEST)
            product = spread if product is None else product * spread
        valid = lax.broadcasted_iota(jnp.int32, (cells, seq), 0) < base_count * base_count
        r.table[...] = jnp.where(valid, product, 0.0)
        r.stage[...] = jnp.zeros_like(r.stage)
        for b in range(base_count):
            r.stage[b * base_count:(b + 1) * base_count, :] = r.pos_grid[b]
        r.posb[...] = tn(r.table[...], r.stage[0:cells, :], HIGHEST) + r.bias_embed[...]

    repeat(make_position)
    r.sums[...] = jnp.zeros_like(r.sums)
    r.sums_up[...] = jnp.zeros_like(r.sums_up)
    for one, used in zip(groups, ((ff + width), ff * pairs, 3 * width * pairs)):
        if one.rows > used:
            r_pad = one.grad.shape
            one.grad[used:, :] = jnp.zeros((r_pad[0] - used, r_pad[1]), BF)
    for copy in loads:
        copy.wait()
    for copy in own_loads:
        copy.wait()

    def wide_rows(k, rows):
        return rows_of(k * seq + rows.start, rows.size)

    lane = lax.broadcasted_iota(jnp.int32, (1, 128), 1)
    first_head = lane < HD

    def norm(x, gain, shift):
        center = x - jnp.mean(x, axis=-1, keepdims=True)
        inv = lax.rsqrt(jnp.mean(center * center, axis=-1, keepdims=True) + EPSILON)
        unit = center * inv
        return unit * gain + shift, unit, inv

    def norm_back(g, unit, inv, gain):
        gu = g * gain
        return inv * (
            gu - jnp.mean(gu, axis=-1, keepdims=True)
            - unit * jnp.mean(gu * unit, axis=-1, keepdims=True)
        )

    def add_sum(row, x):
        r.sums[row] += fold8(x)

    B_EMBED, GAIN, SHIFT, B_Q, B_V, B_O, B_DOWN = 0, 1, 3, 5, 6, 7, 8

    def near_first(t):
        return (t + me // group) % blocks

    def wait_rows(t, kind, slot):
        if not COMM:
            return
        for part in range(group):
            d = (me - t * group - part + n_strip) % n_strip

            @pl.when(d > 0)
            def _():
                z_in(kind, slot, d).wait_recv()

    def embed(i):
        def body(t, carry):
            b = near_first(t)
            rows = rows_of(b * block, block)
            wait_rows(b, MAIN, i)
            if i == 0:
                wait_rows(b, TAIL, 0)

            @pl.when(t == 0)
            def _():
                if i + 1 < slots:
                    z_all(MAIN, i + 1, begin)
                else:
                    z_all(COT, i, begin)

            emb = (
                nn(r.pmain[i, rows, :], r.kmain[...])
                + nn(r.ptail[rows, :], r.ktail[i])
                + r.posb[rows, :]
            )
            r.wide[wide_rows(i, rows), :] = emb
            y, unit, inv = norm(emb, r.norm_gain[0:1, :], r.norm_shift[0:1, :])
            y = y.astype(BF)
            r.normed[i, rows, :] = y
            r.unit[i, rows, :] = unit.astype(BF)
            r.inv[i, rows, :] = jnp.broadcast_to(inv, (block, 128))
            q = nn(y, r.wqkv[:, 0:width]) + r.bias_attn[0:1, :]
            r.qkv[i, rows, 0:width] = (q * (1.0 / math.sqrt(HD))).astype(BF)
            r.qkv[i, rows, width:2 * width] = nn(y, r.wqkv[:, width:2 * width]).astype(BF)
            v = nn(y, r.wqkv[:, 2 * width:3 * width]) + r.bias_attn[1:2, :]
            r.qkv[i, rows, 2 * width:3 * width] = v.astype(BF)
            return carry

        lax.fori_loop(0, blocks, body, 0)

    def lanes(p, part=0):
        return slice(part * width + p * 128, part * width + (p + 1) * 128)

    def ahead(tasks, front, rest, depth):
        ready = [front(*task) for task in tasks[:depth]]
        for n, task in enumerate(tasks):
            if n + depth < len(tasks):
                ready.append(front(*tasks[n + depth]))
            rest(*task, ready[n])
            ready[n] = None

    heads = [(p, h) for p in range(pairs) for h in range(2)]

    def pick(x, h):
        return jnp.where(first_head == (h == 0), x, jnp.zeros_like(x))

    def attend(i):
        outs, recips = {}, {}

        def front(p, h):
            return nt(pick(r.qkv[i, :, lanes(p)], h), r.qkv[i, :, lanes(p, 1)])

        def rest(p, h, s):
            e = jnp.exp(s - jnp.max(s, axis=-1, keepdims=True))
            recip = 1.0 / jnp.sum(e, axis=-1, keepdims=True)
            e = e.astype(BF)
            r.expo[i, 2 * p + h] = e
            outs[h] = nn(e, r.qkv[i, :, lanes(p, 2)]) * recip
            recips[h] = jnp.broadcast_to(recip, (seq, 128))
            if h == 1:
                r.att[i, :, lanes(p)] = jnp.where(first_head, outs[0], outs[1]).astype(BF)
                r.wide[(2 * slots + i) * seq:(2 * slots + i + 1) * seq, lanes(p)] = jnp.where(first_head, recips[0], recips[1])

        ahead(heads, front, rest, 2)

    c0 = math.sqrt(2.0 / math.pi)
    c1 = 0.044715

    def out_copy(i, d):
        strip = (me + d) % n_strip
        return pltpu.make_async_remote_copy(
            src_ref=r.outb.at[i, rows_of(strip * strip_rows, strip_rows), :],
            dst_ref=r.output.at[me * slots + i],
            send_sem=r.zout_s.at[i, d - 1], recv_sem=r.zout_r.at[i, d - 1],
            device_id={STRIP: strip}, device_id_type=MESH)

    def own_out(i):
        return pltpu.make_async_copy(
            r.outb.at[i, rows_of(me * strip_rows, strip_rows), :],
            r.output.at[me * slots + i], r.own_sem.at[i])

    def send_out(i):
        if not COMM:
            return
        for d in range(1, n_strip):
            out_copy(i, d).start()
        own_out(i).start()

    def mlp(i):
        def body(n, carry):
            t = near_first(n)
            rows = rows_of(t * block, block)
            wait_rows(t, COT, i)
            if i > 0:

                @pl.when(n == blocks - 1)
                def _():
                    send_out(i - 1)

            mid = r.wide[wide_rows(i, rows), :] + nn(r.att[i, rows, :], r.wout[...]) + r.bias_attn[2:3, :]
            gain = r.norm_gain[1:2, :]
            y, unit, inv = norm(mid, gain, r.norm_shift[1:2, :])
            y = y.astype(BF)
            r.nm[i, rows, :] = y
            cot = r.cot[i, rows, :]

            def front(cols):
                return nn(y, r.wup[:, cols]), nt(cot, r.wdown[cols, :])

            def rest(cols, ready):
                u = ready[0] + r.bias_up[cols]
                square = u * u
                half = 0.5 + 0.5 * jnp.tanh(u * (c0 + (c0 * c1) * square))
                act = u * half
                r.act[i, rows, cols] = act.astype(BF)
                slope = half + (act - act * half) * (2.0 * c0 + (6.0 * c0 * c1) * square)
                gu = ready[1] * slope
                r.gup[i, rows, cols] = gu.astype(BF)
                r.sums_up[:, cols] += fold8(gu)

            ahead([(slice(c, c + 256),) for c in range(0, ff, 256)], front, rest, 2)
            out = mid + r.bias_down[...] + nn(r.act[i, rows, :], r.wdown[...])
            g_nm = nt(r.gup[i, rows, :], r.wup[...])
            r.outb[i, rows, :] = out.astype(BF)
            add_sum(GAIN + 1, g_nm * unit)
            add_sum(SHIFT + 1, g_nm)
            cotf = cot.astype(F32)
            add_sum(B_DOWN, cotf)
            g_mid = cotf + norm_back(g_nm, unit, inv, gain)
            r.wide[wide_rows(slots + i, rows), :] = g_mid
            add_sum(B_O, g_mid)
            gb = g_mid.astype(BF)
            r.gb[i, rows, :] = gb
            r.datt[i, rows, :] = (nt(gb, r.wout[...]) * r.wide[wide_rows(2 * slots + i, rows), :]).astype(BF)
            return carry

        lax.fori_loop(0, blocks, body, 0)

    def ds_slot(p, h):
        wide = -(-seq // 128) * 128
        return (r.act, r.gup)[p % 2].at[slots - 1, :, h * wide:h * wide + seq]

    def attend_back(i):
        gq = {}

        def front(p, h):
            return nt(pick(r.datt[i, :, lanes(p)], h), r.qkv[i, :, lanes(p, 2)])

        def rest(p, h, dp):
            prod = r.datt[i, :, lanes(p)].astype(F32) * r.att[i, :, lanes(p)].astype(F32)
            delta = jnp.sum(pick(prod, h), axis=-1, keepdims=True)
            expo = r.expo[i, 2 * p + h]
            ds = (expo.astype(F32) * (dp - delta)).astype(BF)
            ds_slot(p, h)[...] = ds
            gq[h] = nn(ds, r.qkv[i, :, lanes(p, 1)])
            if h == 0:
                return
            g_q = jnp.where(first_head, gq[0], gq[1]) * (1.0 / math.sqrt(HD))
            r.gproj[i, :, lanes(p)] = g_q.astype(BF)
            q_t, d_t = r.qkv[i, :, lanes(p)].T, r.datt[i, :, lanes(p)].T
            for part in range(2):
                half = slice(part * HD, (part + 1) * HD)
                r.tk[p, half, :] = nn(q_t[half, :], ds_slot(p, part)[...]).astype(BF)
                r.tv[p, half, :] = nn(d_t[half, :], r.expo[i, 2 * p + part]).astype(BF)
            r.gproj[i, :, lanes(p, 1)] = r.tk[p].T
            r.gproj[i, :, lanes(p, 2)] = r.tv[p].T

        ahead(heads, front, rest, 1)

    def gp_copy(i, d):
        strip = (me + d) % n_strip
        return pltpu.make_async_remote_copy(
            src_ref=r.gup.at[i, rows_of(strip * strip_rows, strip_rows), ff - main_w:ff],
            dst_ref=r.gp_main.at[me * slots + i],
            send_sem=r.zout_s.at[slots + i, d - 1], recv_sem=r.zout_r.at[slots + i, d - 1],
            device_id={STRIP: strip}, device_id_type=MESH)

    def own_gp(i):
        return pltpu.make_async_copy(
            r.gup.at[i, rows_of(me * strip_rows, strip_rows), ff - main_w:ff],
            r.gp_main.at[me * slots + i], r.own_sem.at[slots + i])

    def gpt_copy(i, d):
        strip = (me + d) % n_strip
        return pltpu.make_async_remote_copy(
            src_ref=r.gpt.at[rows_of(strip * strip_rows, strip_rows), :],
            dst_ref=r.gp_tail.at[me],
            send_sem=r.zout_s.at[2 * slots, d - 1], recv_sem=r.zout_r.at[2 * slots, d - 1],
            device_id={STRIP: strip}, device_id_type=MESH)

    def own_gpt(i):
        return pltpu.make_async_copy(
            r.gpt.at[rows_of(me * strip_rows, strip_rows), :],
            r.gp_tail.at[me], r.own_sem.at[2 * slots])

    def embed_back(i):
        def body(t, carry):
            rows = rows_of(t * block, block)
            gain = r.norm_gain[0:1, :]
            unit = r.unit[i, rows, :].astype(F32)
            gproj = r.gproj[i, rows, :]
            add_sum(B_Q, gproj[:, 0:width].astype(F32))
            add_sum(B_V, gproj[:, 2 * width:3 * width].astype(F32))
            g_n = nt(gproj, r.wqkv[...])
            add_sum(GAIN, g_n * unit)
            add_sum(SHIFT, g_n)
            inv = r.inv[i, rows, :][:, 0:1]
            g_emb = r.wide[wide_rows(slots + i, rows), :] + norm_back(g_n, unit, inv, gain)
            add_sum(B_EMBED, g_emb)
            ge = g_emb.astype(BF)
            r.act[i, rows, ff - width:ff] = ge
            r.gup[i, rows, ff - main_w:ff] = nt(ge, r.kmain[...]).astype(BF)
            part = nt(ge, r.ktail[i])
            if i > 0:
                part = part + r.gpt[rows, :].astype(F32)
            r.gpt[rows, :] = part.astype(BF)
            return carry

        lax.fori_loop(0, blocks, body, 0)

    early = 2 if n_strip > 2 else 1

    def send_early():
        if COMM:
            gp_copy(0, early).start()

    def send_gp(i):
        if not COMM:
            return
        for d in range(1, n_strip):
            if i > 0 or d != early:
                gp_copy(i, d).start()
        own_gp(i).start()

    def send_tail():
        if not COMM:
            return
        for d in range(1, n_strip):
            gpt_copy(0, d).start()
        own_gpt(0).start()

    def both(ref, cols=slice(None)):
        return ref[:, :, cols].reshape(slots * seq, -1)

    def grads_d():
        lhs = both(r.cot).T
        for c in range(0, ff, 512):
            r.gd[c:c + 512, :] = nn(lhs, both(r.act, slice(c, c + 512))).T.astype(BF)
        r.gd[ff:ff + width, :] = tn(both(r.att), both(r.gb)).astype(BF)

    def grads_u():
        lhs = both(r.nm).T
        for c in range(0, ff, 512):
            part = nn(lhs, both(r.gup, slice(c, c + 512))).astype(BF)
            for n in range(4):
                r.gu[(c // 128 + n) * width:(c // 128 + n + 1) * width, :] = part[:, n * 128:(n + 1) * 128]

    def grads_q():
        lhs = both(r.normed).T
        for c in range(3):
            part = nn(lhs, both(r.gproj, slice(c * width, (c + 1) * width))).astype(BF)
            for n in range(pairs):
                at = (c * pairs + n) * width
                r.gq[at:at + width, :] = part[:, n * 128:(n + 1) * 128]

    def grads_k():
        r.kf[0:main_w, :] = tn(both(r.pmain), both(r.act, slice(ff - width, ff)))
        at = main_w
        total = None
        for slot in range(slots):
            part = tn(r.ptail[...], r.act[slot, :, ff - width:ff])
            start = slot * (128 // slots)
            part = part[start:start + tail, :]
            total = part if total is None else total + part
        r.kf[main_w:pixels, :] = total
        summed = sum(r.act[slot, :, ff - width:ff].astype(F32) for slot in range(slots))
        g_grid = nn(r.table[...], summed, HIGHEST)
        cells = base_count * base_count
        r.kf[pixels:pixels + cells, :] = g_grid[0:cells, :]
        small = jnp.sum(r.sums[...], axis=1)
        at = cfg.small_at + small.shape[0]
        r.kf[cfg.small_at:at, :] = small
        small_up = jnp.sum(r.sums_up[...], axis=0, keepdims=True)
        for c in range(ff_chunks):
            r.kf[at + c:at + c + 1, :] = small_up[:, c * width:(c + 1) * width]
        r.gk[0:r.kf.shape[0], :] = r.kf[...].astype(BF)
        if cfg.groups[3].rows > r.kf.shape[0]:
            more = cfg.groups[3].rows - r.kf.shape[0]
            r.gk[r.kf.shape[0]:, :] = jnp.zeros((more, width), BF)

    def step(*sums):
        if COMM:
            for one in sums:
                if one.left():
                    one.step()

    for i in range(slots):
        repeat(embed, i)
        if i + 1 < slots:
            z_all(COT, i, begin)
        repeat(attend, i)
    for i in range(slots):
        repeat(mlp, i)
    repeat(grads_d)
    step(sum_d)
    send_out(slots - 1)
    repeat(grads_u)
    step(sum_u, sum_d)
    repeat(attend_back, 0)
    step(sum_u)
    for i in range(1, slots):
        repeat(attend_back, i)
    repeat(grads_q)
    step(sum_q, sum_d)
    repeat(embed_back, 0)
    step(sum_q)
    send_early()
    for i in range(1, slots):
        repeat(embed_back, i)
    repeat(grads_k)
    step(sum_k, sum_u, sum_k, sum_d, sum_q, sum_k, sum_u, sum_d, sum_k, sum_q)
    for i in range(slots):
        send_gp(i)
    send_tail()
    if COMM:
        for slot in range(slots):
            z_all(MAIN, slot, sent)
            z_all(COT, slot, sent)
            for d in range(1, n_strip):
                out_copy(slot, d).wait()
            own_out(slot).wait()
        z_all(TAIL, 0, sent)
    step(sum_u, sum_d, sum_k, sum_q, sum_u, sum_d, sum_k, sum_q, sum_u, sum_d)
    while COMM and any(one.left() for one in groups):
        step(sum_d, sum_q, sum_k, sum_u)
    if COMM:
        for slot in range(slots):
            for d in range(1, n_strip):
                gp_copy(slot, d).wait()
            own_gp(slot).wait()
        for d in range(1, n_strip):
            gpt_copy(0, d).wait()
        own_gpt(0).wait()


def finish_kernel(cfg, *refs):
    r = SimpleNamespace(**dict(zip(cfg.names, refs)))
    width, ff, slots = cfg.width, cfg.ff, cfg.slots
    pixels, area, main_w = cfg.pixels, cfg.area, cfg.main_w
    tail = pixels - main_w
    ff_chunks = ff // width
    copies = []

    def load(k, src, dst):
        copy = pltpu.make_async_copy(src, dst, r.sem.at[k])
        copy.start()
        return copy

    def send(src, dst, k):
        copy = pltpu.make_async_copy(src, dst, r.sem.at[k])
        copy.start()
        copies.append(copy)

    loads = [
        load(9, r.gk.at[0:r.kf.shape[0], :], r.tail_in),
        load(10, r.gd, r.gd_in),
        load(11, r.gu, r.gu_in),
        load(12, r.gp_main, r.main_in),
        load(13, r.gp_tail, r.last_in),
        load(14, r.out_in, r.out_buf),
        load(15, r.gq, r.gq_in),
        load(16, r.pinv, r.pinv_in),
    ]
    loads[0].wait()
    r.kf[...] = r.tail_in[...].astype(F32)
    small = r.kf[cfg.small_at:cfg.small_at + 16, :]
    for b in range(cfg.base_count):
        at = pixels + b * cfg.base_count
        r.s_grid[b] = r.kf[at:at + cfg.base_count, :]
    r.s_bias_embed[...] = small[0]
    r.s_gain[...] = small[1:3]
    r.s_shift[...] = small[3:5]
    r.s_attn[...] = small[5:8]
    r.s_bias_down[...] = small[8]
    for c in range(ff_chunks):
        r.s_bias_up[c * width:(c + 1) * width] = small[9 + c]
    few = ((r.s_grid, r.g_grid), (r.s_bias_embed, r.g_bias_embed), (r.s_gain, r.g_gain), (r.s_shift, r.g_shift),
           (r.s_attn, r.g_attn), (r.s_bias_down, r.g_bias_down), (r.s_bias_up, r.g_bias_up))
    for n, (held, place) in enumerate(few):
        send(held, place, 17 + n)
    loads[7].wait()
    pinv = r.pinv_in[...].astype(BF)
    for c in range(3):
        part = r.kf[c * area:(c + 1) * area, :].astype(BF)
        r.base[c] = tn(pinv, part)
        send(r.base.at[c], r.g_base.at[c], 1 + c)
    loads[1].wait()
    r.down[...] = r.gd_in[0:ff, :].astype(F32)
    r.wo[...] = r.gd_in[ff:ff + width, :].astype(F32)
    send(r.wo, r.g_out, 7)
    send(r.down, r.g_down, 4)
    loads[2].wait()
    for n in range(ff // 128):
        r.up[:, n * 128:(n + 1) * 128] = r.gu_in[n * width:(n + 1) * width, :].astype(F32)
    send(r.up, r.g_up, 5)
    loads[6].wait()
    pairs = width // 128
    for n in range(3 * pairs):
        r.qkv[:, n * 128:(n + 1) * 128] = r.gq_in[n * width:(n + 1) * width, :].astype(F32)
    send(r.qkv, r.g_qkv, 6)
    loads[5].wait()
    send(r.out_buf, r.output, 0)
    loads[3].wait()
    loads[4].wait()
    for image in range(r.gp.shape[0]):
        r.gp[image, :, 0:main_w] = r.main_in[image]
        start = (image % slots) * (128 // slots)
        last = r.last_in[image // slots].astype(F32)[:, start:start + tail]
        r.gp[image, :, main_w:pixels] = last.astype(BF)
    send(r.gp, r.g_patches, 8)
    for copy in copies:
        copy.wait()


def per_device(cfg, patches, pinv, base_embed, bias_embed, pos_grid, pos_index, pos_frac, norm_gain,
               norm_shift, w_qkv, bias_attn, w_out, w_up, bias_up, w_down, bias_down, cotangent):
    images, strip_rows, pixels = patches.shape
    width, ff = w_up.shape
    n_img, n_strip = cfg.n_img, cfg.n_strip
    slots = images // n_strip
    seq = strip_rows * n_strip
    base_count = pos_grid.shape[0]
    area = pinv.shape[0]
    main_w = pixels // 128 * 128
    core = [(IMG, 1, min(2, n_img))]
    plane = [(IMG, 2, min(4, n_img // 2))] if n_img > 2 else []
    stages = core + plane + [(STRIP, 1, n_strip)]
    halves = [(STRIP, 1, 2), (STRIP, 2, n_strip // 2)] if n_strip % 2 == 0 else [(STRIP, 1, n_strip)]
    left = [(IMG, 8, n_img // 8)] if n_img > 8 else []
    cells = base_count * base_count
    small_at = -(-(pixels + cells) // 8) * 8
    k_rows = -(-(small_at + 9 + ff // width) // 128) * 128

    def sum_of(values, lanes, order, extras, relay=False):
        unit = 16 * math.prod(s[2] for s in order)
        return SimpleNamespace(rows=-(-(values // lanes) // unit) * unit, lanes=lanes, stages=order,
                               extras=extras + left, relay=relay)

    groups = [sum_of((ff + width) * width, width, stages, [], True), sum_of(ff * width, 128, stages, [], True),
              sum_of(3 * width * width, 128, stages, []),
              sum_of(k_rows * width, width, core + plane, halves)]
    conf = SimpleNamespace(n_strip=n_strip, strip_rows=strip_rows, slots=slots, seq=seq, width=width, ff=ff,
                           pixels=pixels, area=area, main_w=main_w, grid_side=pos_frac.shape[1],
                           base_count=base_count, stages=stages, left=left, groups=groups,
                           small_at=small_at)
    vmem = pl.BlockSpec(memory_space=pltpu.VMEM)
    hbm = pl.BlockSpec(memory_space=pl.ANY)
    ins = dict(
        patches=(patches, hbm), cotangent=(cotangent, hbm), base_embed=(base_embed, hbm),
        w_qkv=(w_qkv, hbm), w_out=(w_out, hbm), w_up=(w_up, hbm), w_down=(w_down, hbm),
        pinv=(pinv, vmem), bias_embed=(bias_embed, vmem), pos_grid=(pos_grid, vmem),
        pos_index=(pos_index, vmem), pos_frac=(pos_frac, vmem), norm_gain=(norm_gain, vmem),
        norm_shift=(norm_shift, vmem), bias_attn=(bias_attn, vmem),
        bias_up=(bias_up, vmem), bias_down=(bias_down, vmem),
    )
    outs = dict(
        output=jax.ShapeDtypeStruct((images, strip_rows, width), BF),
        gp_main=jax.ShapeDtypeStruct((images, strip_rows, main_w), BF),
        gp_tail=jax.ShapeDtypeStruct((n_strip, strip_rows, 128), BF),
        **dict(zip(("gd_out", "gu_out", "gq_out", "gk_out"),
                   (jax.ShapeDtypeStruct((g.rows, g.lanes), BF) for g in groups))),
    )
    V = pltpu.VMEM
    DMA = pltpu.SemaphoreType.DMA
    scratch = dict(
        wqkv=V(w_qkv.shape, BF), wout=V(w_out.shape, BF), wup=V(w_up.shape, BF), wdown=V(w_down.shape, BF),
        wide=V((max(3 * base_embed.shape[1], 3 * slots * seq), width), F32),
        ptails=V((images, strip_rows, pixels - main_w), BF), packed=V((n_strip, strip_rows, 128), BF),
        pmain=V((slots, seq, main_w), BF), ptail=V((seq, 128), BF), cot=V((slots, seq, width), BF),
        kf=V((k_rows, width), F32), kmain=V((main_w, width), BF), ktail=V((slots, 128, width), BF),
        stage=V((128, width), F32), table=V((-(-cells // 8) * 8, seq), F32), posb=V((seq, width), F32),
        normed=V((slots, seq, width), BF), unit=V((slots, seq, width), BF),
        inv=V((slots, seq, 128), F32), qkv=V((slots, seq, 3 * width), BF),
        expo=V((slots, width // HD, seq, seq), BF),
        att=V((slots, seq, width), BF), nm=V((slots, seq, width), BF),
        act=V((slots, seq, ff), BF), gup=V((slots, seq, ff), BF), outb=V((slots, seq, width), BF),
        gb=V((slots, seq, width), BF), datt=V((slots, seq, width), BF),
        tk=V((width // 128, 128, seq), BF), tv=V((width // 128, 128, seq), BF),
        gproj=V((slots, seq, 3 * width), BF), gpt=V((seq, 128), BF),
        sums=V((9, 8, width), F32), sums_up=V((8, ff), F32),
        gd=V((groups[0].rows, groups[0].lanes), BF), gu=V((groups[1].rows, groups[1].lanes), BF),
        gq=V((groups[2].rows, groups[2].lanes), BF), gk=V((groups[3].rows, groups[3].lanes), BF),
    )
    reduce_scratch = []
    for g in groups:
        size = g.rows
        for stage in g.stages:
            size //= stage[2]
            reduce_scratch.append(V((stage[2] - 1, size, g.lanes), BF))
        reduce_scratch += [V((stage[2] - 1, size, g.lanes), BF) for stage in g.extras]
        many = max([s[2] - 1 for s in g.extras] + [1])
        reduce_scratch += [DMA((len(g.stages), 4))] * 4 + [DMA((max(len(g.extras), 1), many))] * 2 + [DMA((1,))]
    scratch.update(
        load_sem=DMA((8 + 2 * slots,)), zin_s=DMA((2 * slots + 1, n_strip - 1)),
        zin_r=DMA((2 * slots + 1, n_strip - 1)), zout_s=DMA((2 * slots + 1, n_strip - 1)),
        zout_r=DMA((2 * slots + 1, n_strip - 1)), own_sem=DMA((2 * slots + 1,)),
    )
    conf.names = list(ins) + list(outs) + list(scratch)
    results = pl.pallas_call(
        functools.partial(layer_kernel, conf),
        out_shape=list(outs.values()),
        in_specs=[spec for _, spec in ins.values()],
        out_specs=[hbm] * len(outs),
        scratch_shapes=list(scratch.values()) + reduce_scratch,
        compiler_params=pltpu.CompilerParams(
            collective_id=0 if COMM else None, has_side_effects=True, vmem_limit_bytes=60 << 20),
        name="layer",
    )(*[value for value, _ in ins.values()])
    output, gp_main, gp_tail, gd, gu, gq, gk = results

    f_ins = dict(out_in=(output, hbm), gp_main=(gp_main, hbm), gp_tail=(gp_tail, hbm),
                 gd=(gd, hbm), gu=(gu, hbm), gq=(gq, hbm), gk=(gk, hbm), pinv=(pinv, hbm))
    shape = jax.ShapeDtypeStruct
    f_outs = dict(
        output=(shape(output.shape, BF), hbm), g_patches=(shape(patches.shape, BF), hbm),
        g_base=(shape(base_embed.shape, F32), hbm), g_bias_embed=(shape((width,), F32), hbm),
        g_grid=(shape(pos_grid.shape, F32), hbm), g_gain=(shape(norm_gain.shape, F32), hbm),
        g_shift=(shape(norm_shift.shape, F32), hbm), g_qkv=(shape(w_qkv.shape, F32), hbm),
        g_attn=(shape(bias_attn.shape, F32), hbm), g_out=(shape(w_out.shape, F32), hbm),
        g_up=(shape(w_up.shape, F32), hbm), g_bias_up=(shape((ff,), F32), hbm),
        g_down=(shape(w_down.shape, F32), hbm), g_bias_down=(shape((width,), F32), hbm),
    )
    f_scratch = dict(
        kf=V((k_rows, width), F32), base=V(base_embed.shape, F32), down=V(w_down.shape, F32),
        up=V(w_up.shape, F32), qkv=V(w_qkv.shape, F32), wo=V(w_out.shape, F32), gp=V(patches.shape, BF),
        tail_in=V((k_rows, width), BF), gd_in=V(gd.shape, BF), gu_in=V(gu.shape, BF), gq_in=V(gq.shape, BF),
        main_in=V(gp_main.shape, BF), last_in=V(gp_tail.shape, BF), out_buf=V(output.shape, BF), pinv_in=V(pinv.shape, F32), s_grid=V(pos_grid.shape, F32), s_bias_embed=V((width,), F32),
        s_gain=V(norm_gain.shape, F32), s_shift=V(norm_shift.shape, F32), s_attn=V(bias_attn.shape, F32),
        s_bias_down=V((width,), F32), s_bias_up=V((ff,), F32), sem=DMA((24,)),
    )
    f_conf = SimpleNamespace(**dict(vars(conf), names=list(f_ins) + list(f_outs) + list(f_scratch)))
    final = pl.pallas_call(
        functools.partial(finish_kernel, f_conf),
        out_shape=[s for s, _ in f_outs.values()],
        in_specs=[spec for _, spec in f_ins.values()],
        out_specs=[spec for _, spec in f_outs.values()],
        scratch_shapes=list(f_scratch.values()),
        compiler_params=pltpu.CompilerParams(vmem_limit_bytes=56 << 20),
        name="finish",
    )(*[value for value, _ in f_ins.values()])
    (output, g_patches, g_base, g_bias_embed, g_grid, g_gain, g_shift, g_qkv, g_attn, g_out, g_up,
     g_bias_up, g_down, g_bias_down) = final
    return (output, g_patches, g_base, g_bias_embed, g_grid, g_gain, g_shift, g_qkv, g_attn, g_out, g_up,
            g_bias_up, g_down, g_bias_down)


def solution(mesh):
    cfg = SimpleNamespace(n_img=mesh.shape[IMG], n_strip=mesh.shape[STRIP])
    split = P(IMG, STRIP, None)
    return jax.shard_map(
        functools.partial(per_device, cfg), mesh=mesh,
        in_specs=(split,) + (P(),) * 15 + (split,),
        out_specs=(split, split) + (P(),) * 12, check_vma=False,
    )
```
